128 devices in a mesh: row: 8 (over z, x_hi), col: 16 (over x_lo, y, core).
Axes of the slice: x: 4 (x_hi: 2, x_lo: 2; x = x_hi * 2 + x_lo), y: 4, z: 4, core: 2. Of those that a mesh axis runs over, the one named last changes fastest.
Arguments:
- activations: bfloat16 [512, 512, 384], P('row', 'col'), may hold values from -6 to 6
- cotangent: bfloat16 [512, 512, 384], P('row', 'col'), may hold values from -6 to 6
- first_gain: float32 [384], replicated, may hold values from 0.1 to 1.9
- joint_weight: bfloat16 [384, 1152], replicated, may hold values from -4 to 4, as said below
- output_weight: bfloat16 [384, 384], replicated, may hold values from -0.3125 to 0.3125
- second_gain: float32 [384], replicated, may hold values from 0.1 to 1.9
- expand_weight: bfloat16 [384, 1536], replicated, may hold values from -0.3125 to 0.3125
- reduce_weight: bfloat16 [1536, 384], replicated, may hold values from -0.15625 to 0.15625
Outputs:
- block_out: bfloat16 [512, 512, 384], P('row', 'col')
- grad_input: bfloat16 [512, 512, 384], P('row', 'col')
- grad_joint: float32 [384, 1152], replicated
- grad_project: float32 [384, 384], replicated
- grad_expand: float32 [384, 1536], replicated
- grad_reduce: float32 [1536, 384], replicated
- grad_first_gain: float32 [384], replicated
- grad_second_gain: float32 [384], replicated
The draws below stay inside these ranges and needn't reach their ends.
Inputs may be any that keep to these rules, and one draw needn't show every extreme that they name: `joint_weight`: Queries, keys and values side by side along the columns, each 384 wide, heads of 32 consecutive columns.
All inputs are finite; a program needn't handle non-finite values.
Results may differ from the reference program's by a relative error of at most 0.014.
The reference program's roundings to bfloat16 on the way count: a program that leaves them out, or rounds other values in their place, can miss the bound.
Values may be sent and summed in bfloat16 or wider, within the bound.
A program may use at most 192 MiB of HBM per device.

```python
import math
import jax
import jax.numpy as jnp
from jax import lax

D = 384
HEADS = 12
FF = 1536
GRID = 16
IMG_H = 512
IMG_W = 512
STRIDE_H = 32
STRIDE_W = 32
POSITIONS = 262144


def draw_joint_weight(key, part):
    subkeys = jax.random.split(jax.random.fold_in(key, 7), 3)
    key_part = jnp.clip(jax.random.normal(subkeys[1], (D, D), jnp.float32), -4.0, 4.0) * D ** (-0.5)
    value_part = jnp.clip(jax.random.normal(subkeys[2], (D, D), jnp.float32), -4.0, 4.0) * D ** (-0.5)
    query_part = jnp.clip(jax.random.normal(subkeys[0], (D, D), jnp.float32), -4.0, 4.0) * D ** (-0.5)
    return jnp.concatenate([query_part, key_part, value_part], axis=1).astype(jnp.bfloat16)


def block_scale(own_key, extent, cuts, low, top_value):
    def one(position, shards_of):
        steps = jax.random.uniform(jax.random.fold_in(jax.random.fold_in(own_key, 6), position), (shards_of,), jnp.float32, low / len(cuts), top_value / len(cuts))
        return jnp.repeat(jnp.exp(steps), extent[position] // shards_of).reshape((-1,) + (1,) * (len(extent) - position - 1))

    loudness = one(*cuts[0])
    for cut in cuts[1:]:
        loudness = loudness * one(*cut)
    return loudness


def gaussian(key, extent, width, reach, cuts=(), dtype=jnp.bfloat16):
    values = width * jax.random.normal(key, extent, jnp.float32)
    if cuts:
        values = values * block_scale(key, extent, cuts, -0.22, 0.18)
    return jnp.clip(values, -reach, reach).astype(dtype)


def setup_inputs(seed: int = 0) -> dict:
    keys = jax.random.split(jax.random.key(seed), 9)
    activations = gaussian(keys[0], (IMG_H, IMG_W, D), 1.0, 6.0, ((0, 8), (1, 16)))
    cotangent = gaussian(keys[1], (IMG_H, IMG_W, D), 1.0, 6.0, ((0, 8), (1, 16)))
    first_gain = jnp.clip(1.0 + 0.18 * jax.random.normal(keys[2], (D,), jnp.float32), 0.1, 1.9)
    joint_weight = draw_joint_weight(jax.random.fold_in(keys[8], 71), 0)
    output_weight = gaussian(keys[4], (D, D), D ** -0.5, 0.3125)
    second_gain = jnp.clip(1.0 + 0.18 * jax.random.normal(keys[5], (D,), jnp.float32), 0.1, 1.9)
    expand_weight = gaussian(keys[6], (D, FF), D ** -0.5, 0.3125)
    reduce_weight = gaussian(keys[7], (FF, D), FF ** -0.5, 0.15625)
    return dict(activations=activations, cotangent=cotangent, first_gain=first_gain, joint_weight=joint_weight, output_weight=output_weight, second_gain=second_gain, expand_weight=expand_weight, reduce_weight=reduce_weight)


EPSILON = 1e-05
SQRT_HALF = 0.7071067811865476
INV_ROOT_TAU = 0.3989422804014327

def normalize(values):
    center = values - lax.optimization_barrier(jnp.mean(values, axis=-1, keepdims=True))
    inv_std = lax.rsqrt(lax.optimization_barrier(jnp.mean(center * center, axis=-1, keepdims=True)) + EPSILON)
    return (center * inv_std, inv_std)

def norm_back(grad_norm, gain_vec, normed, inv_std):
    scaled = grad_norm * gain_vec
    return inv_std * (scaled - lax.optimization_barrier(jnp.mean(scaled, axis=-1, keepdims=True)) - normed * lax.optimization_barrier(jnp.mean(scaled * normed, axis=-1, keepdims=True)))

def gelu_value(pre_act):
    return 0.5 * pre_act * (1.0 + jax.scipy.special.erf(pre_act * SQRT_HALF))

def gelu_slope(pre_act):
    return 0.5 * (1.0 + jax.scipy.special.erf(pre_act * SQRT_HALF)) + pre_act * jnp.exp(-0.5 * pre_act * pre_act) * INV_ROOT_TAU

def project_rows(inputs, gain_vec, weight):
    normed, inv_std = normalize(inputs)
    scaled = (normed * gain_vec).astype(jnp.bfloat16)
    triple = jnp.dot(scaled, weight, preferred_element_type=jnp.float32).astype(jnp.bfloat16)
    return (triple, scaled, normed, inv_std)

def split_heads(rows, feature_dim):
    return rows.reshape(rows.shape[0], rows.shape[1], HEADS, feature_dim // HEADS).astype(jnp.float32)

def attend(triple):
    feature_dim = triple.shape[-1] // 3
    queries = split_heads(triple[..., :feature_dim], feature_dim)
    key_rows = split_heads(triple[..., feature_dim:2 * feature_dim], feature_dim)
    value_rows = split_heads(triple[..., 2 * feature_dim:], feature_dim)
    score_scale = (feature_dim // HEADS) ** (-0.5)
    scores = jnp.einsum('bqhe,bkhe->bhqk', queries, key_rows) * score_scale
    row_max = lax.optimization_barrier(jnp.max(scores, axis=-1, keepdims=True))
    weights = jnp.exp(scores - row_max)
    weights = weights / lax.optimization_barrier(jnp.sum(weights, axis=-1, keepdims=True))
    return (weights, queries, key_rows, value_rows, score_scale)

def attend_forward(triple):
    weights, queries, key_rows, value_rows, score_scale = attend(triple)
    weights_b = weights.astype(jnp.bfloat16).astype(jnp.float32)
    mixed_rows = jnp.einsum('bhqk,bkhe->bqhe', weights_b, value_rows).astype(jnp.bfloat16)
    return mixed_rows.reshape(triple.shape[0], triple.shape[1], -1)

def attend_backward(triple, grad_mixed):
    weights, queries, key_rows, value_rows, score_scale = attend(triple)
    feature_dim = triple.shape[-1] // 3
    grad_heads = split_heads(grad_mixed, feature_dim)
    grad_weights = jnp.einsum('bqhe,bkhe->bhqk', grad_heads, value_rows)
    inner_sum = lax.optimization_barrier(jnp.sum(weights * grad_weights, axis=-1, keepdims=True))
    grad_scores = (weights * (grad_weights - inner_sum) * score_scale).astype(jnp.bfloat16).astype(jnp.float32)
    weights_b = weights.astype(jnp.bfloat16).astype(jnp.float32)
    grad_query = jnp.einsum('bhqk,bkhe->bqhe', grad_scores, key_rows).astype(jnp.bfloat16)
    grad_key = jnp.einsum('bhqk,bqhe->bkhe', grad_scores, queries).astype(jnp.bfloat16)
    grad_value = jnp.einsum('bhqk,bqhe->bkhe', weights_b, grad_heads).astype(jnp.bfloat16)
    shape_out = (triple.shape[0], triple.shape[1], feature_dim)
    return jnp.concatenate([grad_query.reshape(shape_out), grad_key.reshape(shape_out), grad_value.reshape(shape_out)], axis=-1)

def tail_back(inputs, mixed_rows, out_weight, gain_vec, up_weight, down_weight, cot_rows):
    attended = inputs + jnp.dot(mixed_rows, out_weight, preferred_element_type=jnp.float32)
    normed, inv_std = normalize(attended)
    scaled = (normed * gain_vec).astype(jnp.bfloat16)
    pre_act = jnp.dot(scaled, up_weight, preferred_element_type=jnp.float32)
    hidden = gelu_value(pre_act).astype(jnp.bfloat16)
    result = (attended + jnp.dot(hidden, down_weight, preferred_element_type=jnp.float32)).astype(jnp.bfloat16)
    grad_down = jnp.dot(hidden.T, cot_rows, preferred_element_type=jnp.float32)
    grad_hidden = jnp.dot(cot_rows, down_weight.T, preferred_element_type=jnp.float32).astype(jnp.bfloat16)
    grad_pre = (grad_hidden.astype(jnp.float32) * gelu_slope(pre_act)).astype(jnp.bfloat16)
    grad_up = jnp.dot(scaled.T, grad_pre, preferred_element_type=jnp.float32)
    grad_scaled = jnp.dot(grad_pre, up_weight.T, preferred_element_type=jnp.float32)
    grad_gain = lax.optimization_barrier(jnp.sum(grad_scaled * normed, axis=0))
    grad_attended = cot_rows.astype(jnp.float32) + norm_back(grad_scaled, gain_vec, normed, inv_std)
    grad_attended_b = grad_attended.astype(jnp.bfloat16)
    grad_out = jnp.dot(mixed_rows.T, grad_attended_b, preferred_element_type=jnp.float32)
    grad_mixed = jnp.dot(grad_attended_b, out_weight.T, preferred_element_type=jnp.float32).astype(jnp.bfloat16)
    return (result, grad_attended, grad_mixed, (grad_out, grad_gain, grad_up, grad_down))

def head_back(normed, inv_std, scaled, gain_vec, weight, grad_triple, grad_attended):
    grad_joint = jnp.dot(scaled.T, grad_triple, preferred_element_type=jnp.float32)
    grad_scaled = jnp.dot(grad_triple, weight.T, preferred_element_type=jnp.float32)
    grad_gain = lax.optimization_barrier(jnp.sum(grad_scaled * normed, axis=0))
    grad_input = (grad_attended + norm_back(grad_scaled, gain_vec, normed, inv_std)).astype(jnp.bfloat16)
    return (grad_input, (grad_joint, grad_gain))

def reference(activations, cotangent, first_gain, joint_weight, output_weight, second_gain, expand_weight, reduce_weight):
    group_count = STRIDE_H * STRIDE_W
    tokens = GRID * GRID
    per_step = math.gcd(group_count, 8)

    def regroup(tile):
        return tile.reshape(GRID, STRIDE_H, GRID, STRIDE_W, D).transpose(1, 3, 0, 2, 4).reshape(group_count // per_step, per_step * tokens, D)

    def restore(rows):
        return rows.reshape(STRIDE_H, STRIDE_W, GRID, GRID, D).transpose(2, 0, 3, 1, 4).reshape(IMG_H, IMG_W, D)

    def step_fn(running, pieces):
        act_rows, cot_rows = pieces
        inputs = act_rows.astype(jnp.float32)
        triple, scaled_first, normed_first, inv_first = project_rows(inputs, first_gain, joint_weight)
        triple_grp = triple.reshape(per_step, tokens, 3 * D)
        mixed_rows = attend_forward(triple_grp).reshape(-1, D)
        result, grad_attended, grad_mixed, tail_grads = tail_back(inputs, mixed_rows, output_weight, second_gain, expand_weight, reduce_weight, cot_rows)
        grad_triple = attend_backward(triple_grp, grad_mixed.reshape(per_step, tokens, D)).reshape(-1, 3 * D)
        grad_input, head_grads = head_back(normed_first, inv_first, scaled_first, first_gain, joint_weight, grad_triple, grad_attended)
        partials = head_grads + tail_grads
        running = tuple((old + new for old, new in zip(running, partials)))
        return (running, (result, grad_input))
    initial = (jnp.zeros((D, 3 * D), jnp.float32), jnp.zeros((D,), jnp.float32), jnp.zeros((D, D), jnp.float32), jnp.zeros((D,), jnp.float32), jnp.zeros((D, FF), jnp.float32), jnp.zeros((FF, D), jnp.float32))
    running, outputs = lax.scan(step_fn, initial, (regroup(activations), regroup(cotangent)))
    factor = POSITIONS ** (-0.5)
    grad_joint, grad_first, grad_project, grad_second, grad_expand, grad_reduce = running
    return (restore(outputs[0]), restore(outputs[1]), grad_joint * factor, grad_project * factor, grad_expand * factor, grad_reduce * factor, grad_first * factor, grad_second * factor)
```

```python
import jax
import jax.numpy as jnp
from jax import lax
from jax.experimental import pallas as pl
from jax.experimental.pallas import tpu as pltpu
from jax.sharding import PartitionSpec as P

HEADS = 12
GRID = 16


EPSILON = 1e-05
SQRT_HALF = 0.7071067811865476
INV_ROOT_TAU = 0.3989422804014327


def cut_along(array, dim, size):
    dims = array.shape
    blocks = array.reshape(*dims[:dim], size, dims[dim] // size, *dims[dim + 1 :])
    return jnp.moveaxis(blocks, dim, 0)


def in_order(blocks, dim):
    blocks = jnp.moveaxis(blocks, 0, dim)
    dims = blocks.shape
    return blocks.reshape(*dims[:dim], dims[dim] * dims[dim + 1], *dims[dim + 2 :])


def swap_kernel(source, arrived, send_sem, recv_sem):
    rows = lax.axis_size("row")
    cols = lax.axis_size("col")
    count = rows * cols
    me = lax.axis_index("row") * cols + lax.axis_index("col")
    barrier = pltpu.get_barrier_semaphore()

    def place(step):
        peer = lax.rem(me + step, count)
        return peer, (peer // cols, lax.rem(peer, cols))

    def greet(step, carry):
        pl.semaphore_signal(
            barrier, inc=1, device_id=place(step)[1], device_id_type=pl.DeviceIdType.MESH
        )
        return carry

    def send(step, carry):
        peer, where = place(step)
        pltpu.make_async_remote_copy(
            src_ref=source.at[peer],
            dst_ref=arrived.at[me],
            send_sem=send_sem,
            recv_sem=recv_sem,
            device_id=where,
            device_id_type=pl.DeviceIdType.MESH,
        ).start()
        return carry

    lax.fori_loop(1, count, greet, 0)
    pl.semaphore_wait(barrier, count - 1)
    lax.fori_loop(1, count, send, 0)
    arrived[me] = source[me]
    others = pl.ds(0, count - 1)
    pltpu.make_async_copy(source.at[others], source.at[others], send_sem).wait()
    pltpu.make_async_copy(arrived.at[others], arrived.at[others], recv_sem).wait()


def swap_blocks(blocks):
    return pl.pallas_call(
        swap_kernel,
        out_shape=jax.ShapeDtypeStruct(blocks.shape, blocks.dtype),
        in_specs=[pl.BlockSpec(memory_space=pltpu.VMEM)],
        out_specs=pl.BlockSpec(memory_space=pltpu.VMEM),
        scratch_shapes=[pltpu.SemaphoreType.DMA, pltpu.SemaphoreType.DMA],
        compiler_params=pltpu.CompilerParams(
            collective_id=0, has_side_effects=True, vmem_limit_bytes=32 * 2**20
        ),
    )(blocks)


def exchange_both(array, axis, axes, splits, concats):
    sizes = [lax.axis_size(a) for a in axes]
    blocks = cut_along(array, splits[0], sizes[0])
    blocks = jnp.moveaxis(cut_along(blocks, splits[1] + 1, sizes[1]), 0, 1)
    inside = blocks.shape[2:]
    blocks = blocks.reshape(-1, *inside)
    shape = blocks.shape
    blocks = swap_blocks(blocks.reshape(shape[0], 16, shape[-1])).reshape(shape)
    blocks = in_order(blocks.reshape(*sizes, *inside), concats[0] + 1)
    return in_order(blocks, concats[1])


def normalize(values):
    center = values - jnp.mean(values, axis=-1, keepdims=True)
    inv_std = lax.rsqrt(jnp.mean(center * center, axis=-1, keepdims=True) + EPSILON)
    return (center * inv_std, inv_std)


def norm_back(grad_norm, gain_vec, normed, inv_std):
    scaled = grad_norm * gain_vec
    return inv_std * (
        scaled
        - jnp.mean(scaled, axis=-1, keepdims=True)
        - normed * jnp.mean(scaled * normed, axis=-1, keepdims=True)
    )


def gelu_value(pre_act):
    return 0.5 * pre_act * (1.0 + jax.scipy.special.erf(pre_act * SQRT_HALF))


def gelu_slope(pre_act):
    return (
        0.5 * (1.0 + jax.scipy.special.erf(pre_act * SQRT_HALF))
        + pre_act * jnp.exp(-0.5 * pre_act * pre_act) * INV_ROOT_TAU
    )


def project_rows(inputs, gain_vec, weight):
    normed, inv_std = normalize(inputs)
    scaled = (normed * gain_vec).astype(jnp.bfloat16)
    triple = jnp.dot(scaled, weight, preferred_element_type=jnp.float32).astype(jnp.bfloat16)
    return (triple, scaled, normed, inv_std)


def split_heads(rows, feature_dim):
    return rows.reshape(rows.shape[0], rows.shape[1], HEADS, feature_dim // HEADS)


def attend(triple):
    feature_dim = triple.shape[-1] // 3
    queries = split_heads(triple[..., :feature_dim], feature_dim)
    key_rows = split_heads(triple[..., feature_dim : 2 * feature_dim], feature_dim)
    value_rows = split_heads(triple[..., 2 * feature_dim :], feature_dim)
    score_scale = (feature_dim // HEADS) ** (-0.5)
    scores = (
        jnp.einsum("bqhe,bkhe->bhqk", queries, key_rows, preferred_element_type=jnp.float32)
        * score_scale
    )
    row_max = jnp.max(scores, axis=-1, keepdims=True)
    weights = jnp.exp(scores - row_max)
    weights = weights / jnp.sum(weights, axis=-1, keepdims=True)
    return (weights, queries, key_rows, value_rows, score_scale)


def attend_forward(triple):
    weights, queries, key_rows, value_rows, score_scale = attend(triple)
    mixed_rows = jnp.einsum(
        "bhqk,bkhe->bqhe",
        weights.astype(jnp.bfloat16),
        value_rows,
        preferred_element_type=jnp.float32,
    ).astype(jnp.bfloat16)
    return mixed_rows.reshape(triple.shape[0], triple.shape[1], -1)


def attend_backward(triple, grad_mixed):
    weights, queries, key_rows, value_rows, score_scale = attend(triple)
    feature_dim = triple.shape[-1] // 3
    grad_heads = split_heads(grad_mixed, feature_dim)
    grad_weights = jnp.einsum(
        "bqhe,bkhe->bhqk", grad_heads, value_rows, preferred_element_type=jnp.float32
    )
    inner_sum = jnp.sum(weights * grad_weights, axis=-1, keepdims=True)
    grad_scores = (weights * (grad_weights - inner_sum) * score_scale).astype(jnp.bfloat16)
    grad_query = jnp.einsum(
        "bhqk,bkhe->bqhe", grad_scores, key_rows, preferred_element_type=jnp.float32
    ).astype(jnp.bfloat16)
    grad_key = jnp.einsum(
        "bhqk,bqhe->bkhe", grad_scores, queries, preferred_element_type=jnp.float32
    ).astype(jnp.bfloat16)
    grad_value = jnp.einsum(
        "bhqk,bqhe->bkhe",
        weights.astype(jnp.bfloat16),
        grad_heads,
        preferred_element_type=jnp.float32,
    ).astype(jnp.bfloat16)
    shape_out = (triple.shape[0], triple.shape[1], feature_dim)
    return jnp.concatenate(
        [grad_query.reshape(shape_out), grad_key.reshape(shape_out), grad_value.reshape(shape_out)],
        axis=-1,
    )


def by_blocks(function, operands):
    groups = operands[0].shape[0]
    per_step = 2
    stacked = tuple(
        (
            operand.reshape((groups // per_step, per_step) + operand.shape[1:])
            for operand in operands
        )
    )
    result = lax.map(lambda pieces: function(*pieces), stacked)
    return result.reshape((groups,) + result.shape[2:])


def tail_back(inputs, mixed_rows, out_weight, gain_vec, up_weight, down_weight, cot_rows):
    attended = inputs + jnp.dot(mixed_rows, out_weight, preferred_element_type=jnp.float32)
    normed, inv_std = normalize(attended)
    scaled = (normed * gain_vec).astype(jnp.bfloat16)
    pre_act = jnp.dot(scaled, up_weight, preferred_element_type=jnp.float32)
    hidden = gelu_value(pre_act).astype(jnp.bfloat16)
    result = (attended + jnp.dot(hidden, down_weight, preferred_element_type=jnp.float32)).astype(
        jnp.bfloat16
    )
    grad_down = jnp.einsum("nf,nd->fd", hidden, cot_rows, preferred_element_type=jnp.float32)
    grad_hidden = jnp.einsum(
        "nd,fd->nf", cot_rows, down_weight, preferred_element_type=jnp.float32
    ).astype(jnp.bfloat16)
    grad_pre = (grad_hidden * gelu_slope(pre_act)).astype(jnp.bfloat16)
    grad_up = jnp.einsum("nd,nf->df", scaled, grad_pre, preferred_element_type=jnp.float32)
    grad_scaled = jnp.einsum("nf,df->nd", grad_pre, up_weight, preferred_element_type=jnp.float32)
    grad_gain = jnp.sum(grad_scaled * normed, axis=0)
    grad_attended = cot_rows.astype(jnp.float32) + norm_back(grad_scaled, gain_vec, normed, inv_std)
    grad_attended_b = grad_attended.astype(jnp.bfloat16)
    grad_out = jnp.einsum(
        "nd,ne->de", mixed_rows, grad_attended_b, preferred_element_type=jnp.float32
    )
    grad_mixed = jnp.einsum(
        "ne,de->nd", grad_attended_b, out_weight, preferred_element_type=jnp.float32
    ).astype(jnp.bfloat16)
    tail_grads = (grad_out, grad_gain, grad_up, grad_down)
    return (result, grad_attended, grad_mixed, tail_grads)


def head_back(normed, inv_std, scaled, gain_vec, weight, grad_triple, grad_attended):
    grad_joint = jnp.einsum("nd,nt->dt", scaled, grad_triple, preferred_element_type=jnp.float32)
    grad_scaled = jnp.einsum("nt,dt->nd", grad_triple, weight, preferred_element_type=jnp.float32)
    grad_gain = jnp.sum(grad_scaled * normed, axis=0)
    grad_input = (grad_attended + norm_back(grad_scaled, gain_vec, normed, inv_std)).astype(
        jnp.bfloat16
    )
    return (grad_input, (grad_joint, grad_gain))


def shards(
    activations,
    cotangent,
    first_gain,
    joint_weight,
    output_weight,
    second_gain,
    expand_weight,
    reduce_weight,
):
    row_devs = lax.axis_size("row")
    col_devs = lax.axis_size("col")
    tile_rows, tile_cols, channels = activations.shape
    local_rows = GRID // row_devs
    local_cols = GRID // col_devs
    stride_rows = tile_rows // local_rows
    stride_cols = tile_cols // local_cols
    part_rows = stride_rows // row_devs
    part_cols = stride_cols // col_devs
    tokens = GRID * GRID
    factor = float(tile_rows * tile_cols * row_devs * col_devs) ** (-0.5)

    def to_layout(tile):
        return tile.reshape(
            local_rows, stride_rows, local_cols, stride_cols, tile.shape[-1]
        ).transpose(1, 3, 0, 2, 4)

    def regroup(grouped):
        return grouped.reshape(part_rows, part_cols, GRID, GRID, grouped.shape[-1])

    def from_layout(arrived):
        return arrived.transpose(2, 0, 3, 1, 4).reshape(tile_rows, tile_cols, arrived.shape[-1])

    arrived_pair = (
        exchange_both(to_layout(activations), ("row", "col"), ("row", "col"), (0, 1), (2, 3)),
        exchange_both(to_layout(cotangent), ("row", "col"), ("row", "col"), (0, 1), (2, 3)),
    )
    inputs = arrived_pair[0].reshape(-1, channels).astype(jnp.float32)
    cot_rows = arrived_pair[1].reshape(-1, channels)
    triple, scaled_first, normed_first, inv_first = project_rows(inputs, first_gain, joint_weight)
    triple_grp = triple.reshape(-1, tokens, 3 * channels)
    mixed_rows = by_blocks(attend_forward, (triple_grp,)).reshape(-1, channels)
    result, grad_attended, grad_mixed, tail_grads = tail_back(
        inputs, mixed_rows, output_weight, second_gain, expand_weight, reduce_weight, cot_rows
    )
    grad_triple = by_blocks(
        attend_backward, (triple_grp, grad_mixed.reshape(-1, tokens, channels))
    ).reshape(-1, 3 * channels)
    grad_input, head_grads = head_back(
        normed_first, inv_first, scaled_first, first_gain, joint_weight, grad_triple, grad_attended
    )
    returned = (
        exchange_both(
            regroup(result.reshape(-1, tokens, channels)),
            ("row", "col"),
            ("row", "col"),
            (2, 3),
            (0, 1),
        ),
        exchange_both(
            regroup(grad_input.reshape(-1, tokens, channels)),
            ("row", "col"),
            ("row", "col"),
            (2, 3),
            (0, 1),
        ),
    )
    block_out = from_layout(returned[0])
    grad_in_tile = from_layout(returned[1])
    grad_out, grad_second, grad_up, grad_down = tail_grads
    grad_joint, grad_first = head_grads
    summed = lax.psum(
        (grad_joint, grad_out, grad_up, grad_down, grad_first, grad_second), ("row", "col")
    )
    return (block_out, grad_in_tile) + tuple((summand * factor for summand in summed))


def solution(mesh):
    placed = (P("row", "col", None), P("row", "col", None), P(), P(), P(), P(), P(), P())
    return jax.shard_map(
        shards,
        mesh=mesh,
        in_specs=placed,
        out_specs=(P("row", "col", None), P("row", "col", None), P(), P(), P(), P(), P(), P()),
        check_vma=False,
    )
```

```python
import functools

import jax
import jax.numpy as jnp
from jax import lax
from jax.experimental import pallas as pl
from jax.experimental.pallas import tpu as pltpu
from jax.sharding import PartitionSpec as P

HEADS = 12
GRID = 16
GROUPS = 8
TOKENS = 256
D = 384
FF = 1536
WIDE = 32
CHUNK = 512

EPSILON = 1e-05
SQRT_HALF = 0.7071067811865476
INV_ROOT_TAU = 0.3989422804014327
LOG2E = 1.4426950408889634
SCORE_SCALE = WIDE ** (-0.5)
F32 = jnp.float32
BF16 = jnp.bfloat16


def dot_nn(a, b):
    return lax.dot_general(a, b, (((1,), (0,)), ((), ())), preferred_element_type=F32)


def dot_nt(a, b):
    return lax.dot_general(a, b, (((1,), (1,)), ((), ())), preferred_element_type=F32)


def dot_tn(a, b):
    return lax.dot_general(a, b, (((0,), (0,)), ((), ())), preferred_element_type=F32)


def mean0(values):
    return jnp.sum(values, axis=0, keepdims=True) * (1.0 / D)


def gelu_parts(pre):
    gauss = jnp.exp2(pre * pre * (-0.5 * LOG2E))
    t = 1.0 / (1.0 + (0.3275911 * SQRT_HALF) * jnp.abs(pre))
    poly = t * (0.127414796 + t * (-0.142248368 + t * (0.7107068705 + t * (-0.7265760135 + t * 0.5307027145))))
    tail = poly * gauss
    cdf = jnp.where(pre >= 0.0, 1.0 - tail, tail)
    return pre * cdf, cdf + pre * gauss * INV_ROOT_TAU


def spread(rows, values):
    for lane in range(D // 128):
        rows[lane] = values[:, lane * 128 : lane * 128 + 128].astype(F32)


def joined(rows):
    return jnp.concatenate([rows[lane] for lane in range(D // 128)], axis=1)


def take_group(rows, group):
    members = pl.ds(group, TOKENS, stride=GROUPS)
    return jnp.concatenate([rows[lane, members, :].T for lane in range(D // 128)], axis=0)


def put_group(rows, group, values):
    members = pl.ds(group, TOKENS, stride=GROUPS)
    for lane in range(D // 128):
        rows[lane, members, :] = values[lane * 128 : lane * 128 + 128].T


def project_group(group, x_rows, gain, joint_t, x_feat, triple, stats):
    values = take_group(x_rows, group)
    x_feat[group] = values.astype(BF16)
    center = values - mean0(values)
    inv = lax.rsqrt(mean0(center * center) + EPSILON)
    scaled = (center * inv * gain[...]).astype(BF16)
    triple[group] = dot_nn(joint_t[...], scaled).astype(BF16)


def attend_group(group, triple, mixed, stats):
    for head in range(HEADS):
        at = head * WIDE
        query = triple[group, at : at + WIDE]
        key = triple[group, D + at : D + at + WIDE]
        value = triple[group, 2 * D + at : 2 * D + at + WIDE]
        scores = dot_tn(key, query) * (SCORE_SCALE * LOG2E)
        top = jnp.max(scores, axis=0, keepdims=True)
        raised = jnp.exp2(scores - top)
        share = 1.0 / jnp.sum(raised, axis=0, keepdims=True)
        stats[group, 2 * head : 2 * head + 1] = top
        stats[group, 2 * head + 1 : 2 * head + 2] = share
        weights = (raised * share).astype(BF16)
        mixed[group, at : at + WIDE] = dot_nn(value, weights).astype(BF16)


def tail_group(
    group, x_feat, cot_rows, mixed, project, project_t, gain, expand, expand_t, reduce, reduce_t,
    result_rows, grad_att, grad_mixed, sum_project, sum_expand, sum_reduce, sum_gain,
):
    blend = mixed[group]
    cot32 = take_group(cot_rows, group)
    cot = cot32.astype(BF16)
    attended = x_feat[group].astype(F32) + dot_nn(project_t[...], blend)
    center = attended - mean0(attended)
    inv = lax.rsqrt(mean0(center * center) + EPSILON)
    normed = center * inv
    scaled = (normed * gain[...]).astype(BF16)
    result = attended
    grad_scaled = None
    for start in range(0, FF, CHUNK):
        part = slice(start, start + CHUNK)
        pre = dot_nn(expand_t[part, :], scaled)
        value, slope = gelu_parts(pre)
        hidden = value.astype(BF16)
        grad_hidden = dot_nn(reduce[part, :], cot).astype(BF16).astype(F32)
        grad_pre = (grad_hidden * slope).astype(BF16)
        result = result + dot_nn(reduce_t[:, part], hidden)
        back = dot_nn(expand[:, part], grad_pre)
        grad_scaled = back if grad_scaled is None else grad_scaled + back
        sum_reduce[part, :] += dot_nt(hidden, cot)
        sum_expand[part, :] += dot_nt(grad_pre, scaled)
    put_group(result_rows, group, result)
    sum_gain[...] += grad_scaled * normed
    lifted = grad_scaled * gain[...]
    grad = cot32 + inv * (lifted - mean0(lifted) - normed * mean0(lifted * normed))
    grad_att[group] = grad
    grad_b = grad.astype(BF16)
    sum_project[...] += dot_nt(blend, grad_b)
    grad_mixed[group] = dot_nn(project[...], grad_b).astype(BF16)


def attend_back_group(group, triple, stats, grad_mixed, grad_triple):
    for head in range(HEADS):
        at = head * WIDE
        query = triple[group, at : at + WIDE]
        key = triple[group, D + at : D + at + WIDE]
        value = triple[group, 2 * D + at : 2 * D + at + WIDE]
        grad_out = grad_mixed[group, at : at + WIDE]
        top = stats[group, 2 * head : 2 * head + 1]
        share = stats[group, 2 * head + 1 : 2 * head + 2]
        scores = dot_tn(key, query) * (SCORE_SCALE * LOG2E)
        weights = jnp.exp2(scores - top) * share
        grad_weights = dot_tn(value, grad_out)
        inner = jnp.sum(weights * grad_weights, axis=0, keepdims=True)
        grad_scores = (weights * (grad_weights - inner) * SCORE_SCALE).astype(BF16)
        grad_triple[at : at + WIDE] = dot_nn(key, grad_scores).astype(BF16)
        grad_triple[D + at : D + at + WIDE] = dot_nt(query, grad_scores).astype(BF16)
        grad_triple[2 * D + at : 2 * D + at + WIDE] = dot_nt(grad_out, weights.astype(BF16)).astype(BF16)


def head_back_group(group, x_feat, grad_att, grad_triple, gain, joint, grad_rows, sum_joint, sum_gain):
    values = x_feat[group].astype(F32)
    center = values - mean0(values)
    inv = lax.rsqrt(mean0(center * center) + EPSILON)
    normed = center * inv
    scaled = (normed * gain[...]).astype(BF16)
    sum_joint[...] += dot_nt(grad_triple[...], scaled)
    grad_scaled = dot_nn(joint[...], grad_triple[...])
    sum_gain[...] += grad_scaled * normed
    lifted = grad_scaled * gain[...]
    grad = grad_att[group] + inv * (lifted - mean0(lifted) - normed * mean0(lifted * normed))
    put_group(grad_rows, group, grad)


AXES = ("row", "col")
MESH = pl.DeviceIdType.MESH
POSITIONS = 262144
LANES = 128
BLOCK = 16
PIECE = 9
HALF = 8 * PIECE
SHARE = 2 * HALF
STRIDE = 32
ROWS = (D // LANES, GROUPS * TOKENS, LANES)
WHOLE = pl.BlockSpec(memory_space=pltpu.VMEM)


def shape(dims, dtype=BF16):
    return jax.ShapeDtypeStruct(dims, dtype)


def local_call(kernel, inputs, outs, scratch=(), flops=0, nbytes=0):
    single = not isinstance(outs, (list, tuple))
    count = 1 if single else len(outs)
    return pl.pallas_call(
        kernel,
        in_specs=[WHOLE] * len(inputs),
        out_specs=WHOLE if single else [WHOLE] * count,
        out_shape=outs,
        scratch_shapes=list(scratch),
        cost_estimate=pl.CostEstimate(flops=flops, bytes_accessed=nbytes, transcendentals=0),
        compiler_params=pltpu.CompilerParams(vmem_limit_bytes=56 * 2**20),
    )(*inputs)


def pack_kernel(tile, packed):
    def step(a, carry):
        near = tile[a].astype(F32)
        far = tile[STRIDE + a].astype(F32)
        for block in range(STRIDE // GROUPS):
            part = slice(block * GROUPS, block * GROUPS + GROUPS)
            packed[a * (STRIDE // GROUPS) + block] = jnp.concatenate([near[part], far[part]], axis=0).astype(BF16)
        return carry

    lax.fori_loop(0, STRIDE, step, 0, unroll=4)


def unpack_kernel(arrived, tile):
    def step(a, carry):
        blocks = [arrived[a * (STRIDE // GROUPS) + block].astype(F32) for block in range(STRIDE // GROUPS)]
        tile[a] = jnp.concatenate([b[:GROUPS] for b in blocks], axis=0).astype(BF16)
        tile[STRIDE + a] = jnp.concatenate([b[GROUPS:] for b in blocks], axis=0).astype(BF16)
        return carry

    lax.fori_loop(0, STRIDE, step, 0, unroll=4)


def front_kernel(arrived, gain, joint_t, x_feat, triple, mixed, stats, rows):
    spread(rows, arrived)

    def step(group, carry):
        project_group(group, rows, gain, joint_t, x_feat, triple, stats)
        attend_group(group, triple, mixed, stats)
        return carry

    lax.fori_loop(0, GROUPS, step, 0)


def middle_kernel(
    x_feat, cot, mixed, project, project_t, gain, expand, expand_t, reduce, reduce_t,
    result, grad_att, grad_mixed, grad_project, grad_expand, grad_reduce, grad_gain,
    cot_rows, result_rows, sum_project, sum_expand, sum_reduce, sum_gain,
):
    spread(cot_rows, cot)
    for total in (sum_project, sum_expand, sum_reduce, sum_gain):
        total[...] = jnp.zeros_like(total)

    def step(group, carry):
        tail_group(
            group, x_feat, cot_rows, mixed, project, project_t, gain, expand, expand_t, reduce, reduce_t,
            result_rows, grad_att, grad_mixed, sum_project, sum_expand, sum_reduce, sum_gain,
        )
        return carry

    lax.fori_loop(0, GROUPS, step, 0)
    result[...] = joined(result_rows).astype(BF16)
    for out, total in ((grad_project, sum_project), (grad_expand, sum_expand), (grad_reduce, sum_reduce)):
        out[...] = total[...].astype(BF16)
    grad_gain[...] = jnp.sum(sum_gain[...].T, axis=0, keepdims=True)


def back_kernel(
    x_feat, triple, stats, grad_mixed, grad_att, gain, joint,
    grad_in, grad_joint, grad_gain,
    grad_triple, grad_rows, sum_joint, sum_gain,
):
    for total in (sum_joint, sum_gain):
        total[...] = jnp.zeros_like(total)

    def step(group, carry):
        attend_back_group(group, triple, stats, grad_mixed, grad_triple)
        head_back_group(group, x_feat, grad_att, grad_triple, gain, joint, grad_rows, sum_joint, sum_gain)
        return carry

    lax.fori_loop(0, GROUPS, step, 0)
    grad_in[...] = joined(grad_rows).astype(BF16)
    grad_joint[...] = sum_joint[...].astype(BF16)
    grad_gain[...] = jnp.sum(sum_gain[...].T, axis=0, keepdims=True)


def total_kernel(
    expand, reduce, joint, project, gains,
    total, gain_total,
    mine, sibling, own, in_a, part, in_b, gain_pair, gain_a, gain_b,
    pair_sems, a_sems, b_sems, gather_sems, last_sems, gain_sems,
):
    row, col = lax.axis_index("row"), lax.axis_index("col")
    core = lax.rem(col, 2)
    place = col // 2
    other = (row, col + 1 - 2 * core)
    slots = (place, row)

    def peer(half, index):
        return (row, index * 2 + core) if half == 0 else (index, col)

    barrier = pltpu.get_barrier_semaphore()
    pl.semaphore_signal(barrier, inc=1, device_id=other, device_id_type=MESH)
    for half in range(2):
        for step in range(1, 8):
            index = lax.rem(slots[half] + step, 8)
            pl.semaphore_signal(barrier, inc=1, device_id=peer(half, index), device_id_type=MESH)

    for side in range(2):
        at = side * SHARE
        for source in (expand, reduce, joint, project):
            blocks = source.shape[0] // 2
            mine[at : at + blocks] = source[side * blocks : side * blocks + blocks]
            at += blocks
    gain_pair[0] = gains[...]
    pl.semaphore_wait(barrier, 15)

    def copy(source, target, sems, index, device):
        return pltpu.make_async_remote_copy(
            src_ref=source, dst_ref=target, send_sem=sems.at[0, index], recv_sem=sems.at[1, index],
            device_id=device, device_id_type=MESH,
        )

    def settle(sent, landed, sems, index):
        pltpu.make_async_copy(sent, sent, sems.at[0, index]).wait()
        pltpu.make_async_copy(landed, landed, sems.at[1, index]).wait()

    def start_all(source, target, sems, index, half):
        def step(offset, carry):
            q = lax.rem(slots[half] + offset, 8)
            copy(source(q), target, sems, index, peer(half, q)).start()
            return carry

        lax.fori_loop(1, 8, step, 0)

    away = (1 - core) * SHARE
    here = core * SHARE
    pair = [
        copy(mine.at[pl.ds(away + half * HALF, HALF)], sibling.at[half], pair_sems, half, other) for half in range(2)
    ]
    gain_first = copy(gain_pair.at[0], gain_pair.at[1], gain_sems, 0, other)
    for one in pair:
        one.start()
    gain_first.start()
    for half in range(2):
        pair[half].wait()

        def add(q, carry):
            kept = mine[pl.ds(here + half * HALF + q * PIECE, PIECE)].astype(F32)
            own[half, q] = (kept + sibling[half, pl.ds(q * PIECE, PIECE)].astype(F32)).astype(BF16)
            return carry

        lax.fori_loop(0, 8, add, 0)
        start_all(lambda q: own.at[half, q], in_a.at[half, slots[half]], a_sems, half, half)
        in_a[half, slots[half]] = own[half, slots[half]]
    gain_first.wait()
    gain_a[place] = gain_pair[0] + gain_pair[1]
    start_all(lambda q: gain_a.at[place], gain_a.at[place], gain_sems, 1, 0)

    def summed(pieces):
        acc = pieces[0].astype(F32)
        for q in range(1, 8):
            acc = acc + pieces[q].astype(F32)
        return acc

    for half in range(2):
        settle(own.at[half, pl.ds(0, 7)], in_a.at[half, pl.ds(0, 7)], a_sems, half)

        def add(block, carry):
            part[half, block] = summed([in_a[half, q, block] for q in range(8)]).astype(BF16)
            return carry

        lax.fori_loop(0, PIECE, add, 0)
        start_all(lambda q: part.at[half], in_b.at[half, slots[1 - half]], b_sems, half, 1 - half)
        in_b[half, slots[1 - half]] = part[half]
    settle(gain_a.at[pl.ds(0, 7)], gain_a.at[pl.ds(0, 7)], gain_sems, 1)
    gain_b[row] = summed([gain_a[q] for q in range(8)])
    start_all(lambda q: gain_b.at[row], gain_b.at[row], gain_sems, 2, 1)

    for half in range(2):
        settle(in_b.at[half, pl.ds(0, 7)], in_b.at[half, pl.ds(0, 7)], b_sems, half)
        base = here + half * HALF + slots[half] * PIECE

        def add(block, carry):
            total[base + block] = summed([in_b[half, q, block] for q in range(8)]).astype(BF16)
            return carry

        lax.fori_loop(0, PIECE, add, 0)
        spot = total.at[pl.ds(base, PIECE)]
        start_all(lambda q: spot, spot, gather_sems, half, half)
    settle(gain_b.at[pl.ds(0, 7)], gain_b.at[pl.ds(0, 7)], gain_sems, 2)
    gain_total[...] = summed([gain_b[q] for q in range(8)])

    last = []
    for half in range(2):
        seven = total.at[pl.ds(0, 7 * PIECE)]
        settle(seven, seven, gather_sems, half)
        spot = total.at[pl.ds(here + half * HALF, HALF)]
        last.append(copy(spot, spot, last_sems, half, other))
        last[-1].start()
    for one in last:
        one.wait()


def sum_over_devices(expand, reduce, joint, project, gains):
    dma = pltpu.SemaphoreType.DMA
    piece = (PIECE, BLOCK, D)
    return pl.pallas_call(
        total_kernel,
        in_specs=[WHOLE] * 5,
        out_specs=[WHOLE] * 2,
        out_shape=[shape((2 * SHARE, BLOCK, D)), shape((8, D), F32)],
        scratch_shapes=[
            pltpu.VMEM((2 * SHARE, BLOCK, D), BF16),
            pltpu.VMEM((2, HALF, BLOCK, D), BF16),
            pltpu.VMEM((2, 8) + piece, BF16),
            pltpu.VMEM((2, 8) + piece, BF16),
            pltpu.VMEM((2,) + piece, BF16),
            pltpu.VMEM((2, 8) + piece, BF16),
            pltpu.VMEM((2, 8, D), F32),
            pltpu.VMEM((8, 8, D), F32),
            pltpu.VMEM((8, 8, D), F32),
            dma((2, 2)), dma((2, 2)), dma((2, 2)), dma((2, 2)), dma((2, 2)), dma((2, 3)),
        ],
        cost_estimate=pl.CostEstimate(flops=10**9, bytes_accessed=10**8, transcendentals=0),
        compiler_params=pltpu.CompilerParams(
            collective_id=0, has_side_effects=True, vmem_limit_bytes=48 * 2**20
        ),
    )(*[g.reshape(-1, BLOCK, D) for g in (expand, reduce, joint, project)], gains)


def swap(blocks):
    return lax.all_to_all(blocks, AXES, split_axis=0, concat_axis=0, tiled=True)


def shards(
    activations, cotangent, first_gain, joint_weight, output_weight, second_gain, expand_weight, reduce_weight
):
    devices = lax.axis_size("row") * lax.axis_size("col")
    blocks = (devices, BLOCK, D)
    rows = (devices * BLOCK, D)
    feat = (GROUPS, D, TOKENS)
    gain_a = first_gain[:, None]
    gain_b = second_gain[:, None]

    act = swap(local_call(pack_kernel, [activations], shape(blocks))).reshape(rows)
    cot = swap(local_call(pack_kernel, [cotangent], shape(blocks))).reshape(rows)
    x_feat, triple, mixed, stats = local_call(
        front_kernel,
        [act, gain_a, joint_weight.T],
        [shape(feat), shape((GROUPS, 3 * D, TOKENS)), shape(feat), shape((GROUPS, 2 * HEADS, TOKENS), F32)],
        [pltpu.VMEM(ROWS, F32)],
        flops=4 * 10**10, nbytes=10**7,
    )
    result, grad_att, grad_mixed, part_project, part_expand, part_reduce, part_second = local_call(
        middle_kernel,
        [
            x_feat, cot, mixed, output_weight, output_weight.T, gain_b,
            expand_weight, expand_weight.T, reduce_weight, reduce_weight.T,
        ],
        [
            shape(rows), shape(feat, F32), shape(feat),
            shape((D, D)), shape((FF, D)), shape((FF, D)), shape((1, D), F32),
        ],
        [
            pltpu.VMEM(ROWS, F32), pltpu.VMEM(ROWS, F32),
            pltpu.VMEM((D, D), F32), pltpu.VMEM((FF, D), F32), pltpu.VMEM((FF, D), F32), pltpu.VMEM((D, TOKENS), F32),
        ],
        flops=4 * 10**10, nbytes=10**7,
    )
    block_out = swap(result.reshape(blocks))
    grad_in, part_joint, part_first = local_call(
        back_kernel,
        [x_feat, triple, stats, grad_mixed, grad_att, gain_a, joint_weight],
        [shape(rows), shape((3 * D, D)), shape((1, D), F32)],
        [
            pltpu.VMEM((3 * D, TOKENS), BF16), pltpu.VMEM(ROWS, F32),
            pltpu.VMEM((3 * D, D), F32), pltpu.VMEM((D, TOKENS), F32),
        ],
        flops=4 * 10**10, nbytes=10**7,
    )
    grad_in = swap(grad_in.reshape(blocks))
    gains = jnp.concatenate([part_first, part_second, jnp.zeros((6, D), F32)], axis=0)
    total, gain_total = sum_over_devices(part_expand, part_reduce, part_joint, part_project, gains)
    tile = activations.shape
    block_out = local_call(unpack_kernel, [block_out], shape(tile))
    grad_in = local_call(unpack_kernel, [grad_in], shape(tile))

    factor = float(POSITIONS) ** -0.5
    sides = total.reshape(2, SHARE * BLOCK, D)

    def cut(start, size):
        return sides[:, start : start + size].reshape(2 * size, D).astype(F32) * factor

    half = FF // 2
    grad_expand = cut(0, half).T
    grad_reduce = cut(half, half)
    grad_joint = cut(FF, 3 * D // 2).T
    grad_project = cut(FF + 3 * D // 2, D // 2)
    return (
        block_out, grad_in, grad_joint, grad_project, grad_expand, grad_reduce,
        gain_total[0] * factor, gain_total[1] * factor,
    )


def solution(mesh):
    tile = P("row", "col", None)
    return jax.shard_map(
        shards,
        mesh=mesh,
        in_specs=(tile, tile) + (P(),) * 6,
        out_specs=(tile, tile) + (P(),) * 6,
        check_vma=False,
    )
```

```python
import jax
import jax.numpy as jnp
from jax import lax
from jax.experimental import pallas as pl
from jax.experimental.pallas import tpu as pltpu
from jax.sharding import PartitionSpec as P

HEADS = 12
GRID = 16
GROUPS = 8
TOKENS = 256
D = 384
FF = 1536
WIDE = 32
CHUNK = 512

EPSILON = 1e-05
SQRT_HALF = 0.7071067811865476
INV_ROOT_TAU = 0.3989422804014327
LOG2E = 1.4426950408889634
SCORE_SCALE = WIDE ** (-0.5)
F32 = jnp.float32
BF16 = jnp.bfloat16


def dot_nn(a, b):
    return lax.dot_general(a, b, (((1,), (0,)), ((), ())), preferred_element_type=F32)


def dot_nt(a, b):
    return lax.dot_general(a, b, (((1,), (1,)), ((), ())), preferred_element_type=F32)


def dot_tn(a, b):
    return lax.dot_general(a, b, (((0,), (0,)), ((), ())), preferred_element_type=F32)


def mean0(values):
    return jnp.sum(values, axis=0, keepdims=True) * (1.0 / D)


def gelu_parts(pre):
    gauss = jnp.exp2(pre * pre * (-0.5 * LOG2E))
    t = 1.0 / (1.0 + (0.3275911 * SQRT_HALF) * jnp.abs(pre))
    poly = t * (0.127414796 + t * (-0.142248368 + t * (0.7107068705 + t * (-0.7265760135 + t * 0.5307027145))))
    tail = poly * gauss
    cdf = jnp.where(pre >= 0.0, 1.0 - tail, tail)
    return pre * cdf, cdf + pre * gauss * INV_ROOT_TAU


def take_group(rows, group):
    members = pl.ds(group, TOKENS, stride=GROUPS)
    return jnp.concatenate([rows[lane, members, :].T for lane in range(D // 128)], axis=0)


def put_group(rows, group, values):
    members = pl.ds(group, TOKENS, stride=GROUPS)
    for lane in range(D // 128):
        rows[lane, members, :] = values[lane * 128 : lane * 128 + 128].T


def project_group(group, x_rows, gain, joint_t, x_feat, triple, stats):
    values = take_group(x_rows, group)
    x_feat[group] = values.astype(BF16)
    center = values - mean0(values)
    inv = lax.rsqrt(mean0(center * center) + EPSILON)
    scaled = (center * inv * gain[...]).astype(BF16)
    triple[group] = dot_nn(joint_t[...], scaled).astype(BF16)


def attend_group(group, triple, mixed, stats):
    for head in range(HEADS):
        at = head * WIDE
        query = triple[group, at : at + WIDE]
        key = triple[group, D + at : D + at + WIDE]
        value = triple[group, 2 * D + at : 2 * D + at + WIDE]
        scores = dot_tn(key, query) * (SCORE_SCALE * LOG2E)
        top = jnp.max(scores, axis=0, keepdims=True)
        raised = jnp.exp2(scores - top)
        share = 1.0 / jnp.sum(raised, axis=0, keepdims=True)
        stats[group, 2 * head : 2 * head + 1] = top
        stats[group, 2 * head + 1 : 2 * head + 2] = share
        weights = (raised * share).astype(BF16)
        mixed[group, at : at + WIDE] = dot_nn(value, weights).astype(BF16)


def tail_group(
    group, x_feat, cot_rows, mixed, project, project_t, gain, expand, expand_t, reduce, reduce_t,
    result_rows, grad_att, grad_mixed, sum_project, sum_expand, sum_reduce, sum_gain,
):
    blend = mixed[group]
    cot32 = take_group(cot_rows, group)
    cot = cot32.astype(BF16)
    attended = x_feat[group].astype(F32) + dot_nn(project_t[...], blend)
    center = attended - mean0(attended)
    inv = lax.rsqrt(mean0(center * center) + EPSILON)
    normed = center * inv
    scaled = (normed * gain[...]).astype(BF16)
    result = attended
    grad_scaled = None
    for start in range(0, FF, CHUNK):
        part = slice(start, start + CHUNK)
        pre = dot_nn(expand_t[part, :], scaled)
        value, slope = gelu_parts(pre)
        hidden = value.astype(BF16)
        grad_hidden = dot_nn(reduce[part, :], cot).astype(BF16).astype(F32)
        grad_pre = (grad_hidden * slope).astype(BF16)
        result = result + dot_nn(reduce_t[:, part], hidden)
        back = dot_nn(expand[:, part], grad_pre)
        grad_scaled = back if grad_scaled is None else grad_scaled + back
        sum_reduce[part, :] += dot_nt(hidden, cot)
        sum_expand[part, :] += dot_nt(grad_pre, scaled)
    put_group(result_rows, group, result)
    sum_gain[...] += grad_scaled * normed
    lifted = grad_scaled * gain[...]
    grad = cot32 + inv * (lifted - mean0(lifted) - normed * mean0(lifted * normed))
    grad_att[group] = grad
    grad_b = grad.astype(BF16)
    sum_project[...] += dot_nt(blend, grad_b)
    grad_mixed[group] = dot_nn(project[...], grad_b).astype(BF16)


def attend_back_group(group, triple, stats, grad_mixed, grad_triple):
    for head in range(HEADS):
        at = head * WIDE
        query = triple[group, at : at + WIDE]
        key = triple[group, D + at : D + at + WIDE]
        value = triple[group, 2 * D + at : 2 * D + at + WIDE]
        grad_out = grad_mixed[group, at : at + WIDE]
        top = stats[group, 2 * head : 2 * head + 1]
        share = stats[group, 2 * head + 1 : 2 * head + 2]
        scores = dot_tn(key, query) * (SCORE_SCALE * LOG2E)
        weights = jnp.exp2(scores - top) * share
        grad_weights = dot_tn(value, grad_out)
        inner = jnp.sum(weights * grad_weights, axis=0, keepdims=True)
        grad_scores = (weights * (grad_weights - inner) * SCORE_SCALE).astype(BF16)
        grad_triple[at : at + WIDE] = dot_nn(key, grad_scores).astype(BF16)
        grad_triple[D + at : D + at + WIDE] = dot_nt(query, grad_scores).astype(BF16)
        grad_triple[2 * D + at : 2 * D + at + WIDE] = dot_nt(grad_out, weights.astype(BF16)).astype(BF16)


def head_back_group(group, x_feat, grad_att, grad_triple, gain, joint, grad_rows, sum_joint, sum_gain):
    values = x_feat[group].astype(F32)
    center = values - mean0(values)
    inv = lax.rsqrt(mean0(center * center) + EPSILON)
    normed = center * inv
    scaled = (normed * gain[...]).astype(BF16)
    sum_joint[...] += dot_nt(grad_triple[...], scaled)
    grad_scaled = dot_nn(joint[...], grad_triple[...])
    sum_gain[...] += grad_scaled * normed
    lifted = grad_scaled * gain[...]
    grad = grad_att[group] + inv * (lifted - mean0(lifted) - normed * mean0(lifted * normed))
    put_group(grad_rows, group, grad)


AXES = ("row", "col")
MESH = pl.DeviceIdType.MESH
POSITIONS = 262144
DEVICES = 128
LANES = 128
BLOCK = 16
STRIDE = 32
SPLIT = STRIDE // GROUPS
ROWS = (D // LANES, GROUPS * TOKENS, LANES)
WHOLE = pl.BlockSpec(memory_space=pltpu.VMEM)


def shape(dims, dtype=BF16):
    return jax.ShapeDtypeStruct(dims, dtype)


def pack(tile, packed):
    def step(a, carry):
        near = tile[a].astype(F32)
        far = tile[STRIDE + a].astype(F32)
        for block in range(SPLIT):
            part = slice(block * GROUPS, block * GROUPS + GROUPS)
            packed[a * SPLIT + block] = jnp.concatenate([near[part], far[part]], axis=0).astype(BF16)
        return carry

    lax.fori_loop(0, STRIDE, step, 0, unroll=2)


def unpack(arrived, tile):
    def step(a, carry):
        blocks = [arrived[a * SPLIT + block].astype(F32) for block in range(SPLIT)]
        tile[a] = jnp.concatenate([b[:GROUPS] for b in blocks], axis=0).astype(BF16)
        tile[STRIDE + a] = jnp.concatenate([b[GROUPS:] for b in blocks], axis=0).astype(BF16)
        return carry

    lax.fori_loop(0, STRIDE, step, 0, unroll=4)


def spread(rows, arrived):
    def step(part, carry):
        values = arrived[pl.ds(part * 8, 8)].astype(F32).reshape(8 * BLOCK, D)
        at = pl.multiple_of(part * 8 * BLOCK, 8 * BLOCK)
        for lane in range(D // LANES):
            rows[lane, pl.ds(at, 8 * BLOCK), :] = values[:, lane * LANES : lane * LANES + LANES]
        return carry

    lax.fori_loop(0, DEVICES // 8, step, 0)


def gather_rows(rows, packed):
    def step(part, carry):
        at = pl.multiple_of(part * 8 * BLOCK, 8 * BLOCK)
        values = jnp.concatenate([rows[lane, pl.ds(at, 8 * BLOCK), :] for lane in range(D // LANES)], axis=1)
        packed[pl.ds(part * 8, 8)] = values.astype(BF16).reshape(8, BLOCK, D)
        return carry

    lax.fori_loop(0, DEVICES // 8, step, 0)


class Place:
    def __init__(self):
        self.row = lax.axis_index("row")
        self.col = lax.axis_index("col")
        self.core = lax.rem(self.col, 2)
        self.other = (self.row, self.col + 1 - 2 * self.core)
        self.slots = (self.col // 2, self.row)
        self.me = self.row * 16 + self.col

    def along(self, half, index):
        return (self.row, index * 2 + self.core) if half == 0 else (index, self.col)

    def apart(self, step):
        jump = lax.rem(step * 45, DEVICES)
        x = lax.rem(lax.rem(self.row, 2) * 2 + self.col // 8 + (jump // 2) % 4, 4)
        y = lax.rem((self.col // 2) % 4 + (jump // 8) % 4, 4)
        z = lax.rem(self.row // 2 + jump // 32, 4)
        core = lax.rem(self.core + jump % 2, 2)
        row = z * 2 + x // 2
        col = (x % 2) * 8 + y * 2 + core
        return row, col


def remote(source, target, sems, index, device):
    return pltpu.make_async_remote_copy(
        src_ref=source, dst_ref=target, send_sem=sems.at[0, index], recv_sem=sems.at[1, index],
        device_id=device, device_id_type=MESH,
    )


def settle(some, sems, side, index):
    pltpu.make_async_copy(some, some, sems.at[side, index]).wait()


def swap_start(place, packed, arrived, sems, index):
    def send(step, carry):
        row, col = place.apart(step)
        remote(packed.at[row * 16 + col], arrived.at[place.me], sems, index, (row, col)).start()
        return carry

    lax.fori_loop(1, DEVICES, send, 0)
    arrived[place.me] = packed[place.me]


def summed(pieces):
    acc = pieces[0].astype(F32)
    for piece in pieces[1:]:
        acc = acc + piece.astype(F32)
    return acc


class DeviceSum:
    def __init__(self, place, sums, total, away, sibling, in_a, part, in_b, sems):
        self.place, self.sums, self.total = place, sums, total
        self.away, self.sibling, self.in_a, self.part, self.in_b, self.sems = away, sibling, in_a, part, in_b, sems
        self.piece = part.shape[1]
        self.half = 8 * self.piece
        self.here = place.core * 2 * self.half

    def rows_of(self, core, half, q):
        start = pl.multiple_of((core * 2 * self.half + half * self.half + q * self.piece) * BLOCK, BLOCK)
        return self.sums[pl.ds(start, self.piece * BLOCK), :]

    def shout(self, source, target, index, half):
        def step(offset, carry):
            q = lax.rem(self.place.slots[half] + offset, 8)
            remote(source(q), target, self.sems, index, self.place.along(half, q)).start()
            return carry

        lax.fori_loop(1, 8, step, 0)

    def start(self):
        for half in range(2):
            def cast(q, carry):
                rows = self.rows_of(1 - self.place.core, half, q).astype(BF16)
                self.away[half, q] = rows.reshape(self.piece, BLOCK, D)
                return carry

            lax.fori_loop(0, 8, cast, 0)
            remote(self.away.at[half], self.sibling.at[half], self.sems, half, self.place.other).start()

    def round_a(self):
        for half in range(2):
            settle(self.away.at[half], self.sems, 0, half)
            settle(self.sibling.at[half], self.sems, 1, half)

            def add(q, carry):
                kept = self.rows_of(self.place.core, half, q).reshape(self.piece, BLOCK, D)
                self.away[half, q] = (kept + self.sibling[half, q].astype(F32)).astype(BF16)
                return carry

            lax.fori_loop(0, 8, add, 0)
            slot = self.place.slots[half]
            self.shout(lambda q: self.away.at[half, q], self.in_a.at[half, slot], 2 + half, half)
            self.in_a[half, slot] = self.away[half, slot]

    def round_b(self):
        for half in range(2):
            settle(self.away.at[half, pl.ds(0, 7)], self.sems, 0, 2 + half)
            settle(self.in_a.at[half, pl.ds(0, 7)], self.sems, 1, 2 + half)

            def add(block, carry):
                self.part[half, block] = summed([self.in_a[half, q, block] for q in range(8)]).astype(BF16)
                return carry

            lax.fori_loop(0, self.piece, add, 0)
            slot = self.place.slots[1 - half]
            self.shout(lambda q: self.part.at[half], self.in_b.at[half, slot], 4 + half, 1 - half)
            self.in_b[half, slot] = self.part[half]

    def round_c(self):
        for half in range(2):
            settle(self.in_b.at[half, pl.ds(0, 7)], self.sems, 0, 4 + half)
            settle(self.in_b.at[half, pl.ds(0, 7)], self.sems, 1, 4 + half)
            base = self.here + half * self.half + self.place.slots[half] * self.piece

            def add(block, carry):
                self.total[base + block] = summed([self.in_b[half, q, block] for q in range(8)]).astype(BF16)
                return carry

            lax.fori_loop(0, self.piece, add, 0)
            spot = self.total.at[pl.ds(base, self.piece)]
            self.shout(lambda q: spot, spot, 6 + half, half)

    def round_d(self):
        for half in range(2):
            seven = self.total.at[pl.ds(0, 7 * self.piece)]
            settle(seven, self.sems, 0, 6 + half)
            settle(seven, self.sems, 1, 6 + half)
            spot = self.total.at[pl.ds(self.here + half * self.half, self.half)]
            remote(spot, spot, self.sems, 8 + half, self.place.other).start()

    def finish(self):
        for half in range(2):
            spot = self.total.at[pl.ds(0, self.half)]
            settle(spot, self.sems, 0, 8 + half)
            settle(spot, self.sems, 1, 8 + half)


def whole_kernel(
    activations, cotangent, first_gain, joint, project, second_gain, expand, reduce,
    block_out, grad_in, total_mlp, total_rest, total_gain,
    packed_a, packed_b, act, cot, rows_a, rows_b,
    gain_a, gain_b, joint_t, project_t, expand_t, reduce_t,
    x_feat, triple, mixed, stats, grad_att, grad_mixed, grad_triple,
    sum_mlp, sum_rest, sum_first, sum_second,
    mlp_away, mlp_sibling, mlp_in_a, mlp_part, mlp_in_b,
    rest_away, rest_sibling, rest_in_a, rest_part, rest_in_b,
    gain_pair, gain_x, gain_y,
    swap_sems, mlp_sems, rest_sems, gain_sems,
):
    place = Place()
    barrier = pltpu.get_barrier_semaphore()

    def greet(step, carry):
        pl.semaphore_signal(barrier, inc=1, device_id=place.apart(step), device_id_type=MESH)
        return carry

    lax.fori_loop(1, DEVICES, greet, 0)
    pack(activations, packed_a)
    pl.semaphore_wait(barrier, DEVICES - 1)
    swap_start(place, packed_a, act, swap_sems, 0)
    pack(cotangent, packed_b)
    swap_start(place, packed_b, cot, swap_sems, 1)
    gain_a[...] = jnp.broadcast_to(first_gain[...], (TOKENS, D)).T
    gain_b[...] = jnp.broadcast_to(second_gain[...], (TOKENS, D)).T
    for natural, turned in ((joint, joint_t), (project, project_t), (expand, expand_t)):
        for start in range(0, natural.shape[1], D):
            turned[start : start + D, :] = natural[:, start : start + D].T
    for start in range(0, FF, D):
        reduce_t[:, start : start + D] = reduce[start : start + D, :].T
    for sums in (sum_mlp, sum_rest, sum_first, sum_second):
        sums[...] = jnp.zeros_like(sums)

    others = pl.ds(0, DEVICES - 1)
    settle(act.at[others], swap_sems, 1, 0)
    spread(rows_a, act)

    def front(group, carry):
        project_group(group, rows_a, gain_a, joint_t, x_feat, triple, stats)
        attend_group(group, triple, mixed, stats)
        return carry

    lax.fori_loop(0, GROUPS, front, 0)
    settle(cot.at[others], swap_sems, 1, 1)
    spread(rows_b, cot)
    sum_project = sum_rest.at[pl.ds(3 * D, D)]
    sum_joint = sum_rest.at[pl.ds(0, 3 * D)]
    sum_expand = sum_mlp.at[pl.ds(0, FF)]
    sum_reduce = sum_mlp.at[pl.ds(FF, FF)]

    def middle(group, carry):
        tail_group(
            group, x_feat, rows_b, mixed, project, project_t, gain_b, expand, expand_t, reduce, reduce_t,
            rows_a, grad_att, grad_mixed, sum_project, sum_expand, sum_reduce, sum_second,
        )
        return carry

    lax.fori_loop(0, GROUPS, middle, 0)
    mlp = DeviceSum(place, sum_mlp, total_mlp, mlp_away, mlp_sibling, mlp_in_a, mlp_part, mlp_in_b, mlp_sems)
    mlp.start()
    settle(packed_a.at[others], swap_sems, 0, 0)
    gather_rows(rows_a, packed_a)
    swap_start(place, packed_a, block_out, swap_sems, 2)

    def back(group, carry):
        for turn, work in ((1, mlp.round_a), (3, mlp.round_b), (5, mlp.round_c), (7, mlp.round_d)):
            pl.when(group == turn)(work)
        attend_back_group(group, triple, stats, grad_mixed, grad_triple)
        head_back_group(group, x_feat, grad_att, grad_triple, gain_a, joint, rows_b, sum_joint, sum_first)
        return carry

    lax.fori_loop(0, GROUPS, back, 0)
    rest = DeviceSum(place, sum_rest, total_rest, rest_away, rest_sibling, rest_in_a, rest_part, rest_in_b, rest_sems)
    rest.start()
    both = [jnp.sum(sums[...].T, axis=0, keepdims=True) for sums in (sum_first, sum_second)]
    gain_pair[0] = jnp.concatenate(both + [jnp.zeros((6, D), F32)], axis=0)
    gain_first = remote(gain_pair.at[0], gain_pair.at[1], gain_sems, 0, place.other)
    gain_first.start()
    settle(packed_b.at[others], swap_sems, 0, 1)
    gather_rows(rows_b, packed_b)
    swap_start(place, packed_b, grad_in, swap_sems, 3)
    mlp.finish()

    def gain_round(values, slots, index, half):
        slot = place.slots[half]
        slots[slot] = values

        def step(offset, carry):
            q = lax.rem(slot + offset, 8)
            remote(slots.at[slot], slots.at[slot], gain_sems, index, place.along(half, q)).start()
            return carry

        lax.fori_loop(1, 8, step, 0)

    def gain_sum(slots, index):
        settle(slots.at[pl.ds(0, 7)], gain_sems, 0, index)
        settle(slots.at[pl.ds(0, 7)], gain_sems, 1, index)
        return summed([slots[q] for q in range(8)])

    rest.round_a()
    gain_first.wait()
    gain_round(gain_pair[0] + gain_pair[1], gain_x, 1, 0)
    rest.round_b()
    gain_round(gain_sum(gain_x, 1), gain_y, 2, 1)
    rest.round_c()
    total_gain[...] = gain_sum(gain_y, 2)
    rest.round_d()
    settle(packed_a.at[others], swap_sems, 0, 2)
    settle(block_out.at[others], swap_sems, 1, 2)
    settle(packed_b.at[others], swap_sems, 0, 3)
    settle(grad_in.at[others], swap_sems, 1, 3)
    rest.finish()


def finish_kernel(out_blocks, grad_blocks, mlp, rest, gains, block_out, grad_in, g_joint, g_project, g_expand, g_reduce, g_first, g_second):
    factor = float(POSITIONS) ** -0.5
    unpack(out_blocks, block_out)
    unpack(grad_blocks, grad_in)

    def natural(source, at, count):
        return source[at : at + count].astype(F32).reshape(count * BLOCK, D) * factor

    step = D // BLOCK
    for part in range(FF // D):
        span = slice(part * D, part * D + D)
        g_expand[:, span] = natural(mlp, part * step, step).T
        g_reduce[span, :] = natural(mlp, FF // BLOCK + part * step, step)
    for part in range(3):
        g_joint[:, part * D : part * D + D] = natural(rest, part * step, step).T
    g_project[...] = natural(rest, 3 * step, step)
    g_first[...] = gains[0:1] * factor
    g_second[...] = gains[1:2] * factor


def shards(
    activations, cotangent, first_gain, joint_weight, output_weight, second_gain, expand_weight, reduce_weight
):
    dma = pltpu.SemaphoreType.DMA
    blocks = (DEVICES, BLOCK, D)
    feat = (GROUPS, D, TOKENS)
    mlp, rest = 2 * FF, 4 * D

    def sum_scratch(rows):
        piece = rows // 32 // BLOCK
        spread_out = (2, 8, piece, BLOCK, D)
        return [
            pltpu.VMEM(spread_out, BF16), pltpu.VMEM(spread_out, BF16), pltpu.VMEM(spread_out, BF16),
            pltpu.VMEM((2, piece, BLOCK, D), BF16), pltpu.VMEM(spread_out, BF16),
        ]

    out_blocks, grad_blocks, total_mlp, total_rest, total_gain = pl.pallas_call(
        whole_kernel,
        in_specs=[WHOLE] * 8,
        out_specs=[WHOLE] * 5,
        out_shape=[
            shape(blocks), shape(blocks), shape((mlp // BLOCK, BLOCK, D)), shape((rest // BLOCK, BLOCK, D)),
            shape((8, D), F32),
        ],
        scratch_shapes=[
            pltpu.VMEM(blocks, BF16), pltpu.VMEM(blocks, BF16), pltpu.VMEM(blocks, BF16), pltpu.VMEM(blocks, BF16),
            pltpu.VMEM(ROWS, F32), pltpu.VMEM(ROWS, F32),
            pltpu.VMEM((D, TOKENS), F32), pltpu.VMEM((D, TOKENS), F32),
            pltpu.VMEM((3 * D, D), BF16), pltpu.VMEM((D, D), BF16), pltpu.VMEM((FF, D), BF16), pltpu.VMEM((D, FF), BF16),
            pltpu.VMEM(feat, BF16), pltpu.VMEM((GROUPS, 3 * D, TOKENS), BF16), pltpu.VMEM(feat, BF16),
            pltpu.VMEM((GROUPS, 2 * HEADS, TOKENS), F32), pltpu.VMEM(feat, F32), pltpu.VMEM(feat, BF16),
            pltpu.VMEM((3 * D, TOKENS), BF16),
            pltpu.VMEM((mlp, D), F32), pltpu.VMEM((rest, D), F32), pltpu.VMEM((D, TOKENS), F32), pltpu.VMEM((D, TOKENS), F32),
            *sum_scratch(mlp), *sum_scratch(rest),
            pltpu.VMEM((2, 8, D), F32), pltpu.VMEM((8, 8, D), F32), pltpu.VMEM((8, 8, D), F32),
            dma((2, 4)), dma((2, 10)), dma((2, 10)), dma((2, 3)),
        ],
        cost_estimate=pl.CostEstimate(flops=12 * 10**10, bytes_accessed=10**8, transcendentals=0),
        compiler_params=pltpu.CompilerParams(
            collective_id=0, has_side_effects=True, vmem_limit_bytes=63 * 2**20
        ),
    )(
        activations, cotangent, first_gain[None, :], joint_weight, output_weight, second_gain[None, :],
        expand_weight, reduce_weight,
    )
    tile = activations.shape
    outs = [
        shape(tile), shape(tile), shape((D, 3 * D), F32), shape((D, D), F32), shape((D, FF), F32), shape((FF, D), F32),
        shape((1, D), F32), shape((1, D), F32),
    ]
    results = pl.pallas_call(
        finish_kernel,
        in_specs=[WHOLE] * 5,
        out_specs=[WHOLE] * len(outs),
        out_shape=outs,
        compiler_params=pltpu.CompilerParams(vmem_limit_bytes=48 * 2**20),
    )(out_blocks, grad_blocks, total_mlp, total_rest, total_gain)
    return tuple(results[:6]) + (results[6][0], results[7][0])


def solution(mesh):
    tile = P("row", "col", None)
    return jax.shard_map(
        shards,
        mesh=mesh,
        in_specs=(tile, tile) + (P(),) * 6,
        out_specs=(tile, tile) + (P(),) * 6,
        check_vma=False,
    )
```

```python
import jax
import jax.numpy as jnp
from jax import lax
from jax.experimental import pallas as pl
from jax.experimental.pallas import tpu as pltpu
from jax.sharding import PartitionSpec as P

HEADS = 12
GRID = 16
GROUPS = 8
TOKENS = 256
D = 384
FF = 1536
WIDE = 32
CHUNK = 512

EPSILON = 1e-05
SQRT_HALF = 0.7071067811865476
INV_ROOT_TAU = 0.3989422804014327
LOG2E = 1.4426950408889634
SCORE_SCALE = WIDE ** (-0.5)
F32 = jnp.float32
BF16 = jnp.bfloat16


def dot_nn(a, b):
    return lax.dot_general(a, b, (((1,), (0,)), ((), ())), preferred_element_type=F32)


def dot_nt(a, b):
    return lax.dot_general(a, b, (((1,), (1,)), ((), ())), preferred_element_type=F32)


def dot_tn(a, b):
    return lax.dot_general(a, b, (((0,), (0,)), ((), ())), preferred_element_type=F32)


def mean0(values):
    return jnp.sum(values, axis=0, keepdims=True) * (1.0 / D)


def gelu_parts(pre):
    gauss = jnp.exp2(pre * pre * (-0.5 * LOG2E))
    t = 1.0 / (1.0 + (0.3275911 * SQRT_HALF) * jnp.abs(pre))
    poly = t * (0.127414796 + t * (-0.142248368 + t * (0.7107068705 + t * (-0.7265760135 + t * 0.5307027145))))
    tail = poly * gauss
    cdf = jnp.where(pre >= 0.0, 1.0 - tail, tail)
    return pre * cdf, cdf + pre * gauss * INV_ROOT_TAU


def members(group):
    start = (group // (GROUPS // 2)) * (GROUPS // 2 * TOKENS) + lax.rem(group, GROUPS // 2)
    return pl.ds(start, TOKENS, stride=GROUPS // 2)


def take_group(rows, group):
    return jnp.concatenate([rows[lane, members(group), :].T for lane in range(D // 128)], axis=0)


def put_group(rows, group, values):
    for lane in range(D // 128):
        rows[lane, members(group), :] = values[lane * 128 : lane * 128 + 128].T


def project_group(group, x_rows, gain, joint_t, x_feat, scaled_first, triple):
    values = take_group(x_rows, group)
    x_feat[group] = values.astype(BF16)
    center = values - mean0(values)
    inv = lax.rsqrt(mean0(center * center) + EPSILON)
    scaled = (center * inv * gain[...]).astype(BF16)
    scaled_first[group] = scaled
    triple[group] = dot_nn(joint_t[...], scaled).astype(BF16)


def head_scores(triple, group, head):
    at = head * WIDE
    query = triple[group, at : at + WIDE]
    key = triple[group, D + at : D + at + WIDE]
    return dot_tn(key, query) * (SCORE_SCALE * LOG2E)


def attend_group(group, triple, mixed, stats):
    ahead = head_scores(triple, group, 0)
    for head in range(HEADS):
        at = head * WIDE
        scores = ahead
        if head + 1 < HEADS:
            ahead = head_scores(triple, group, head + 1)
        value = triple[group, 2 * D + at : 2 * D + at + WIDE]
        top = jnp.max(scores, axis=0, keepdims=True)
        raised = jnp.exp2(scores - top)
        share = 1.0 / jnp.sum(raised, axis=0, keepdims=True)
        stats[group, 2 * head : 2 * head + 1] = top
        stats[group, 2 * head + 1 : 2 * head + 2] = share
        weights = (raised * share).astype(BF16)
        mixed[group, at : at + WIDE] = dot_nn(value, weights).astype(BF16)


def tail_group(
    group, x_feat, cot_rows, mixed, project, project_t, gain, expand, expand_t, reduce, reduce_t,
    result_rows, grad_att, grad_mixed, sum_project, sum_expand, sum_reduce, sum_gain,
):
    blend = mixed[group]
    cot32 = take_group(cot_rows, group)
    cot = cot32.astype(BF16)
    attended = x_feat[group].astype(F32) + dot_nn(project_t[...], blend)
    center = attended - mean0(attended)
    inv = lax.rsqrt(mean0(center * center) + EPSILON)
    normed = center * inv
    scaled = (normed * gain[...]).astype(BF16)
    result = attended
    grad_scaled = None
    def chunk_pair(start):
        part = slice(start, start + CHUNK)
        return dot_nn(expand_t[part, :], scaled), dot_nn(reduce[part, :], cot)

    ahead = chunk_pair(0)
    for start in range(0, FF, CHUNK):
        part = slice(start, start + CHUNK)
        pre, grad_hidden = ahead
        if start + CHUNK < FF:
            ahead = chunk_pair(start + CHUNK)
        value, slope = gelu_parts(pre)
        hidden = value.astype(BF16)
        grad_pre = (grad_hidden.astype(BF16).astype(F32) * slope).astype(BF16)
        result = result + dot_nn(reduce_t[:, part], hidden)
        back = dot_nn(expand[:, part], grad_pre)
        grad_scaled = back if grad_scaled is None else grad_scaled + back
        sum_reduce[part, :] += dot_nt(hidden, cot)
        sum_expand[part, :] += dot_nt(grad_pre, scaled)
    put_group(result_rows, group, result)
    sum_gain[...] += grad_scaled * normed
    lifted = grad_scaled * gain[...]
    grad = cot32 + inv * (lifted - mean0(lifted) - normed * mean0(lifted * normed))
    grad_att[group] = grad
    grad_b = grad.astype(BF16)
    sum_project[...] += dot_nt(blend, grad_b)
    grad_mixed[group] = dot_nn(project[...], grad_b).astype(BF16)


def head_pair(triple, grad_mixed, group, head):
    at = head * WIDE
    value = triple[group, 2 * D + at : 2 * D + at + WIDE]
    return head_scores(triple, group, head), dot_tn(value, grad_mixed[group, at : at + WIDE])


def attend_back_group(group, scaled_first, triple, stats, grad_mixed, grad_triple, sum_joint):
    def spill(head, grad_scores, weights):
        at = head * WIDE
        query = triple[group, at : at + WIDE]
        key = triple[group, D + at : D + at + WIDE]
        grad_out = grad_mixed[group, at : at + WIDE]
        grad_triple[at : at + WIDE] = dot_nn(key, grad_scores).astype(BF16)
        grad_triple[D + at : D + at + WIDE] = dot_nt(query, grad_scores).astype(BF16)
        grad_triple[2 * D + at : 2 * D + at + WIDE] = dot_nt(grad_out, weights).astype(BF16)

    ahead = head_pair(triple, grad_mixed, group, 0)
    for head in range(HEADS):
        scores, grad_weights = ahead
        if head + 1 < HEADS:
            ahead = head_pair(triple, grad_mixed, group, head + 1)
        top = stats[group, 2 * head : 2 * head + 1]
        share = stats[group, 2 * head + 1 : 2 * head + 2]
        weights = jnp.exp2(scores - top) * share
        inner = jnp.sum(weights * grad_weights, axis=0, keepdims=True)
        grad_scores = (weights * (grad_weights - inner) * SCORE_SCALE).astype(BF16)
        spill(head, grad_scores, weights.astype(BF16))
    triple[group] = grad_triple[...]
    sum_joint[...] += dot_nt(grad_triple[...], scaled_first[group])


def head_back_group(group, x_feat, grad_att, grad_triple, gain, joint, grad_rows, sum_gain):
    values = x_feat[group].astype(F32)
    center = values - mean0(values)
    inv = lax.rsqrt(mean0(center * center) + EPSILON)
    normed = center * inv
    grad_scaled = dot_nn(joint[...], grad_triple[group])
    sum_gain[...] += grad_scaled * normed
    lifted = grad_scaled * gain[...]
    grad = grad_att[group] + inv * (lifted - mean0(lifted) - normed * mean0(lifted * normed))
    put_group(grad_rows, group, grad)


AXES = ("row", "col")
MESH = pl.DeviceIdType.MESH
POSITIONS = 262144
DEVICES = 128
LANES = 128
BLOCK = 8
TALL = 16
STRIDE = 32
SPLIT = STRIDE // GROUPS
ROWS = (D // LANES, GROUPS * TOKENS, LANES)
WHOLE = pl.BlockSpec(memory_space=pltpu.VMEM)


def shape(dims, dtype=BF16):
    return jax.ShapeDtypeStruct(dims, dtype)


def pack(tile, packed):
    few = GROUPS // 2

    def step(a, carry):
        near = tile[a].astype(F32)
        far = tile[STRIDE + a].astype(F32)
        for block in range(SPLIT):
            for half in range(2):
                at = block * GROUPS + half * few
                both = jnp.concatenate([near[at : at + few], far[at : at + few]], axis=0)
                packed[half, a * SPLIT + block] = both.astype(BF16)
        return carry

    lax.fori_loop(0, STRIDE, step, 0, unroll=2)


def spread(rows, arrived, half):
    def step(part, carry):
        values = arrived[half, pl.ds(part * 16, 16)].astype(F32).reshape(16 * BLOCK, D)
        at = pl.multiple_of((half * DEVICES + part * 16) * BLOCK, 16 * BLOCK)
        for lane in range(D // LANES):
            rows[lane, pl.ds(at, 16 * BLOCK), :] = values[:, lane * LANES : lane * LANES + LANES]
        return carry

    lax.fori_loop(0, DEVICES // 16, step, 0)


def gather_rows(rows, packed, half):
    def step(part, carry):
        at = pl.multiple_of((half * DEVICES + part * 16) * BLOCK, 16 * BLOCK)
        values = jnp.concatenate([rows[lane, pl.ds(at, 16 * BLOCK), :] for lane in range(D // LANES)], axis=1)
        packed[half, pl.ds(part * 16, 16)] = values.reshape(16, BLOCK, D).astype(BF16)
        return carry

    lax.fori_loop(0, DEVICES // 16, step, 0)


class Place:
    def __init__(self):
        self.row = lax.axis_index("row")
        self.col = lax.axis_index("col")
        self.core = lax.rem(self.col, 2)
        self.other = (self.row, self.col + 1 - 2 * self.core)
        self.slots = (self.col // 2, self.row)
        self.me = self.row * 16 + self.col

    def along(self, half, index):
        return (self.row, index * 2 + self.core) if half == 0 else (index, self.col)

    def apart(self, step):
        jump = lax.rem(step * 45, DEVICES)
        x = lax.rem(lax.rem(self.row, 2) * 2 + self.col // 8 + (jump // 2) % 4, 4)
        y = lax.rem((self.col // 2) % 4 + (jump // 8) % 4, 4)
        z = lax.rem(self.row // 2 + jump // 32, 4)
        core = lax.rem(self.core + jump % 2, 2)
        row = z * 2 + x // 2
        col = (x % 2) * 8 + y * 2 + core
        return row, col


def remote(source, target, sems, index, device):
    return pltpu.make_async_remote_copy(
        src_ref=source, dst_ref=target, send_sem=sems.at[0, index], recv_sem=sems.at[1, index],
        device_id=device, device_id_type=MESH,
    )


def settle(some, sems, side, index):
    pltpu.make_async_copy(some, some, sems.at[side, index]).wait()


def swap_start(place, packed, arrived, sems, which, half):
    def send(step, carry):
        row, col = place.apart(step)
        source, target = packed.at[half, row * 16 + col], arrived.at[half, place.me]
        remote(source, target, sems, which * 2 + half, (row, col)).start()
        return carry

    lax.fori_loop(1, DEVICES, send, 0)
    arrived[half, place.me] = packed[half, place.me]


def swap_wait(some, sems, side, which, half):
    settle(some.at[half, pl.ds(0, DEVICES - 1)], sems, side, which * 2 + half)


def summed(pieces):
    acc = pieces[0].astype(F32)
    for piece in pieces[1:]:
        acc = acc + piece.astype(F32)
    return acc


class DeviceSum:
    def __init__(self, place, sums, total, away, sibling, in_a, part, in_b, sems):
        self.place, self.sums, self.total = place, sums, total
        self.away, self.sibling, self.in_a, self.part, self.in_b, self.sems = away, sibling, in_a, part, in_b, sems
        self.piece = part.shape[1]
        self.half = 8 * self.piece
        self.here = place.core * 2 * self.half

    def rows_of(self, core, half, q):
        start = pl.multiple_of((core * 2 * self.half + half * self.half + q * self.piece) * TALL, TALL)
        return self.sums[pl.ds(start, self.piece * TALL), :]

    def shout(self, source, target, index, half):
        def step(offset, carry):
            q = lax.rem(self.place.slots[half] + offset, 8)
            remote(source(q), target, self.sems, index, self.place.along(half, q)).start()
            return carry

        lax.fori_loop(1, 8, step, 0)

    def start(self):
        for half in range(2):
            def cast(q, carry):
                rows = self.rows_of(1 - self.place.core, half, q).astype(BF16)
                self.away[half, q] = rows.reshape(self.piece, TALL, D)
                return carry

            lax.fori_loop(0, 8, cast, 0)
            remote(self.away.at[half], self.sibling.at[half], self.sems, half, self.place.other).start()

    def round_a(self):
        for half in range(2):
            settle(self.away.at[half], self.sems, 0, half)
            settle(self.sibling.at[half], self.sems, 1, half)

            def add(q, carry):
                kept = self.rows_of(self.place.core, half, q).reshape(self.piece, TALL, D)
                self.away[half, q] = (kept + self.sibling[half, q].astype(F32)).astype(BF16)
                return carry

            lax.fori_loop(0, 8, add, 0)
            slot = self.place.slots[half]
            self.shout(lambda q: self.away.at[half, q], self.in_a.at[half, slot], 2 + half, half)
            self.in_a[half, slot] = self.away[half, slot]

    def round_b(self):
        for half in range(2):
            settle(self.away.at[half, pl.ds(0, 7)], self.sems, 0, 2 + half)
            settle(self.in_a.at[half, pl.ds(0, 7)], self.sems, 1, 2 + half)

            def add(block, carry):
                self.part[half, block] = summed([self.in_a[half, q, block] for q in range(8)]).astype(BF16)
                return carry

            lax.fori_loop(0, self.piece, add, 0)
            slot = self.place.slots[1 - half]
            self.shout(lambda q: self.part.at[half], self.in_b.at[half, slot], 4 + half, 1 - half)
            self.in_b[half, slot] = self.part[half]

    def round_c(self):
        for half in range(2):
            settle(self.in_b.at[half, pl.ds(0, 7)], self.sems, 0, 4 + half)
            settle(self.in_b.at[half, pl.ds(0, 7)], self.sems, 1, 4 + half)
            base = self.here + half * self.half + self.place.slots[half] * self.piece

            def add(block, carry):
                self.total[base + block] = summed([self.in_b[half, q, block] for q in range(8)]).astype(BF16)
                return carry

            lax.fori_loop(0, self.piece, add, 0)
            spot = self.total.at[pl.ds(base, self.piece)]
            self.shout(lambda q: spot, spot, 6 + half, half)

    def round_d(self):
        for half in range(2):
            seven = self.total.at[pl.ds(0, 7 * self.piece)]
            settle(seven, self.sems, 0, 6 + half)
            settle(seven, self.sems, 1, 6 + half)
            spot = self.total.at[pl.ds(self.here + half * self.half, self.half)]
            remote(spot, spot, self.sems, 8 + half, self.place.other).start()

    def finish(self):
        for half in range(2):
            spot = self.total.at[pl.ds(0, self.half)]
            settle(spot, self.sems, 0, 8 + half)
            settle(spot, self.sems, 1, 8 + half)


def whole_kernel(
    activations, cotangent, first_gain, joint, project, second_gain, expand, reduce,
    block_out, grad_in, total_mlp, total_rest, total_gain,
    packed_a, packed_b, act, cot, rows_a, rows_b,
    gain_a, gain_b, joint_t, project_t, expand_t, reduce_t,
    x_feat, scaled_first, triple, mixed, stats, grad_att, grad_mixed, grad_triple,
    sum_mlp, sum_rest, sum_first, sum_second,
    mlp_away, mlp_sibling, mlp_in_a, mlp_part, mlp_in_b,
    rest_away, rest_sibling, rest_in_a, rest_part, rest_in_b,
    gain_pair, gain_x, gain_y,
    swap_sems, mlp_sems, rest_sems, gain_sems,
):
    place = Place()
    barrier = pltpu.get_barrier_semaphore()

    def greet(step, carry):
        pl.semaphore_signal(barrier, inc=1, device_id=place.apart(step), device_id_type=MESH)
        return carry

    lax.fori_loop(1, DEVICES, greet, 0)
    pack(activations, packed_a)
    pl.semaphore_wait(barrier, DEVICES - 1)
    for half in range(2):
        swap_start(place, packed_a, act, swap_sems, 0, half)
    pack(cotangent, packed_b)
    for half in range(2):
        swap_start(place, packed_b, cot, swap_sems, 1, half)
    gain_a[...] = jnp.broadcast_to(first_gain[...].reshape(1, D), (TOKENS, D)).T
    gain_b[...] = jnp.broadcast_to(second_gain[...].reshape(1, D), (TOKENS, D)).T
    for natural, turned in ((joint, joint_t), (project, project_t), (expand, expand_t)):
        for start in range(0, natural.shape[1], D):
            turned[start : start + D, :] = natural[:, start : start + D].T
    for start in range(0, FF, D):
        reduce_t[:, start : start + D] = reduce[start : start + D, :].T
    for sums in (sum_mlp, sum_rest, sum_first, sum_second):
        sums[...] = jnp.zeros_like(sums)

    def by_halves(work):
        def step(half, carry):
            work(half)
            return carry

        lax.fori_loop(0, 2, step, 0)

    def groups_of(half, work):
        def step(group, carry):
            work(group)
            return carry

        lax.fori_loop(half * (GROUPS // 2), half * (GROUPS // 2) + GROUPS // 2, step, 0)

    def front(half):
        swap_wait(act, swap_sems, 1, 0, half)
        spread(rows_a, act, half)

        def work(group):
            project_group(group, rows_a, gain_a, joint_t, x_feat, scaled_first, triple)
            attend_group(group, triple, mixed, stats)

        groups_of(half, work)

    by_halves(front)
    for half in range(2):
        swap_wait(packed_a, swap_sems, 0, 0, half)
    sum_project = sum_rest.at[pl.ds(3 * D, D)]
    sum_joint = sum_rest.at[pl.ds(0, 3 * D)]
    sum_expand = sum_mlp.at[pl.ds(0, FF)]
    sum_reduce = sum_mlp.at[pl.ds(FF, FF)]

    def middle(half):
        swap_wait(cot, swap_sems, 1, 1, half)
        spread(rows_b, cot, half)

        def work(group):
            tail_group(
                group, x_feat, rows_b, mixed, project, project_t, gain_b, expand, expand_t, reduce, reduce_t,
                rows_a, grad_att, grad_mixed, sum_project, sum_expand, sum_reduce, sum_second,
            )

        groups_of(half, work)
        gather_rows(rows_a, packed_a, half)
        swap_start(place, packed_a, block_out, swap_sems, 2, half)

    by_halves(middle)
    for half in range(2):
        swap_wait(packed_b, swap_sems, 0, 1, half)
    mlp = DeviceSum(place, sum_mlp, total_mlp, mlp_away, mlp_sibling, mlp_in_a, mlp_part, mlp_in_b, mlp_sems)
    rest = DeviceSum(place, sum_rest, total_rest, rest_away, rest_sibling, rest_in_a, rest_part, rest_in_b, rest_sems)
    mlp.start()

    def back(half):
        def attention(group):
            for turn, work in ((1, mlp.round_a), (3, mlp.round_b), (5, mlp.round_c), (7, mlp.round_d)):
                pl.when(group == turn)(work)
            attend_back_group(group, scaled_first, triple, stats, grad_mixed, grad_triple, sum_joint)

        groups_of(half, attention)
        pl.when(half == 1)(rest.start)

        def head(group):
            pl.when(group == 7)(rest.round_a)
            head_back_group(group, x_feat, grad_att, triple, gain_a, joint, rows_b, sum_first)

        groups_of(half, head)
        gather_rows(rows_b, packed_b, half)
        swap_start(place, packed_b, grad_in, swap_sems, 3, half)

    by_halves(back)
    both = [jnp.sum(sums[...].T, axis=0, keepdims=True) for sums in (sum_first, sum_second)]
    gain_pair[0] = jnp.concatenate(both + [jnp.zeros((6, D), F32)], axis=0)
    gain_first = remote(gain_pair.at[0], gain_pair.at[1], gain_sems, 0, place.other)
    gain_first.start()

    def gain_round(values, slots, index, half):
        slot = place.slots[half]
        slots[slot] = values

        def step(offset, carry):
            q = lax.rem(slot + offset, 8)
            remote(slots.at[slot], slots.at[slot], gain_sems, index, place.along(half, q)).start()
            return carry

        lax.fori_loop(1, 8, step, 0)

    def gain_sum(slots, index):
        settle(slots.at[pl.ds(0, 7)], gain_sems, 0, index)
        settle(slots.at[pl.ds(0, 7)], gain_sems, 1, index)
        return summed([slots[q] for q in range(8)])

    rest.round_b()
    gain_first.wait()
    gain_round(gain_pair[0] + gain_pair[1], gain_x, 1, 0)
    rest.round_c()
    gain_round(gain_sum(gain_x, 1), gain_y, 2, 1)
    rest.round_d()
    total_gain[...] = gain_sum(gain_y, 2)
    mlp.finish()
    for packed, arrived, which in ((packed_a, block_out, 2), (packed_b, grad_in, 3)):
        for half in range(2):
            swap_wait(packed, swap_sems, 0, which, half)
            swap_wait(arrived, swap_sems, 1, which, half)
    rest.finish()


PARTS = 4


def finish_kernel(
    out_blocks, grad_blocks, expand, reduce, joint, project, gains,
    block_out, grad_in, g_joint, g_project, g_expand, g_reduce, g_first, g_second,
):
    factor = float(POSITIONS) ** -0.5
    few = GROUPS // 2
    for arrived, tile in ((out_blocks, block_out), (grad_blocks, grad_in)):
        for a in range(STRIDE // PARTS):
            early = [arrived[0, a * SPLIT + block].astype(F32) for block in range(SPLIT)]
            late = [arrived[1, a * SPLIT + block].astype(F32) for block in range(SPLIT)]
            for side in range(2):
                part = slice(side * few, side * few + few)
                pieces = [piece[part] for pair in zip(early, late) for piece in pair]
                tile[side, a] = jnp.concatenate(pieces, axis=0).astype(BF16)

    def natural(source):
        return source[...].astype(F32).reshape(D, D) * factor

    g_expand[...] = natural(expand).T
    g_reduce[...] = natural(reduce)
    g_joint[...] = natural(joint).T
    g_project[...] = natural(project)
    g_first[...] = gains[0] * factor
    g_second[...] = gains[1] * factor


def shards(
    activations, cotangent, first_gain, joint_weight, output_weight, second_gain, expand_weight, reduce_weight
):
    dma = pltpu.SemaphoreType.DMA
    blocks = (2, DEVICES, BLOCK, D)
    feat = (GROUPS, D, TOKENS)
    mlp, rest = 2 * FF, 4 * D

    def sum_scratch(rows):
        piece = rows // 32 // TALL
        spread_out = (2, 8, piece, TALL, D)
        return [
            pltpu.VMEM(spread_out, BF16), pltpu.VMEM(spread_out, BF16), pltpu.VMEM(spread_out, BF16),
            pltpu.VMEM((2, piece, TALL, D), BF16), pltpu.VMEM(spread_out, BF16),
        ]

    out_blocks, grad_blocks, total_mlp, total_rest, total_gain = pl.pallas_call(
        whole_kernel,
        in_specs=[WHOLE] * 8,
        out_specs=[WHOLE] * 5,
        out_shape=[
            shape(blocks), shape(blocks), shape((mlp // TALL, TALL, D)), shape((rest // TALL, TALL, D)),
            shape((8, D), F32),
        ],
        scratch_shapes=[
            pltpu.VMEM(blocks, BF16), pltpu.VMEM(blocks, BF16), pltpu.VMEM(blocks, BF16), pltpu.VMEM(blocks, BF16),
            pltpu.VMEM(ROWS, F32), pltpu.VMEM(ROWS, F32),
            pltpu.VMEM((D, TOKENS), F32), pltpu.VMEM((D, TOKENS), F32),
            pltpu.VMEM((3 * D, D), BF16), pltpu.VMEM((D, D), BF16), pltpu.VMEM((FF, D), BF16), pltpu.VMEM((D, FF), BF16),
            pltpu.VMEM(feat, BF16), pltpu.VMEM(feat, BF16), pltpu.VMEM((GROUPS, 3 * D, TOKENS), BF16),
            pltpu.VMEM(feat, BF16), pltpu.VMEM((GROUPS, 2 * HEADS, TOKENS), F32), pltpu.VMEM(feat, F32),
            pltpu.VMEM(feat, BF16), pltpu.VMEM((3 * D, TOKENS), BF16),
            pltpu.VMEM((mlp, D), F32), pltpu.VMEM((rest, D), F32), pltpu.VMEM((D, TOKENS), F32), pltpu.VMEM((D, TOKENS), F32),
            *sum_scratch(mlp), *sum_scratch(rest),
            pltpu.VMEM((2, 8, D), F32), pltpu.VMEM((8, 8, D), F32), pltpu.VMEM((8, 8, D), F32),
            dma((2, 8)), dma((2, 10)), dma((2, 10)), dma((2, 3)),
        ],
        cost_estimate=pl.CostEstimate(flops=12 * 10**10, bytes_accessed=10**8, transcendentals=0),
        compiler_params=pltpu.CompilerParams(
            collective_id=0, has_side_effects=True, vmem_limit_bytes=63 * 2**20
        ),
    )(
        activations, cotangent, first_gain, joint_weight, output_weight, second_gain, expand_weight, reduce_weight,
    )
    tile = (2, STRIDE, STRIDE, D)
    last = 3 * D // D - 1
    arrived = pl.BlockSpec((2, DEVICES // PARTS, BLOCK, D), lambda i: (0, i, 0, 0))
    placed = pl.BlockSpec((2, STRIDE // PARTS, STRIDE, D), lambda i: (0, i, 0, 0))

    def sums(index):
        return pl.BlockSpec((D // TALL, TALL, D), lambda i: (index(i), 0, 0))

    results = pl.pallas_call(
        finish_kernel,
        grid=(PARTS,),
        in_specs=[
            arrived, arrived, sums(lambda i: i), sums(lambda i: PARTS + i), sums(lambda i: jnp.minimum(i, last)),
            sums(lambda i: last + 1), pl.BlockSpec((8, D), lambda i: (0, 0)),
        ],
        out_specs=[
            placed, placed,
            pl.BlockSpec((D, D), lambda i: (0, jnp.minimum(i, last))), pl.BlockSpec((D, D), lambda i: (0, 0)),
            pl.BlockSpec((D, D), lambda i: (0, i)), pl.BlockSpec((D, D), lambda i: (i, 0)),
            pl.BlockSpec((D,), lambda i: (0,)), pl.BlockSpec((D,), lambda i: (0,)),
        ],
        out_shape=[
            shape(tile), shape(tile), shape((D, 3 * D), F32), shape((D, D), F32), shape((D, FF), F32),
            shape((FF, D), F32), shape((D,), F32), shape((D,), F32),
        ],
        compiler_params=pltpu.CompilerParams(vmem_limit_bytes=48 * 2**20),
    )(out_blocks, grad_blocks, total_mlp, total_mlp, total_rest, total_rest, total_gain)
    return tuple(result.reshape(activations.shape) for result in results[:2]) + tuple(results[2:])


def solution(mesh):
    tile = P("row", "col", None)
    return jax.shard_map(
        shards,
        mesh=mesh,
        in_specs=(tile, tile) + (P(),) * 6,
        out_specs=(tile, tile) + (P(),) * 6,
        check_vma=False,
    )
```

```python
import jax
import jax.numpy as jnp
from jax import lax
from jax.experimental import pallas as pl
from jax.experimental.pallas import tpu as pltpu
from jax.sharding import PartitionSpec as P

HEADS = 12
GRID = 16
GROUPS = 8
TOKENS = 256
D = 384
FF = 1536
WIDE = 32
CHUNK = 512

EPSILON = 1e-05
SQRT_HALF = 0.7071067811865476
INV_ROOT_TAU = 0.3989422804014327
LOG2E = 1.4426950408889634
SCORE_SCALE = WIDE ** (-0.5)
F32 = jnp.float32
BF16 = jnp.bfloat16


def dot_nn(a, b):
    return lax.dot_general(a, b, (((1,), (0,)), ((), ())), preferred_element_type=F32)


def dot_nt(a, b):
    return lax.dot_general(a, b, (((1,), (1,)), ((), ())), preferred_element_type=F32)


def dot_tn(a, b):
    return lax.dot_general(a, b, (((0,), (0,)), ((), ())), preferred_element_type=F32)


def mean0(values):
    return jnp.sum(values, axis=0, keepdims=True) * (1.0 / D)


def gelu_parts(pre):
    gauss = jnp.exp2(pre * pre * (-0.5 * LOG2E))
    t = 1.0 / (1.0 + (0.3275911 * SQRT_HALF) * jnp.abs(pre))
    poly = t * (0.127414796 + t * (-0.142248368 + t * (0.7107068705 + t * (-0.7265760135 + t * 0.5307027145))))
    tail = poly * gauss
    cdf = jnp.where(pre >= 0.0, 1.0 - tail, tail)
    return pre * cdf, cdf + pre * gauss * INV_ROOT_TAU


def members(group):
    start = (group // (GROUPS // 2)) * (GROUPS // 2 * TOKENS) + lax.rem(group, GROUPS // 2)
    return pl.ds(start, TOKENS, stride=GROUPS // 2)


def take_group(rows, group):
    return jnp.concatenate([rows[lane, members(group), :].T for lane in range(D // 128)], axis=0)


def put_group(rows, group, values):
    for lane in range(D // 128):
        rows[lane, members(group), :] = values[lane * 128 : lane * 128 + 128].T


def project_group(group, x_rows, gain, joint_t, x_feat, scaled_first, triple):
    values = take_group(x_rows, group)
    x_feat[group] = values.astype(BF16)
    center = values - mean0(values)
    inv = lax.rsqrt(mean0(center * center) + EPSILON)
    scaled = (center * inv * gain[...]).astype(BF16)
    scaled_first[group] = scaled
    triple[group] = dot_nn(joint_t[...], scaled).astype(BF16)


def head_scores(triple, group, head):
    at = head * WIDE
    query = triple[group, at : at + WIDE]
    key = triple[group, D + at : D + at + WIDE]
    return dot_tn(key, query) * (SCORE_SCALE * LOG2E)


def attend_group(group, triple, mixed, stats):
    ahead = head_scores(triple, group, 0)
    for head in range(HEADS):
        at = head * WIDE
        scores = ahead
        if head + 1 < HEADS:
            ahead = head_scores(triple, group, head + 1)
        value = triple[group, 2 * D + at : 2 * D + at + WIDE]
        top = jnp.max(scores, axis=0, keepdims=True)
        raised = jnp.exp2(scores - top)
        share = 1.0 / jnp.sum(raised, axis=0, keepdims=True)
        stats[group, 2 * head : 2 * head + 1] = top
        stats[group, 2 * head + 1 : 2 * head + 2] = share
        weights = (raised * share).astype(BF16)
        mixed[group, at : at + WIDE] = dot_nn(value, weights).astype(BF16)


def tail_group(
    group, x_feat, cot_rows, mixed, project, project_t, gain, expand, expand_t, reduce, reduce_t,
    result_rows, grad_att, grad_mixed, sum_project, sum_expand, sum_reduce, sum_gain,
):
    blend = mixed[group]
    cot32 = take_group(cot_rows, group)
    cot = cot32.astype(BF16)
    attended = x_feat[group].astype(F32) + dot_nn(project_t[...], blend)
    center = attended - mean0(attended)
    inv = lax.rsqrt(mean0(center * center) + EPSILON)
    normed = center * inv
    scaled = (normed * gain[...]).astype(BF16)
    result = attended
    grad_scaled = None
    def chunk_pair(start):
        part = slice(start, start + CHUNK)
        return dot_nn(expand_t[part, :], scaled), dot_nn(reduce[part, :], cot)

    ahead = chunk_pair(0)
    for start in range(0, FF, CHUNK):
        part = slice(start, start + CHUNK)
        pre, grad_hidden = ahead
        if start + CHUNK < FF:
            ahead = chunk_pair(start + CHUNK)
        value, slope = gelu_parts(pre)
        hidden = value.astype(BF16)
        grad_pre = (grad_hidden.astype(BF16).astype(F32) * slope).astype(BF16)
        result = result + dot_nn(reduce_t[:, part], hidden)
        back = dot_nn(expand[:, part], grad_pre)
        grad_scaled = back if grad_scaled is None else grad_scaled + back
        sum_reduce[part, :] += dot_nt(hidden, cot)
        sum_expand[part, :] += dot_nt(grad_pre, scaled)
    put_group(result_rows, group, result)
    sum_gain[...] += grad_scaled * normed
    lifted = grad_scaled * gain[...]
    grad = cot32 + inv * (lifted - mean0(lifted) - normed * mean0(lifted * normed))
    grad_att[group] = grad
    grad_b = grad.astype(BF16)
    sum_project[...] += dot_nt(blend, grad_b)
    grad_mixed[group] = dot_nn(project[...], grad_b).astype(BF16)


def head_pair(triple, grad_mixed, group, head):
    at = head * WIDE
    value = triple[group, 2 * D + at : 2 * D + at + WIDE]
    return head_scores(triple, group, head), dot_tn(value, grad_mixed[group, at : at + WIDE])


def attend_back_group(group, scaled_first, triple, stats, grad_mixed, grad_triple, sum_joint):
    def spill(head, grad_scores, weights):
        at = head * WIDE
        query = triple[group, at : at + WIDE]
        key = triple[group, D + at : D + at + WIDE]
        grad_out = grad_mixed[group, at : at + WIDE]
        grad_triple[at : at + WIDE] = dot_nn(key, grad_scores).astype(BF16)
        grad_triple[D + at : D + at + WIDE] = dot_nt(query, grad_scores).astype(BF16)
        grad_triple[2 * D + at : 2 * D + at + WIDE] = dot_nt(grad_out, weights).astype(BF16)

    ahead = head_pair(triple, grad_mixed, group, 0)
    for head in range(HEADS):
        scores, grad_weights = ahead
        if head + 1 < HEADS:
            ahead = head_pair(triple, grad_mixed, group, head + 1)
        top = stats[group, 2 * head : 2 * head + 1]
        share = stats[group, 2 * head + 1 : 2 * head + 2]
        weights = jnp.exp2(scores - top) * share
        inner = jnp.sum(weights * grad_weights, axis=0, keepdims=True)
        grad_scores = (weights * (grad_weights - inner) * SCORE_SCALE).astype(BF16)
        spill(head, grad_scores, weights.astype(BF16))
    triple[group] = grad_triple[...]
    sum_joint[...] += dot_nt(grad_triple[...], scaled_first[group])


def head_back_group(group, x_feat, grad_att, grad_triple, gain, joint, grad_rows, sum_gain):
    values = x_feat[group].astype(F32)
    center = values - mean0(values)
    inv = lax.rsqrt(mean0(center * center) + EPSILON)
    normed = center * inv
    grad_scaled = dot_nn(joint[...], grad_triple[group])
    sum_gain[...] += grad_scaled * normed
    lifted = grad_scaled * gain[...]
    grad = grad_att[group] + inv * (lifted - mean0(lifted) - normed * mean0(lifted * normed))
    put_group(grad_rows, group, grad)


AXES = ("row", "col")
MESH = pl.DeviceIdType.MESH
POSITIONS = 262144
DEVICES = 128
LANES = 128
BLOCK = 8
TALL = 16
STRIDE = 32
SPLIT = STRIDE // GROUPS
ROWS = (D // LANES, GROUPS * TOKENS, LANES)
WHOLE = pl.BlockSpec(memory_space=pltpu.VMEM)


def shape(dims, dtype=BF16):
    return jax.ShapeDtypeStruct(dims, dtype)


def pack(tile, packed):
    few = GROUPS // 2

    def step(a, carry):
        near = tile[a].astype(F32)
        far = tile[STRIDE + a].astype(F32)
        for block in range(SPLIT):
            for half in range(2):
                at = block * GROUPS + half * few
                both = jnp.concatenate([near[at : at + few], far[at : at + few]], axis=0)
                packed[half, a * SPLIT + block] = both.astype(BF16)
        return carry

    lax.fori_loop(0, STRIDE, step, 0, unroll=2)


def spread(rows, arrived, half):
    def step(part, carry):
        values = arrived[half, pl.ds(part * 16, 16)].astype(F32).reshape(16 * BLOCK, D)
        at = pl.multiple_of((half * DEVICES + part * 16) * BLOCK, 16 * BLOCK)
        for lane in range(D // LANES):
            rows[lane, pl.ds(at, 16 * BLOCK), :] = values[:, lane * LANES : lane * LANES + LANES]
        return carry

    lax.fori_loop(0, DEVICES // 16, step, 0)


def gather_rows(rows, packed, half):
    def step(part, carry):
        at = pl.multiple_of((half * DEVICES + part * 16) * BLOCK, 16 * BLOCK)
        values = jnp.concatenate([rows[lane, pl.ds(at, 16 * BLOCK), :] for lane in range(D // LANES)], axis=1)
        packed[half, pl.ds(part * 16, 16)] = values.reshape(16, BLOCK, D).astype(BF16)
        return carry

    lax.fori_loop(0, DEVICES // 16, step, 0)


class Place:
    def __init__(self):
        self.row = lax.axis_index("row")
        self.col = lax.axis_index("col")
        self.core = lax.rem(self.col, 2)
        self.other = (self.row, self.col + 1 - 2 * self.core)
        self.slots = (self.col // 2, self.row)
        self.me = self.row * 16 + self.col

    def along(self, half, index):
        return (self.row, index * 2 + self.core) if half == 0 else (index, self.col)

    def visit(self, work):
        z, y = lax.div(self.row, 2), lax.rem(lax.div(self.col, 2), 4)
        x = lax.rem(self.row, 2) * 2 + lax.div(self.col, 8)
        near = []
        for jump in range(8):
            to_x, to_core = lax.rem(x + jump // 2, 4), lax.rem(self.core + jump % 2, 2)
            near.append((lax.div(to_x, 2), lax.rem(to_x, 2) * 8 + to_core))

        def corner(z, y, first):
            for row, col in near[first:]:
                work(z * 2 + row, y * 2 + col)

        def step(turn, carry):
            jump = lax.rem(turn * 5, 16)
            corner(lax.rem(z + lax.div(jump, 4), 4), lax.rem(y + lax.rem(jump, 4), 4), 0)
            return carry

        corner(z, y, 1)
        lax.fori_loop(1, 16, step, 0)


def remote(source, target, sems, index, device):
    return pltpu.make_async_remote_copy(
        src_ref=source, dst_ref=target, send_sem=sems.at[0, index], recv_sem=sems.at[1, index],
        device_id=device, device_id_type=MESH,
    )


def settle(some, sems, side, index):
    pltpu.make_async_copy(some, some, sems.at[side, index]).wait()


def swap_start(place, packed, arrived, sems, which, half):
    def send(row, col):
        source, target = packed.at[half, row * 16 + col], arrived.at[half, place.me]
        remote(source, target, sems, which * 2 + half, (row, col)).start()

    place.visit(send)
    arrived[half, place.me] = packed[half, place.me]


def swap_wait(some, sems, side, which, half):
    settle(some.at[half, pl.ds(0, DEVICES - 1)], sems, side, which * 2 + half)


def summed(pieces):
    acc = pieces[0].astype(F32)
    for piece in pieces[1:]:
        acc = acc + piece.astype(F32)
    return acc


class DeviceSum:
    def __init__(self, place, sums, total, away, sibling, in_a, part, in_b, sems):
        self.place, self.sums, self.total = place, sums, total
        self.away, self.sibling, self.in_a, self.part, self.in_b, self.sems = away, sibling, in_a, part, in_b, sems
        self.piece = part.shape[1]
        self.half = 8 * self.piece
        self.here = place.core * 2 * self.half

    def rows_of(self, core, half, q):
        start = pl.multiple_of((core * 2 * self.half + half * self.half + q * self.piece) * TALL, TALL)
        return self.sums[pl.ds(start, self.piece * TALL), :]

    def shout(self, source, target, index, half):
        def step(offset, carry):
            q = lax.rem(self.place.slots[half] + offset, 8)
            remote(source(q), target, self.sems, index, self.place.along(half, q)).start()
            return carry

        lax.fori_loop(1, 8, step, 0)

    def start(self):
        for half in range(2):
            def cast(q, carry):
                rows = self.rows_of(1 - self.place.core, half, q).astype(BF16)
                self.away[half, q] = rows.reshape(self.piece, TALL, D)
                return carry

            lax.fori_loop(0, 8, cast, 0)
            remote(self.away.at[half], self.sibling.at[half], self.sems, half, self.place.other).start()

    def round_a(self):
        for half in range(2):
            settle(self.away.at[half], self.sems, 0, half)
            settle(self.sibling.at[half], self.sems, 1, half)

            def add(q, carry):
                kept = self.rows_of(self.place.core, half, q).reshape(self.piece, TALL, D)
                self.away[half, q] = (kept + self.sibling[half, q].astype(F32)).astype(BF16)
                return carry

            lax.fori_loop(0, 8, add, 0)
            slot = self.place.slots[half]
            self.shout(lambda q: self.away.at[half, q], self.in_a.at[half, slot], 2 + half, half)
            self.in_a[half, slot] = self.away[half, slot]

    def round_b(self):
        for half in range(2):
            settle(self.away.at[half, pl.ds(0, 7)], self.sems, 0, 2 + half)
            settle(self.in_a.at[half, pl.ds(0, 7)], self.sems, 1, 2 + half)

            def add(block, carry):
                self.part[half, block] = summed([self.in_a[half, q, block] for q in range(8)]).astype(BF16)
                return carry

            lax.fori_loop(0, self.piece, add, 0)
            slot = self.place.slots[1 - half]
            self.shout(lambda q: self.part.at[half], self.in_b.at[half, slot], 4 + half, 1 - half)
            self.in_b[half, slot] = self.part[half]

    def round_c(self):
        for half in range(2):
            settle(self.in_b.at[half, pl.ds(0, 7)], self.sems, 0, 4 + half)
            settle(self.in_b.at[half, pl.ds(0, 7)], self.sems, 1, 4 + half)
            base = self.here + half * self.half + self.place.slots[half] * self.piece

            def add(block, carry):
                self.total[base + block] = summed([self.in_b[half, q, block] for q in range(8)]).astype(BF16)
                return carry

            lax.fori_loop(0, self.piece, add, 0)
            spot = self.total.at[pl.ds(base, self.piece)]
            self.shout(lambda q: spot, spot, 6 + half, half)

    def round_d(self):
        for half in range(2):
            seven = self.total.at[pl.ds(0, 7 * self.piece)]
            settle(seven, self.sems, 0, 6 + half)
            settle(seven, self.sems, 1, 6 + half)
            spot = self.total.at[pl.ds(self.here + half * self.half, self.half)]
            remote(spot, spot, self.sems, 8 + half, self.place.other).start()

    def finish(self):
        for half in range(2):
            spot = self.total.at[pl.ds(0, self.half)]
            settle(spot, self.sems, 0, 8 + half)
            settle(spot, self.sems, 1, 8 + half)


def whole_kernel(
    activations, cotangent, first_gain, joint, project, second_gain, expand, reduce,
    block_out, grad_in, total_mlp, total_rest, total_gain,
    packed_a, packed_b, act, cot, rows_a, rows_b,
    gain_a, gain_b, joint_t, project_t, expand_t, reduce_t,
    x_feat, scaled_first, triple, mixed, stats, grad_att, grad_mixed, grad_triple,
    sum_mlp, sum_rest, sum_first, sum_second,
    mlp_away, mlp_sibling, mlp_in_a, mlp_part, mlp_in_b,
    rest_away, rest_sibling, rest_in_a, rest_part, rest_in_b,
    gain_pair, gain_x, gain_y,
    swap_sems, mlp_sems, rest_sems, gain_sems,
):
    place = Place()
    barrier = pltpu.get_barrier_semaphore()

    def greet(row, col):
        pl.semaphore_signal(barrier, inc=1, device_id=(row, col), device_id_type=MESH)

    place.visit(greet)
    pack(activations, packed_a)
    pl.semaphore_wait(barrier, DEVICES - 1)
    for half in range(2):
        swap_start(place, packed_a, act, swap_sems, 0, half)
    pack(cotangent, packed_b)
    for half in range(2):
        swap_start(place, packed_b, cot, swap_sems, 1, half)
    gain_a[...] = jnp.broadcast_to(first_gain[...].reshape(1, D), (TOKENS, D)).T
    gain_b[...] = jnp.broadcast_to(second_gain[...].reshape(1, D), (TOKENS, D)).T
    for natural, turned in ((joint, joint_t), (project, project_t), (expand, expand_t)):
        for start in range(0, natural.shape[1], D):
            turned[start : start + D, :] = natural[:, start : start + D].T
    for start in range(0, FF, D):
        reduce_t[:, start : start + D] = reduce[start : start + D, :].T
    for sums in (sum_mlp, sum_rest, sum_first, sum_second):
        sums[...] = jnp.zeros_like(sums)

    def by_halves(work):
        def step(half, carry):
            work(half)
            return carry

        lax.fori_loop(0, 2, step, 0)

    def groups_of(half, work):
        def step(group, carry):
            work(group)
            return carry

        lax.fori_loop(half * (GROUPS // 2), half * (GROUPS // 2) + GROUPS // 2, step, 0)

    def front(half):
        swap_wait(act, swap_sems, 1, 0, half)
        spread(rows_a, act, half)

        def work(group):
            project_group(group, rows_a, gain_a, joint_t, x_feat, scaled_first, triple)
            attend_group(group, triple, mixed, stats)

        groups_of(half, work)

    by_halves(front)
    for half in range(2):
        swap_wait(packed_a, swap_sems, 0, 0, half)
    sum_project = sum_rest.at[pl.ds(3 * D, D)]
    sum_joint = sum_rest.at[pl.ds(0, 3 * D)]
    sum_expand = sum_mlp.at[pl.ds(0, FF)]
    sum_reduce = sum_mlp.at[pl.ds(FF, FF)]

    mlp = DeviceSum(place, sum_mlp, total_mlp, mlp_away, mlp_sibling, mlp_in_a, mlp_part, mlp_in_b, mlp_sems)
    rest = DeviceSum(place, sum_rest, total_rest, rest_away, rest_sibling, rest_in_a, rest_part, rest_in_b, rest_sems)

    def middle(half):
        swap_wait(cot, swap_sems, 1, 1, half)
        spread(rows_b, cot, half)

        def work(group):
            tail_group(
                group, x_feat, rows_b, mixed, project, project_t, gain_b, expand, expand_t, reduce, reduce_t,
                rows_a, grad_att, grad_mixed, sum_project, sum_expand, sum_reduce, sum_second,
            )

        groups_of(half, work)
        pl.when(half == 1)(mlp.start)
        gather_rows(rows_a, packed_a, half)
        swap_start(place, packed_a, block_out, swap_sems, 2, half)

    by_halves(middle)
    for half in range(2):
        swap_wait(packed_b, swap_sems, 0, 1, half)

    def back(half):
        def attention(group):
            for turn, work in ((2, mlp.round_a), (4, mlp.round_b), (6, mlp.round_c)):
                pl.when(group == turn)(work)
            attend_back_group(group, scaled_first, triple, stats, grad_mixed, grad_triple, sum_joint)

        groups_of(half, attention)
        pl.when(half == 1)(rest.start)

        def head(group):
            pl.when(group == 5)(mlp.round_d)
            pl.when(group == 6)(rest.round_a)
            head_back_group(group, x_feat, grad_att, triple, gain_a, joint, rows_b, sum_first)

        groups_of(half, head)
        gather_rows(rows_b, packed_b, half)
        pl.when(half == 1)(rest.round_b)
        swap_start(place, packed_b, grad_in, swap_sems, 3, half)

    by_halves(back)
    both = [jnp.sum(sums[...].T, axis=0, keepdims=True) for sums in (sum_first, sum_second)]
    gain_pair[0] = jnp.concatenate(both + [jnp.zeros((6, D), F32)], axis=0)
    gain_first = remote(gain_pair.at[0], gain_pair.at[1], gain_sems, 0, place.other)
    gain_first.start()

    def gain_round(values, slots, index, half):
        slot = place.slots[half]
        slots[slot] = values

        def step(offset, carry):
            q = lax.rem(slot + offset, 8)
            remote(slots.at[slot], slots.at[slot], gain_sems, index, place.along(half, q)).start()
            return carry

        lax.fori_loop(1, 8, step, 0)

    def gain_sum(slots, index):
        settle(slots.at[pl.ds(0, 7)], gain_sems, 0, index)
        settle(slots.at[pl.ds(0, 7)], gain_sems, 1, index)
        return summed([slots[q] for q in range(8)])

    gain_first.wait()
    gain_round(gain_pair[0] + gain_pair[1], gain_x, 1, 0)
    rest.round_c()
    gain_round(gain_sum(gain_x, 1), gain_y, 2, 1)
    rest.round_d()
    total_gain[...] = gain_sum(gain_y, 2)
    mlp.finish()
    for packed, arrived, which in ((packed_a, block_out, 2), (packed_b, grad_in, 3)):
        for half in range(2):
            swap_wait(packed, swap_sems, 0, which, half)
            swap_wait(arrived, swap_sems, 1, which, half)
    rest.finish()


PARTS = 4


def finish_kernel(
    out_blocks, grad_blocks, expand, reduce, joint, project, gains,
    block_out, grad_in, g_joint, g_project, g_expand, g_reduce, g_first, g_second,
):
    factor = float(POSITIONS) ** -0.5
    few = GROUPS // 2
    for arrived, tile in ((out_blocks, block_out), (grad_blocks, grad_in)):
        for a in range(STRIDE // PARTS):
            early = [arrived[0, a * SPLIT + block].astype(F32) for block in range(SPLIT)]
            late = [arrived[1, a * SPLIT + block].astype(F32) for block in range(SPLIT)]
            for side in range(2):
                part = slice(side * few, side * few + few)
                pieces = [piece[part] for pair in zip(early, late) for piece in pair]
                tile[side, a] = jnp.concatenate(pieces, axis=0).astype(BF16)

    def natural(source):
        return source[...].astype(F32).reshape(D, D) * factor

    g_expand[...] = natural(expand).T
    g_reduce[...] = natural(reduce)
    g_joint[...] = natural(joint).T
    g_project[...] = natural(project)
    g_first[...] = gains[0] * factor
    g_second[...] = gains[1] * factor


def shards(
    activations, cotangent, first_gain, joint_weight, output_weight, second_gain, expand_weight, reduce_weight
):
    dma = pltpu.SemaphoreType.DMA
    blocks = (2, DEVICES, BLOCK, D)
    feat = (GROUPS, D, TOKENS)
    mlp, rest = 2 * FF, 4 * D

    def sum_scratch(rows):
        piece = rows // 32 // TALL
        spread_out = (2, 8, piece, TALL, D)
        return [
            pltpu.VMEM(spread_out, BF16), pltpu.VMEM(spread_out, BF16), pltpu.VMEM(spread_out, BF16),
            pltpu.VMEM((2, piece, TALL, D), BF16), pltpu.VMEM(spread_out, BF16),
        ]

    out_blocks, grad_blocks, total_mlp, total_rest, total_gain = pl.pallas_call(
        whole_kernel,
        in_specs=[WHOLE] * 8,
        out_specs=[WHOLE] * 5,
        out_shape=[
            shape(blocks), shape(blocks), shape((mlp // TALL, TALL, D)), shape((rest // TALL, TALL, D)),
            shape((8, D), F32),
        ],
        scratch_shapes=[
            pltpu.VMEM(blocks, BF16), pltpu.VMEM(blocks, BF16), pltpu.VMEM(blocks, BF16), pltpu.VMEM(blocks, BF16),
            pltpu.VMEM(ROWS, F32), pltpu.VMEM(ROWS, F32),
            pltpu.VMEM((D, TOKENS), F32), pltpu.VMEM((D, TOKENS), F32),
            pltpu.VMEM((3 * D, D), BF16), pltpu.VMEM((D, D), BF16), pltpu.VMEM((FF, D), BF16), pltpu.VMEM((D, FF), BF16),
            pltpu.VMEM(feat, BF16), pltpu.VMEM(feat, BF16), pltpu.VMEM((GROUPS, 3 * D, TOKENS), BF16),
            pltpu.VMEM(feat, BF16), pltpu.VMEM((GROUPS, 2 * HEADS, TOKENS), F32), pltpu.VMEM(feat, F32),
            pltpu.VMEM(feat, BF16), pltpu.VMEM((3 * D, TOKENS), BF16),
            pltpu.VMEM((mlp, D), F32), pltpu.VMEM((rest, D), F32), pltpu.VMEM((D, TOKENS), F32), pltpu.VMEM((D, TOKENS), F32),
            *sum_scratch(mlp), *sum_scratch(rest),
            pltpu.VMEM((2, 8, D), F32), pltpu.VMEM((8, 8, D), F32), pltpu.VMEM((8, 8, D), F32),
            dma((2, 8)), dma((2, 10)), dma((2, 10)), dma((2, 3)),
        ],
        cost_estimate=pl.CostEstimate(flops=12 * 10**10, bytes_accessed=10**8, transcendentals=0),
        compiler_params=pltpu.CompilerParams(
            collective_id=0, has_side_effects=True, vmem_limit_bytes=63 * 2**20
        ),
    )(
        activations, cotangent, first_gain, joint_weight, output_weight, second_gain, expand_weight, reduce_weight,
    )
    tile = (2, STRIDE, STRIDE, D)
    last = 3 * D // D - 1
    arrived = pl.BlockSpec((2, DEVICES // PARTS, BLOCK, D), lambda i: (0, i, 0, 0))
    placed = pl.BlockSpec((2, STRIDE // PARTS, STRIDE, D), lambda i: (0, i, 0, 0))

    def sums(index):
        return pl.BlockSpec((D // TALL, TALL, D), lambda i: (index(i), 0, 0))

    results = pl.pallas_call(
        finish_kernel,
        grid=(PARTS,),
        in_specs=[
            arrived, arrived, sums(lambda i: i), sums(lambda i: PARTS + i), sums(lambda i: jnp.minimum(i, last)),
            sums(lambda i: last + 1), pl.BlockSpec((8, D), lambda i: (0, 0)),
        ],
        out_specs=[
            placed, placed,
            pl.BlockSpec((D, D), lambda i: (0, jnp.minimum(i, last))), pl.BlockSpec((D, D), lambda i: (0, 0)),
            pl.BlockSpec((D, D), lambda i: (0, i)), pl.BlockSpec((D, D), lambda i: (i, 0)),
            pl.BlockSpec((D,), lambda i: (0,)), pl.BlockSpec((D,), lambda i: (0,)),
        ],
        out_shape=[
            shape(tile), shape(tile), shape((D, 3 * D), F32), shape((D, D), F32), shape((D, FF), F32),
            shape((FF, D), F32), shape((D,), F32), shape((D,), F32),
        ],
        compiler_params=pltpu.CompilerParams(vmem_limit_bytes=48 * 2**20),
    )(out_blocks, grad_blocks, total_mlp, total_mlp, total_rest, total_rest, total_gain)
    return tuple(result.reshape(activations.shape) for result in results[:2]) + tuple(results[2:])


def solution(mesh):
    tile = P("row", "col", None)
    return jax.shard_map(
        shards,
        mesh=mesh,
        in_specs=(tile, tile) + (P(),) * 6,
        out_specs=(tile, tile) + (P(),) * 6,
        check_vma=False,
    )
```

```python
import jax
import jax.numpy as jnp
from jax import lax
from jax.experimental import pallas as pl
from jax.experimental.pallas import tpu as pltpu
from jax.sharding import PartitionSpec as P

HEADS = 12
GRID = 16
GROUPS = 8
TOKENS = 256
D = 384
FF = 1536
WIDE = 32
CHUNK = 512

EPSILON = 1e-05
SQRT_HALF = 0.7071067811865476
INV_ROOT_TAU = 0.3989422804014327
LOG2E = 1.4426950408889634
SCORE_SCALE = WIDE ** (-0.5)
F32 = jnp.float32
BF16 = jnp.bfloat16


def dot_nn(a, b):
    return lax.dot_general(a, b, (((1,), (0,)), ((), ())), preferred_element_type=F32)


def dot_nt(a, b):
    return lax.dot_general(a, b, (((1,), (1,)), ((), ())), preferred_element_type=F32)


def dot_tn(a, b):
    return lax.dot_general(a, b, (((0,), (0,)), ((), ())), preferred_element_type=F32)


def mean0(values):
    return jnp.sum(values, axis=0, keepdims=True) * (1.0 / D)


def gelu_parts(pre):
    gauss = jnp.exp2(pre * pre * (-0.5 * LOG2E))
    t = 1.0 / (1.0 + (0.3275911 * SQRT_HALF) * jnp.abs(pre))
    poly = t * (0.127414796 + t * (-0.142248368 + t * (0.7107068705 + t * (-0.7265760135 + t * 0.5307027145))))
    tail = poly * gauss
    cdf = jnp.where(pre >= 0.0, 1.0 - tail, tail)
    return pre * cdf, cdf + pre * gauss * INV_ROOT_TAU


def members(group):
    start = (group // (GROUPS // 2)) * (GROUPS // 2 * TOKENS) + lax.rem(group, GROUPS // 2)
    return pl.ds(start, TOKENS, stride=GROUPS // 2)


def take_group(rows, group):
    return jnp.concatenate([rows[lane, members(group), :].T for lane in range(D // 128)], axis=0)


def put_group(rows, group, values):
    for lane in range(D // 128):
        rows[lane, members(group), :] = values[lane * 128 : lane * 128 + 128].T


def project_group(group, x_rows, gain, joint_t, x_feat, scaled_first, triple):
    values = take_group(x_rows, group)
    x_feat[group] = values.astype(BF16)
    center = values - mean0(values)
    inv = lax.rsqrt(mean0(center * center) + EPSILON)
    scaled = (center * inv * gain[...]).astype(BF16)
    scaled_first[group] = scaled
    triple[group] = dot_nn(joint_t[...], scaled).astype(BF16)


def head_scores(triple, group, head):
    at = head * WIDE
    query = triple[group, at : at + WIDE]
    key = triple[group, D + at : D + at + WIDE]
    return dot_tn(key, query) * (SCORE_SCALE * LOG2E)


def attend_group(group, triple, mixed, stats):
    ahead = head_scores(triple, group, 0)
    for head in range(HEADS):
        at = head * WIDE
        scores = ahead
        if head + 1 < HEADS:
            ahead = head_scores(triple, group, head + 1)
        value = triple[group, 2 * D + at : 2 * D + at + WIDE]
        top = jnp.max(scores, axis=0, keepdims=True)
        raised = jnp.exp2(scores - top)
        share = 1.0 / jnp.sum(raised, axis=0, keepdims=True)
        stats[group, 2 * head : 2 * head + 1] = top
        stats[group, 2 * head + 1 : 2 * head + 2] = share
        weights = (raised * share).astype(BF16)
        mixed[group, at : at + WIDE] = dot_nn(value, weights).astype(BF16)


def tail_group(
    group, x_feat, cot_rows, mixed, project, project_t, gain, expand, expand_t, reduce, reduce_t,
    result_rows, grad_att, grad_mixed, sum_project, sum_expand, sum_reduce, sum_gain,
):
    blend = mixed[group]
    cot32 = take_group(cot_rows, group)
    cot = cot32.astype(BF16)
    attended = x_feat[group].astype(F32) + dot_nn(project_t[...], blend)
    center = attended - mean0(attended)
    inv = lax.rsqrt(mean0(center * center) + EPSILON)
    normed = center * inv
    scaled = (normed * gain[...]).astype(BF16)
    result = attended
    grad_scaled = None
    def chunk_pair(start):
        part = slice(start, start + CHUNK)
        return dot_nn(expand_t[part, :], scaled), dot_nn(reduce[part, :], cot)

    ahead = chunk_pair(0)
    for start in range(0, FF, CHUNK):
        part = slice(start, start + CHUNK)
        pre, grad_hidden = ahead
        if start + CHUNK < FF:
            ahead = chunk_pair(start + CHUNK)
        value, slope = gelu_parts(pre)
        hidden = value.astype(BF16)
        grad_pre = (grad_hidden.astype(BF16).astype(F32) * slope).astype(BF16)
        result = result + dot_nn(reduce_t[:, part], hidden)
        back = dot_nn(expand[:, part], grad_pre)
        grad_scaled = back if grad_scaled is None else grad_scaled + back
        sum_reduce[part, :] += dot_nt(hidden, cot)
        sum_expand[part, :] += dot_nt(grad_pre, scaled)
    put_group(result_rows, group, result)
    sum_gain[...] += grad_scaled * normed
    lifted = grad_scaled * gain[...]
    grad = cot32 + inv * (lifted - mean0(lifted) - normed * mean0(lifted * normed))
    grad_att[group] = grad
    grad_b = grad.astype(BF16)
    sum_project[...] += dot_nt(blend, grad_b)
    grad_mixed[group] = dot_nn(project[...], grad_b).astype(BF16)


def head_pair(triple, grad_mixed, group, head):
    at = head * WIDE
    value = triple[group, 2 * D + at : 2 * D + at + WIDE]
    return head_scores(triple, group, head), dot_tn(value, grad_mixed[group, at : at + WIDE])


def attend_back_group(group, scaled_first, triple, stats, grad_mixed, grad_triple, sum_joint):
    def spill(head, grad_scores, weights):
        at = head * WIDE
        query = triple[group, at : at + WIDE]
        key = triple[group, D + at : D + at + WIDE]
        grad_out = grad_mixed[group, at : at + WIDE]
        grad_triple[at : at + WIDE] = dot_nn(key, grad_scores).astype(BF16)
        grad_triple[D + at : D + at + WIDE] = dot_nt(query, grad_scores).astype(BF16)
        grad_triple[2 * D + at : 2 * D + at + WIDE] = dot_nt(grad_out, weights).astype(BF16)

    ahead = head_pair(triple, grad_mixed, group, 0)
    for head in range(HEADS):
        scores, grad_weights = ahead
        if head + 1 < HEADS:
            ahead = head_pair(triple, grad_mixed, group, head + 1)
        top = stats[group, 2 * head : 2 * head + 1]
        share = stats[group, 2 * head + 1 : 2 * head + 2]
        weights = jnp.exp2(scores - top) * share
        inner = jnp.sum(weights * grad_weights, axis=0, keepdims=True)
        grad_scores = (weights * (grad_weights - inner) * SCORE_SCALE).astype(BF16)
        spill(head, grad_scores, weights.astype(BF16))
    triple[group] = grad_triple[...]
    sum_joint[...] += dot_nt(grad_triple[...], scaled_first[group])


def head_back_group(group, x_feat, grad_att, grad_triple, gain, joint, grad_rows, sum_gain):
    values = x_feat[group].astype(F32)
    center = values - mean0(values)
    inv = lax.rsqrt(mean0(center * center) + EPSILON)
    normed = center * inv
    grad_scaled = dot_nn(joint[...], grad_triple[group])
    sum_gain[...] += grad_scaled * normed
    lifted = grad_scaled * gain[...]
    grad = grad_att[group] + inv * (lifted - mean0(lifted) - normed * mean0(lifted * normed))
    put_group(grad_rows, group, grad)


AXES = ("row", "col")
MESH = pl.DeviceIdType.MESH
POSITIONS = 262144
DEVICES = 128
LANES = 128
BLOCK = 8
TALL = 16
STRIDE = 32
SPLIT = STRIDE // GROUPS
ROWS = (D // LANES, GROUPS * TOKENS, LANES)
WHOLE = pl.BlockSpec(memory_space=pltpu.VMEM)


def shape(dims, dtype=BF16):
    return jax.ShapeDtypeStruct(dims, dtype)


def pack(tile, packed):
    few = GROUPS // 2

    def step(a, carry):
        near = tile[a].astype(F32)
        far = tile[STRIDE + a].astype(F32)
        for block in range(SPLIT):
            for half in range(2):
                at = block * GROUPS + half * few
                both = jnp.concatenate([near[at : at + few], far[at : at + few]], axis=0)
                packed[half, a * SPLIT + block] = both.astype(BF16)
        return carry

    lax.fori_loop(0, STRIDE, step, 0, unroll=2)


def spread(rows, arrived, half):
    def step(part, carry):
        values = arrived[half, pl.ds(part * 16, 16)].astype(F32).reshape(16 * BLOCK, D)
        at = pl.multiple_of((half * DEVICES + part * 16) * BLOCK, 16 * BLOCK)
        for lane in range(D // LANES):
            rows[lane, pl.ds(at, 16 * BLOCK), :] = values[:, lane * LANES : lane * LANES + LANES]
        return carry

    lax.fori_loop(0, DEVICES // 16, step, 0)


def gather_rows(rows, packed, half):
    def step(part, carry):
        at = pl.multiple_of((half * DEVICES + part * 16) * BLOCK, 16 * BLOCK)
        values = jnp.concatenate([rows[lane, pl.ds(at, 16 * BLOCK), :] for lane in range(D // LANES)], axis=1)
        packed[half, pl.ds(part * 16, 16)] = values.reshape(16, BLOCK, D).astype(BF16)
        return carry

    lax.fori_loop(0, DEVICES // 16, step, 0)


class Place:
    def __init__(self):
        self.row = lax.axis_index("row")
        self.col = lax.axis_index("col")
        self.core = lax.rem(self.col, 2)
        self.other = (self.row, self.col + 1 - 2 * self.core)
        self.slots = (self.col // 2, self.row)
        self.me = self.row * 16 + self.col

    def along(self, half, index):
        return (self.row, index * 2 + self.core) if half == 0 else (index, self.col)

    def visit(self, work):
        z, y = lax.div(self.row, 2), lax.rem(lax.div(self.col, 2), 4)
        x = lax.rem(self.row, 2) * 2 + lax.div(self.col, 8)
        near = []
        for jump in range(8):
            to_x, to_core = lax.rem(x + jump // 2, 4), lax.rem(self.core + jump % 2, 2)
            near.append((lax.div(to_x, 2), lax.rem(to_x, 2) * 8 + to_core))

        def corner(z, y, first):
            for row, col in near[first:]:
                work(z * 2 + row, y * 2 + col)

        def step(turn, carry):
            jump = lax.rem(turn * 5, 16)
            corner(lax.rem(z + lax.div(jump, 4), 4), lax.rem(y + lax.rem(jump, 4), 4), 0)
            return carry

        corner(z, y, 1)
        lax.fori_loop(1, 16, step, 0)


def remote(source, target, sems, index, device):
    return pltpu.make_async_remote_copy(
        src_ref=source, dst_ref=target, send_sem=sems.at[0, index], recv_sem=sems.at[1, index],
        device_id=device, device_id_type=MESH,
    )


def settle(some, sems, side, index):
    pltpu.make_async_copy(some, some, sems.at[side, index]).wait()


def swap_start(place, packed, arrived, sems, which, half):
    def send(row, col):
        source, target = packed.at[half, row * 16 + col], arrived.at[half, place.me]
        remote(source, target, sems, which * 2 + half, (row, col)).start()

    place.visit(send)
    arrived[half, place.me] = packed[half, place.me]


def swap_wait(some, sems, side, which, half):
    settle(some.at[half, pl.ds(0, DEVICES - 1)], sems, side, which * 2 + half)


def summed(pieces):
    acc = pieces[0].astype(F32)
    for piece in pieces[1:]:
        acc = acc + piece.astype(F32)
    return acc


class DeviceSum:
    def __init__(self, place, sums, total, away, sibling, in_a, part, in_b, sems):
        self.place, self.sums, self.total = place, sums, total
        self.away, self.sibling, self.in_a, self.part, self.in_b, self.sems = away, sibling, in_a, part, in_b, sems
        self.piece = part.shape[1]
        self.half = 8 * self.piece
        self.here = place.core * 2 * self.half

    def rows_of(self, core, half, q):
        start = pl.multiple_of((core * 2 * self.half + half * self.half + q * self.piece) * TALL, TALL)
        return self.sums[pl.ds(start, self.piece * TALL), :]

    def shout(self, source, target, index, half):
        def step(offset, carry):
            q = lax.rem(self.place.slots[half] + offset, 8)
            remote(source(q), target, self.sems, index, self.place.along(half, q)).start()
            return carry

        lax.fori_loop(1, 8, step, 0)

    def start(self):
        for half in range(2):
            def cast(q, carry):
                rows = self.rows_of(1 - self.place.core, half, q).astype(BF16)
                self.away[half, q] = rows.reshape(self.piece, TALL, D)
                return carry

            lax.fori_loop(0, 8, cast, 0)
            remote(self.away.at[half], self.sibling.at[half], self.sems, half, self.place.other).start()

    def round_a(self):
        for half in range(2):
            settle(self.away.at[half], self.sems, 0, half)
            settle(self.sibling.at[half], self.sems, 1, half)

            def add(q, carry):
                kept = self.rows_of(self.place.core, half, q).reshape(self.piece, TALL, D)
                self.away[half, q] = (kept + self.sibling[half, q].astype(F32)).astype(BF16)
                return carry

            lax.fori_loop(0, 8, add, 0)
            slot = self.place.slots[half]
            self.shout(lambda q: self.away.at[half, q], self.in_a.at[half, slot], 2 + half, half)
            self.in_a[half, slot] = self.away[half, slot]

    def round_b(self):
        for half in range(2):
            settle(self.away.at[half, pl.ds(0, 7)], self.sems, 0, 2 + half)
            settle(self.in_a.at[half, pl.ds(0, 7)], self.sems, 1, 2 + half)

            def add(block, carry):
                self.part[half, block] = summed([self.in_a[half, q, block] for q in range(8)]).astype(BF16)
                return carry

            lax.fori_loop(0, self.piece, add, 0)
            slot = self.place.slots[1 - half]
            self.shout(lambda q: self.part.at[half], self.in_b.at[half, slot], 4 + half, 1 - half)
            self.in_b[half, slot] = self.part[half]

    def round_c(self):
        for half in range(2):
            settle(self.in_b.at[half, pl.ds(0, 7)], self.sems, 0, 4 + half)
            settle(self.in_b.at[half, pl.ds(0, 7)], self.sems, 1, 4 + half)
            base = self.here + half * self.half + self.place.slots[half] * self.piece

            def add(block, carry):
                self.total[base + block] = summed([self.in_b[half, q, block] for q in range(8)]).astype(BF16)
                return carry

            lax.fori_loop(0, self.piece, add, 0)
            spot = self.total.at[pl.ds(base, self.piece)]
            self.shout(lambda q: spot, spot, 6 + half, half)

    def round_d(self):
        for half in range(2):
            seven = self.total.at[pl.ds(0, 7 * self.piece)]
            settle(seven, self.sems, 0, 6 + half)
            settle(seven, self.sems, 1, 6 + half)
            spot = self.total.at[pl.ds(self.here + half * self.half, self.half)]
            remote(spot, spot, self.sems, 8 + half, self.place.other).start()

    def finish(self):
        for half in range(2):
            spot = self.total.at[pl.ds(0, self.half)]
            settle(spot, self.sems, 0, 8 + half)
            settle(spot, self.sems, 1, 8 + half)


def whole_kernel(
    activations, cotangent, first_gain, joint, project, second_gain, expand, reduce,
    block_out, grad_in, total_mlp, total_rest, total_gain,
    packed_a, packed_b, act, cot, rows_a, rows_b,
    gain_a, gain_b, joint_t, project_t, expand_t, reduce_t,
    x_feat, scaled_first, triple, mixed, stats, grad_att, grad_mixed, grad_triple,
    sum_mlp, sum_rest, sum_first, sum_second,
    mlp_away, mlp_sibling, mlp_in_a, mlp_part, mlp_in_b,
    rest_away, rest_sibling, rest_in_a, rest_part, rest_in_b,
    gain_pair, gain_x, gain_y,
    swap_sems, mlp_sems, rest_sems, gain_sems,
):
    place = Place()
    barrier = pltpu.get_barrier_semaphore()

    def greet(row, col):
        pl.semaphore_signal(barrier, inc=1, device_id=(row, col), device_id_type=MESH)

    place.visit(greet)
    pack(activations, packed_a)
    gain_a[...] = jnp.broadcast_to(first_gain[...].reshape(1, D), (TOKENS, D)).T
    gain_b[...] = jnp.broadcast_to(second_gain[...].reshape(1, D), (TOKENS, D)).T
    for sums in (sum_mlp, sum_rest, sum_first, sum_second):
        sums[...] = jnp.zeros_like(sums)
    pl.semaphore_wait(barrier, DEVICES - 1)
    for half in range(2):
        swap_start(place, packed_a, act, swap_sems, 0, half)
    pack(cotangent, packed_b)
    for half in range(2):
        swap_start(place, packed_b, cot, swap_sems, 1, half)
    for natural, turned in ((joint, joint_t), (project, project_t), (expand, expand_t)):
        for start in range(0, natural.shape[1], D):
            turned[start : start + D, :] = natural[:, start : start + D].T
    for start in range(0, FF, D):
        reduce_t[:, start : start + D] = reduce[start : start + D, :].T

    def by_halves(work):
        def step(half, carry):
            work(half)
            return carry

        lax.fori_loop(0, 2, step, 0)

    def groups_of(half, work):
        def step(group, carry):
            work(group)
            return carry

        lax.fori_loop(half * (GROUPS // 2), half * (GROUPS // 2) + GROUPS // 2, step, 0)

    def front(half):
        swap_wait(act, swap_sems, 1, 0, half)
        spread(rows_a, act, half)

        def work(group):
            project_group(group, rows_a, gain_a, joint_t, x_feat, scaled_first, triple)
            attend_group(group, triple, mixed, stats)

        groups_of(half, work)

    by_halves(front)
    for half in range(2):
        swap_wait(packed_a, swap_sems, 0, 0, half)
    sum_project = sum_rest.at[pl.ds(3 * D, D)]
    sum_joint = sum_rest.at[pl.ds(0, 3 * D)]
    sum_expand = sum_mlp.at[pl.ds(0, FF)]
    sum_reduce = sum_mlp.at[pl.ds(FF, FF)]

    mlp = DeviceSum(place, sum_mlp, total_mlp, mlp_away, mlp_sibling, mlp_in_a, mlp_part, mlp_in_b, mlp_sems)
    rest = DeviceSum(place, sum_rest, total_rest, rest_away, rest_sibling, rest_in_a, rest_part, rest_in_b, rest_sems)

    def middle(half):
        swap_wait(cot, swap_sems, 1, 1, half)
        spread(rows_b, cot, half)

        def work(group):
            tail_group(
                group, x_feat, rows_b, mixed, project, project_t, gain_b, expand, expand_t, reduce, reduce_t,
                rows_a, grad_att, grad_mixed, sum_project, sum_expand, sum_reduce, sum_second,
            )

        groups_of(half, work)
        pl.when(half == 1)(mlp.start)
        gather_rows(rows_a, packed_a, half)
        swap_start(place, packed_a, block_out, swap_sems, 2, half)

    by_halves(middle)
    for half in range(2):
        swap_wait(packed_b, swap_sems, 0, 1, half)

    def attention(group, carry):
        for turn, work in ((2, mlp.round_a), (4, mlp.round_b), (6, mlp.round_c)):
            pl.when(group == turn)(work)
        attend_back_group(group, scaled_first, triple, stats, grad_mixed, grad_triple, sum_joint)
        return carry

    lax.fori_loop(0, GROUPS, attention, 0)
    rest.start()

    def gain_round(values, slots, index, half):
        slot = place.slots[half]
        slots[slot] = values

        def step(offset, carry):
            q = lax.rem(slot + offset, 8)
            remote(slots.at[slot], slots.at[slot], gain_sems, index, place.along(half, q)).start()
            return carry

        lax.fori_loop(1, 8, step, 0)

    def gain_sum(slots, index):
        settle(slots.at[pl.ds(0, 7)], gain_sems, 0, index)
        settle(slots.at[pl.ds(0, 7)], gain_sems, 1, index)
        return summed([slots[q] for q in range(8)])

    def gain_copy():
        return remote(gain_pair.at[0], gain_pair.at[1], gain_sems, 0, place.other)

    def gain_start():
        both = [jnp.sum(sums[...].T, axis=0, keepdims=True) for sums in (sum_first, sum_second)]
        gain_pair[0] = jnp.concatenate(both + [jnp.zeros((6, D), F32)], axis=0)
        gain_copy().start()

    def gain_next():
        gain_copy().wait()
        gain_round(gain_pair[0] + gain_pair[1], gain_x, 1, 0)

    def back(half):
        def head(group):
            for turn, work in ((1, mlp.round_d), (2, rest.round_a), (6, rest.round_c)):
                pl.when(group == turn)(work)
            head_back_group(group, x_feat, grad_att, triple, gain_a, joint, rows_b, sum_first)

        groups_of(half, head)
        pl.when(half == 1)(gain_start)
        gather_rows(rows_b, packed_b, half)
        pl.when(half == 0)(rest.round_b)
        pl.when(half == 1)(gain_next)
        swap_start(place, packed_b, grad_in, swap_sems, 3, half)

    by_halves(back)
    gain_round(gain_sum(gain_x, 1), gain_y, 2, 1)
    rest.round_d()
    total_gain[...] = gain_sum(gain_y, 2)
    mlp.finish()
    for packed, arrived, which in ((packed_a, block_out, 2), (packed_b, grad_in, 3)):
        for half in range(2):
            swap_wait(packed, swap_sems, 0, which, half)
            swap_wait(arrived, swap_sems, 1, which, half)
    rest.finish()


PARTS = 4


def finish_kernel(
    out_blocks, grad_blocks, expand, reduce, joint, project, gains,
    block_out, grad_in, g_joint, g_project, g_expand, g_reduce, g_first, g_second,
):
    factor = float(POSITIONS) ** -0.5
    few = GROUPS // 2
    for arrived, tile in ((out_blocks, block_out), (grad_blocks, grad_in)):
        for a in range(STRIDE // PARTS):
            early = [arrived[0, a * SPLIT + block].astype(F32) for block in range(SPLIT)]
            late = [arrived[1, a * SPLIT + block].astype(F32) for block in range(SPLIT)]
            for side in range(2):
                part = slice(side * few, side * few + few)
                pieces = [piece[part] for pair in zip(early, late) for piece in pair]
                tile[side, a] = jnp.concatenate(pieces, axis=0).astype(BF16)

    def natural(source):
        return source[...].astype(F32).reshape(D, D) * factor

    g_expand[...] = natural(expand).T
    g_reduce[...] = natural(reduce)
    g_joint[...] = natural(joint).T
    g_project[...] = natural(project)
    g_first[...] = gains[0] * factor
    g_second[...] = gains[1] * factor


def shards(
    activations, cotangent, first_gain, joint_weight, output_weight, second_gain, expand_weight, reduce_weight
):
    dma = pltpu.SemaphoreType.DMA
    blocks = (2, DEVICES, BLOCK, D)
    feat = (GROUPS, D, TOKENS)
    mlp, rest = 2 * FF, 4 * D

    def sum_scratch(rows):
        piece = rows // 32 // TALL
        spread_out = (2, 8, piece, TALL, D)
        return [
            pltpu.VMEM(spread_out, BF16), pltpu.VMEM(spread_out, BF16), pltpu.VMEM(spread_out, BF16),
            pltpu.VMEM((2, piece, TALL, D), BF16), pltpu.VMEM(spread_out, BF16),
        ]

    out_blocks, grad_blocks, total_mlp, total_rest, total_gain = pl.pallas_call(
        whole_kernel,
        in_specs=[WHOLE] * 8,
        out_specs=[WHOLE] * 5,
        out_shape=[
            shape(blocks), shape(blocks), shape((mlp // TALL, TALL, D)), shape((rest // TALL, TALL, D)),
            shape((8, D), F32),
        ],
        scratch_shapes=[
            pltpu.VMEM(blocks, BF16), pltpu.VMEM(blocks, BF16), pltpu.VMEM(blocks, BF16), pltpu.VMEM(blocks, BF16),
            pltpu.VMEM(ROWS, F32), pltpu.VMEM(ROWS, F32),
            pltpu.VMEM((D, TOKENS), F32), pltpu.VMEM((D, TOKENS), F32),
            pltpu.VMEM((3 * D, D), BF16), pltpu.VMEM((D, D), BF16), pltpu.VMEM((FF, D), BF16), pltpu.VMEM((D, FF), BF16),
            pltpu.VMEM(feat, BF16), pltpu.VMEM(feat, BF16), pltpu.VMEM((GROUPS, 3 * D, TOKENS), BF16),
            pltpu.VMEM(feat, BF16), pltpu.VMEM((GROUPS, 2 * HEADS, TOKENS), F32), pltpu.VMEM(feat, F32),
            pltpu.VMEM(feat, BF16), pltpu.VMEM((3 * D, TOKENS), BF16),
            pltpu.VMEM((mlp, D), F32), pltpu.VMEM((rest, D), F32), pltpu.VMEM((D, TOKENS), F32), pltpu.VMEM((D, TOKENS), F32),
            *sum_scratch(mlp), *sum_scratch(rest),
            pltpu.VMEM((2, 8, D), F32), pltpu.VMEM((8, 8, D), F32), pltpu.VMEM((8, 8, D), F32),
            dma((2, 8)), dma((2, 10)), dma((2, 10)), dma((2, 3)),
        ],
        cost_estimate=pl.CostEstimate(flops=12 * 10**10, bytes_accessed=10**8, transcendentals=0),
        compiler_params=pltpu.CompilerParams(
            collective_id=0, has_side_effects=True, vmem_limit_bytes=63 * 2**20
        ),
    )(
        activations, cotangent, first_gain, joint_weight, output_weight, second_gain, expand_weight, reduce_weight,
    )
    tile = (2, STRIDE, STRIDE, D)
    last = 3 * D // D - 1
    arrived = pl.BlockSpec((2, DEVICES // PARTS, BLOCK, D), lambda i: (0, i, 0, 0))
    placed = pl.BlockSpec((2, STRIDE // PARTS, STRIDE, D), lambda i: (0, i, 0, 0))

    def sums(index):
        return pl.BlockSpec((D // TALL, TALL, D), lambda i: (index(i), 0, 0))

    results = pl.pallas_call(
        finish_kernel,
        grid=(PARTS,),
        in_specs=[
            arrived, arrived, sums(lambda i: i), sums(lambda i: PARTS + i), sums(lambda i: jnp.minimum(i, last)),
            sums(lambda i: last + 1), pl.BlockSpec((8, D), lambda i: (0, 0)),
        ],
        out_specs=[
            placed, placed,
            pl.BlockSpec((D, D), lambda i: (0, jnp.minimum(i, last))), pl.BlockSpec((D, D), lambda i: (0, 0)),
            pl.BlockSpec((D, D), lambda i: (0, i)), pl.BlockSpec((D, D), lambda i: (i, 0)),
            pl.BlockSpec((D,), lambda i: (0,)), pl.BlockSpec((D,), lambda i: (0,)),
        ],
        out_shape=[
            shape(tile), shape(tile), shape((D, 3 * D), F32), shape((D, D), F32), shape((D, FF), F32),
            shape((FF, D), F32), shape((D,), F32), shape((D,), F32),
        ],
        compiler_params=pltpu.CompilerParams(vmem_limit_bytes=63 * 2**20),
    )(out_blocks, grad_blocks, total_mlp, total_mlp, total_rest, total_rest, total_gain)
    return tuple(result.reshape(activations.shape) for result in results[:2]) + tuple(results[2:])


def solution(mesh):
    tile = P("row", "col", None)
    return jax.shard_map(
        shards,
        mesh=mesh,
        in_specs=(tile, tile) + (P(),) * 6,
        out_specs=(tile, tile) + (P(),) * 6,
        check_vma=False,
    )
```

```python
import jax
import jax.numpy as jnp
from jax import lax
from jax.experimental import pallas as pl
from jax.experimental.pallas import tpu as pltpu
from jax.sharding import PartitionSpec as P

HEADS = 12
GRID = 16
GROUPS = 8
TOKENS = 256
D = 384
FF = 1536
WIDE = 32
CHUNK = 512

EPSILON = 1e-05
SQRT_HALF = 0.7071067811865476
INV_ROOT_TAU = 0.3989422804014327
LOG2E = 1.4426950408889634
SCORE_SCALE = WIDE ** (-0.5)
F32 = jnp.float32
BF16 = jnp.bfloat16


def dot_nn(a, b):
    return lax.dot_general(a, b, (((1,), (0,)), ((), ())), preferred_element_type=F32)


def dot_nt(a, b):
    return lax.dot_general(a, b, (((1,), (1,)), ((), ())), preferred_element_type=F32)


def dot_tn(a, b):
    return lax.dot_general(a, b, (((0,), (0,)), ((), ())), preferred_element_type=F32)


def mean0(values):
    return jnp.sum(values, axis=0, keepdims=True) * (1.0 / D)


def gelu_parts(pre):
    gauss = jnp.exp2(pre * pre * (-0.5 * LOG2E))
    t = 1.0 / (1.0 + (0.3275911 * SQRT_HALF) * jnp.abs(pre))
    poly = t * (0.127414796 + t * (-0.142248368 + t * (0.7107068705 + t * (-0.7265760135 + t * 0.5307027145))))
    tail = poly * gauss
    cdf = jnp.where(pre >= 0.0, 1.0 - tail, tail)
    return pre * cdf, cdf + pre * gauss * INV_ROOT_TAU


def members(group):
    start = (group // (GROUPS // 2)) * (GROUPS // 2 * TOKENS) + lax.rem(group, GROUPS // 2)
    return pl.ds(start, TOKENS, stride=GROUPS // 2)


def take_group(rows, group):
    return jnp.concatenate([rows[lane, members(group), :].T for lane in range(D // 128)], axis=0)


def put_group(rows, group, values):
    for lane in range(D // 128):
        rows[lane, members(group), :] = values[lane * 128 : lane * 128 + 128].T


def project_group(group, x_rows, gain, joint_t, x_feat, scaled_first, triple):
    values = take_group(x_rows, group)
    x_feat[group] = values.astype(BF16)
    center = values - mean0(values)
    inv = lax.rsqrt(mean0(center * center) + EPSILON)
    scaled = (center * inv * gain[...]).astype(BF16)
    scaled_first[group] = scaled
    triple[group] = dot_nn(joint_t[...], scaled).astype(BF16)


def head_scores(triple, group, head):
    at = head * WIDE
    query = triple[group, at : at + WIDE]
    key = triple[group, D + at : D + at + WIDE]
    return dot_tn(key, query) * (SCORE_SCALE * LOG2E)


def attend_group(group, triple, mixed, stats):
    ahead = head_scores(triple, group, 0)
    for head in range(HEADS):
        at = head * WIDE
        scores = ahead
        if head + 1 < HEADS:
            ahead = head_scores(triple, group, head + 1)
        value = triple[group, 2 * D + at : 2 * D + at + WIDE]
        top = jnp.max(scores, axis=0, keepdims=True)
        raised = jnp.exp2(scores - top)
        share = 1.0 / jnp.sum(raised, axis=0, keepdims=True)
        stats[group, 2 * head : 2 * head + 1] = top
        stats[group, 2 * head + 1 : 2 * head + 2] = share
        weights = (raised * share).astype(BF16)
        mixed[group, at : at + WIDE] = dot_nn(value, weights).astype(BF16)


def tail_group(
    group, x_feat, cot_rows, mixed, project, project_t, gain, expand, expand_t, reduce, reduce_t,
    result_rows, grad_att, grad_mixed, sum_project, sum_expand, sum_reduce, sum_gain,
):
    blend = mixed[group]
    cot32 = take_group(cot_rows, group)
    cot = cot32.astype(BF16)
    attended = x_feat[group].astype(F32) + dot_nn(project_t[...], blend)
    center = attended - mean0(attended)
    inv = lax.rsqrt(mean0(center * center) + EPSILON)
    normed = center * inv
    scaled = (normed * gain[...]).astype(BF16)
    result = attended
    grad_scaled = None
    def chunk_pair(start):
        part = slice(start, start + CHUNK)
        return dot_nn(expand_t[part, :], scaled), dot_nn(reduce[part, :], cot)

    ahead = chunk_pair(0)
    for start in range(0, FF, CHUNK):
        part = slice(start, start + CHUNK)
        pre, grad_hidden = ahead
        if start + CHUNK < FF:
            ahead = chunk_pair(start + CHUNK)
        value, slope = gelu_parts(pre)
        hidden = value.astype(BF16)
        grad_pre = (grad_hidden.astype(BF16).astype(F32) * slope).astype(BF16)
        result = result + dot_nn(reduce_t[:, part], hidden)
        back = dot_nn(expand[:, part], grad_pre)
        grad_scaled = back if grad_scaled is None else grad_scaled + back
        sum_reduce[part, :] += dot_nt(hidden, cot)
        sum_expand[part, :] += dot_nt(grad_pre, scaled)
    put_group(result_rows, group, result)
    sum_gain[...] += grad_scaled * normed
    lifted = grad_scaled * gain[...]
    grad = cot32 + inv * (lifted - mean0(lifted) - normed * mean0(lifted * normed))
    grad_att[group] = grad
    grad_b = grad.astype(BF16)
    sum_project[...] += dot_nt(blend, grad_b)
    grad_mixed[group] = dot_nn(project[...], grad_b).astype(BF16)


def head_pair(triple, grad_mixed, group, head):
    at = head * WIDE
    value = triple[group, 2 * D + at : 2 * D + at + WIDE]
    return head_scores(triple, group, head), dot_tn(value, grad_mixed[group, at : at + WIDE])


def attend_back_group(group, scaled_first, triple, stats, grad_mixed, grad_triple, sum_joint):
    def spill(head, grad_scores, weights):
        at = head * WIDE
        query = triple[group, at : at + WIDE]
        key = triple[group, D + at : D + at + WIDE]
        grad_out = grad_mixed[group, at : at + WIDE]
        grad_triple[at : at + WIDE] = dot_nn(key, grad_scores).astype(BF16)
        grad_triple[D + at : D + at + WIDE] = dot_nt(query, grad_scores).astype(BF16)
        grad_triple[2 * D + at : 2 * D + at + WIDE] = dot_nt(grad_out, weights).astype(BF16)

    ahead = head_pair(triple, grad_mixed, group, 0)
    for head in range(HEADS):
        scores, grad_weights = ahead
        if head + 1 < HEADS:
            ahead = head_pair(triple, grad_mixed, group, head + 1)
        top = stats[group, 2 * head : 2 * head + 1]
        share = stats[group, 2 * head + 1 : 2 * head + 2]
        weights = jnp.exp2(scores - top) * share
        inner = jnp.sum(weights * grad_weights, axis=0, keepdims=True)
        grad_scores = (weights * (grad_weights - inner) * SCORE_SCALE).astype(BF16)
        spill(head, grad_scores, weights.astype(BF16))
    triple[group] = grad_triple[...]
    sum_joint[...] += dot_nt(grad_triple[...], scaled_first[group])


def head_back_group(group, x_feat, grad_att, grad_triple, gain, joint, grad_rows, sum_gain):
    values = x_feat[group].astype(F32)
    center = values - mean0(values)
    inv = lax.rsqrt(mean0(center * center) + EPSILON)
    normed = center * inv
    grad_scaled = dot_nn(joint[...], grad_triple[group])
    sum_gain[...] += grad_scaled * normed
    lifted = grad_scaled * gain[...]
    grad = grad_att[group] + inv * (lifted - mean0(lifted) - normed * mean0(lifted * normed))
    put_group(grad_rows, group, grad)


AXES = ("row", "col")
MESH = pl.DeviceIdType.MESH
POSITIONS = 262144
DEVICES = 128
LANES = 128
BLOCK = 8
TALL = 16
STRIDE = 32
SPLIT = STRIDE // GROUPS
ROWS = (D // LANES, GROUPS * TOKENS, LANES)
WHOLE = pl.BlockSpec(memory_space=pltpu.VMEM)


def shape(dims, dtype=BF16):
    return jax.ShapeDtypeStruct(dims, dtype)


def pack(tile, packed):
    few = GROUPS // 2

    def step(a, carry):
        near = tile[a].astype(F32)
        far = tile[STRIDE + a].astype(F32)
        for block in range(SPLIT):
            for half in range(2):
                at = block * GROUPS + half * few
                both = jnp.concatenate([near[at : at + few], far[at : at + few]], axis=0)
                packed[half, a * SPLIT + block] = both.astype(BF16)
        return carry

    lax.fori_loop(0, STRIDE, step, 0, unroll=2)


def spread(rows, arrived, half):
    def step(part, carry):
        values = arrived[half, pl.ds(part * 16, 16)].astype(F32).reshape(16 * BLOCK, D)
        at = pl.multiple_of((half * DEVICES + part * 16) * BLOCK, 16 * BLOCK)
        for lane in range(D // LANES):
            rows[lane, pl.ds(at, 16 * BLOCK), :] = values[:, lane * LANES : lane * LANES + LANES]
        return carry

    lax.fori_loop(0, DEVICES // 16, step, 0)


def gather_rows(rows, packed, half):
    def step(part, carry):
        at = pl.multiple_of((half * DEVICES + part * 16) * BLOCK, 16 * BLOCK)
        values = jnp.concatenate([rows[lane, pl.ds(at, 16 * BLOCK), :] for lane in range(D // LANES)], axis=1)
        packed[half, pl.ds(part * 16, 16)] = values.reshape(16, BLOCK, D).astype(BF16)
        return carry

    lax.fori_loop(0, DEVICES // 16, step, 0)


class Place:
    def __init__(self):
        self.row = lax.axis_index("row")
        self.col = lax.axis_index("col")
        self.core = lax.rem(self.col, 2)
        self.other = (self.row, self.col + 1 - 2 * self.core)
        self.slots = (self.col // 2, self.row)
        self.me = self.row * 16 + self.col

    def along(self, half, index):
        return (self.row, index * 2 + self.core) if half == 0 else (index, self.col)

    def visit(self, work):
        z, y = lax.div(self.row, 2), lax.rem(lax.div(self.col, 2), 4)
        x = lax.rem(self.row, 2) * 2 + lax.div(self.col, 8)
        near = []
        for jump in range(8):
            to_x, to_core = lax.rem(x + jump // 2, 4), lax.rem(self.core + jump % 2, 2)
            near.append((lax.div(to_x, 2), lax.rem(to_x, 2) * 8 + to_core))

        def corner(z, y, first):
            for row, col in near[first:]:
                work(z * 2 + row, y * 2 + col)

        def step(turn, carry):
            jump = lax.rem(turn * 5, 16)
            corner(lax.rem(z + lax.div(jump, 4), 4), lax.rem(y + lax.rem(jump, 4), 4), 0)
            return carry

        corner(z, y, 1)
        lax.fori_loop(1, 16, step, 0)


def remote(source, target, sems, index, device):
    return pltpu.make_async_remote_copy(
        src_ref=source, dst_ref=target, send_sem=sems.at[0, index], recv_sem=sems.at[1, index],
        device_id=device, device_id_type=MESH,
    )


def settle(some, sems, side, index):
    pltpu.make_async_copy(some, some, sems.at[side, index]).wait()


def swap_start(place, packed, arrived, sems, which, half):
    def send(row, col):
        source, target = packed.at[half, row * 16 + col], arrived.at[half, place.me]
        remote(source, target, sems, which * 2 + half, (row, col)).start()

    place.visit(send)
    arrived[half, place.me] = packed[half, place.me]


def swap_wait(some, sems, side, which, half):
    settle(some.at[half, pl.ds(0, DEVICES - 1)], sems, side, which * 2 + half)


def summed(pieces):
    acc = pieces[0].astype(F32)
    for piece in pieces[1:]:
        acc = acc + piece.astype(F32)
    return acc


class DeviceSum:
    def __init__(self, place, sums, total, away, sibling, in_a, part, in_b, sems):
        self.place, self.sums, self.total = place, sums, total
        self.away, self.sibling, self.in_a, self.part, self.in_b, self.sems = away, sibling, in_a, part, in_b, sems
        self.piece = part.shape[1]
        self.half = 8 * self.piece
        self.here = place.core * 2 * self.half

    def rows_of(self, core, half, q):
        start = pl.multiple_of((core * 2 * self.half + half * self.half + q * self.piece) * TALL, TALL)
        return self.sums[pl.ds(start, self.piece * TALL), :]

    def shout(self, source, target, index, half):
        def step(offset, carry):
            q = lax.rem(self.place.slots[half] + offset, 8)
            remote(source(q), target, self.sems, index, self.place.along(half, q)).start()
            return carry

        lax.fori_loop(1, 8, step, 0)

    def start(self):
        for half in range(2):
            def cast(q, carry):
                rows = self.rows_of(1 - self.place.core, half, q).astype(BF16)
                self.away[half, q] = rows.reshape(self.piece, TALL, D)
                return carry

            lax.fori_loop(0, 8, cast, 0)
            remote(self.away.at[half], self.sibling.at[half], self.sems, half, self.place.other).start()

    def round_a(self):
        for half in range(2):
            settle(self.away.at[half], self.sems, 0, half)
            settle(self.sibling.at[half], self.sems, 1, half)

            def add(q, carry):
                kept = self.rows_of(self.place.core, half, q).reshape(self.piece, TALL, D)
                self.away[half, q] = (kept + self.sibling[half, q].astype(F32)).astype(BF16)
                return carry

            lax.fori_loop(0, 8, add, 0)
            slot = self.place.slots[half]
            self.shout(lambda q: self.away.at[half, q], self.in_a.at[half, slot], 2 + half, half)
            self.in_a[half, slot] = self.away[half, slot]

    def round_b(self):
        for half in range(2):
            settle(self.away.at[half, pl.ds(0, 7)], self.sems, 0, 2 + half)
            settle(self.in_a.at[half, pl.ds(0, 7)], self.sems, 1, 2 + half)

            def add(block, carry):
                self.part[half, block] = summed([self.in_a[half, q, block] for q in range(8)]).astype(BF16)
                return carry

            lax.fori_loop(0, self.piece, add, 0)
            slot = self.place.slots[1 - half]
            self.shout(lambda q: self.part.at[half], self.in_b.at[half, slot], 4 + half, 1 - half)
            self.in_b[half, slot] = self.part[half]

    def round_c(self):
        for half in range(2):
            settle(self.in_b.at[half, pl.ds(0, 7)], self.sems, 0, 4 + half)
            settle(self.in_b.at[half, pl.ds(0, 7)], self.sems, 1, 4 + half)
            base = self.here + half * self.half + self.place.slots[half] * self.piece

            def add(block, carry):
                self.total[base + block] = summed([self.in_b[half, q, block] for q in range(8)]).astype(BF16)
                return carry

            lax.fori_loop(0, self.piece, add, 0)
            spot = self.total.at[pl.ds(base, self.piece)]
            self.shout(lambda q: spot, spot, 6 + half, half)

    def round_d(self):
        for half in range(2):
            seven = self.total.at[pl.ds(0, 7 * self.piece)]
            settle(seven, self.sems, 0, 6 + half)
            settle(seven, self.sems, 1, 6 + half)
            spot = self.total.at[pl.ds(self.here + half * self.half, self.half)]
            remote(spot, spot, self.sems, 8 + half, self.place.other).start()

    def finish(self):
        for half in range(2):
            spot = self.total.at[pl.ds(0, self.half)]
            settle(spot, self.sems, 0, 8 + half)
            settle(spot, self.sems, 1, 8 + half)


def whole_kernel(
    activations, cotangent, first_gain, joint, project, second_gain, expand, reduce,
    block_out, grad_in, total_mlp, total_rest, total_gain,
    packed_a, packed_b, act, cot, rows_a, rows_b,
    gain_a, gain_b, joint_t, project_t, expand_t, reduce_t,
    x_feat, scaled_first, triple, mixed, stats, grad_att, grad_mixed, grad_triple,
    sum_mlp, sum_rest, sum_first, sum_second,
    mlp_away, mlp_sibling, mlp_in_a, mlp_part, mlp_in_b,
    rest_away, rest_sibling, rest_in_a, rest_part, rest_in_b,
    gain_pair, gain_x, gain_y,
    swap_sems, mlp_sems, rest_sems, gain_sems,
):
    place = Place()
    barrier = pltpu.get_barrier_semaphore()

    def greet(row, col):
        pl.semaphore_signal(barrier, inc=1, device_id=(row, col), device_id_type=MESH)

    place.visit(greet)
    pack(activations, packed_a)
    gain_a[...] = jnp.broadcast_to(first_gain[...].reshape(1, D), (TOKENS, D)).T
    gain_b[...] = jnp.broadcast_to(second_gain[...].reshape(1, D), (TOKENS, D)).T
    for sums in (sum_mlp, sum_rest, sum_first, sum_second):
        sums[...] = jnp.zeros_like(sums)
    pl.semaphore_wait(barrier, DEVICES - 1)
    for half in range(2):
        swap_start(place, packed_a, act, swap_sems, 0, half)
    pack(cotangent, packed_b)
    for half in range(2):
        swap_start(place, packed_b, cot, swap_sems, 1, half)
    for natural, turned in ((joint, joint_t), (project, project_t), (expand, expand_t)):
        for start in range(0, natural.shape[1], D):
            turned[start : start + D, :] = natural[:, start : start + D].T
    for start in range(0, FF, D):
        reduce_t[:, start : start + D] = reduce[start : start + D, :].T

    def by_halves(work):
        def step(half, carry):
            work(half)
            return carry

        lax.fori_loop(0, 2, step, 0)

    def groups_of(half, work):
        def step(group, carry):
            work(group)
            return carry

        lax.fori_loop(half * (GROUPS // 2), half * (GROUPS // 2) + GROUPS // 2, step, 0)

    def front(half):
        swap_wait(act, swap_sems, 1, 0, half)
        spread(rows_a, act, half)

        def work(group):
            project_group(group, rows_a, gain_a, joint_t, x_feat, scaled_first, triple)
            attend_group(group, triple, mixed, stats)

        groups_of(half, work)

    by_halves(front)
    for half in range(2):
        swap_wait(packed_a, swap_sems, 0, 0, half)
    sum_project = sum_rest.at[pl.ds(3 * D, D)]
    sum_joint = sum_rest.at[pl.ds(0, 3 * D)]
    sum_expand = sum_mlp.at[pl.ds(0, FF)]
    sum_reduce = sum_mlp.at[pl.ds(FF, FF)]

    mlp = DeviceSum(place, sum_mlp, total_mlp, mlp_away, mlp_sibling, mlp_in_a, mlp_part, mlp_in_b, mlp_sems)
    rest = DeviceSum(place, sum_rest, total_rest, rest_away, rest_sibling, rest_in_a, rest_part, rest_in_b, rest_sems)

    def middle(half):
        swap_wait(cot, swap_sems, 1, 1, half)
        spread(rows_b, cot, half)

        def work(group):
            tail_group(
                group, x_feat, rows_b, mixed, project, project_t, gain_b, expand, expand_t, reduce, reduce_t,
                rows_a, grad_att, grad_mixed, sum_project, sum_expand, sum_reduce, sum_second,
            )

        groups_of(half, work)
        pl.when(half == 1)(mlp.start)
        gather_rows(rows_a, packed_a, half)
        swap_start(place, packed_a, block_out, swap_sems, 2, half)

    by_halves(middle)
    for half in range(2):
        swap_wait(packed_b, swap_sems, 0, 1, half)

    def attention(group, carry):
        for turn, work in ((3, mlp.round_a), (5, mlp.round_b), (7, mlp.round_c)):
            pl.when(group == turn)(work)
        attend_back_group(group, scaled_first, triple, stats, grad_mixed, grad_triple, sum_joint)
        return carry

    lax.fori_loop(0, GROUPS, attention, 0)
    rest.start()

    def gain_round(values, slots, index, half):
        slot = place.slots[half]
        slots[slot] = values

        def step(offset, carry):
            q = lax.rem(slot + offset, 8)
            remote(slots.at[slot], slots.at[slot], gain_sems, index, place.along(half, q)).start()
            return carry

        lax.fori_loop(1, 8, step, 0)

    def gain_sum(slots, index):
        settle(slots.at[pl.ds(0, 7)], gain_sems, 0, index)
        settle(slots.at[pl.ds(0, 7)], gain_sems, 1, index)
        return summed([slots[q] for q in range(8)])

    def gain_copy():
        return remote(gain_pair.at[0], gain_pair.at[1], gain_sems, 0, place.other)

    def gain_start():
        both = [jnp.sum(sums[...].T, axis=0, keepdims=True) for sums in (sum_first, sum_second)]
        gain_pair[0] = jnp.concatenate(both + [jnp.zeros((6, D), F32)], axis=0)
        gain_copy().start()

    def gain_next():
        gain_copy().wait()
        gain_round(gain_pair[0] + gain_pair[1], gain_x, 1, 0)

    def back(half):
        def head(group):
            for turn, work in ((2, rest.round_a), (4, mlp.round_d), (6, rest.round_c)):
                pl.when(group == turn)(work)
            head_back_group(group, x_feat, grad_att, triple, gain_a, joint, rows_b, sum_first)

        groups_of(half, head)
        pl.when(half == 1)(gain_start)
        gather_rows(rows_b, packed_b, half)
        pl.when(half == 0)(rest.round_b)
        pl.when(half == 1)(gain_next)
        swap_start(place, packed_b, grad_in, swap_sems, 3, half)

    by_halves(back)
    gain_round(gain_sum(gain_x, 1), gain_y, 2, 1)
    rest.round_d()
    total_gain[...] = gain_sum(gain_y, 2)
    mlp.finish()
    for packed, arrived, which in ((packed_a, block_out, 2), (packed_b, grad_in, 3)):
        for half in range(2):
            swap_wait(packed, swap_sems, 0, which, half)
            swap_wait(arrived, swap_sems, 1, which, half)
    rest.finish()


PARTS = 4


def finish_kernel(
    out_blocks, grad_blocks, expand, reduce, joint, project, gains,
    block_out, grad_in, g_joint, g_project, g_expand, g_reduce, g_first, g_second,
):
    factor = float(POSITIONS) ** -0.5
    few = GROUPS // 2
    for arrived, tile in ((out_blocks, block_out), (grad_blocks, grad_in)):
        for a in range(STRIDE // PARTS):
            early = [arrived[0, a * SPLIT + block].astype(F32) for block in range(SPLIT)]
            late = [arrived[1, a * SPLIT + block].astype(F32) for block in range(SPLIT)]
            for side in range(2):
                part = slice(side * few, side * few + few)
                pieces = [piece[part] for pair in zip(early, late) for piece in pair]
                tile[side, a] = jnp.concatenate(pieces, axis=0).astype(BF16)

    def natural(source):
        return source[...].astype(F32).reshape(D, D) * factor

    g_expand[...] = natural(expand).T
    g_reduce[...] = natural(reduce)
    g_joint[...] = natural(joint).T
    g_project[...] = natural(project)
    g_first[...] = gains[0] * factor
    g_second[...] = gains[1] * factor


def shards(
    activations, cotangent, first_gain, joint_weight, output_weight, second_gain, expand_weight, reduce_weight
):
    dma = pltpu.SemaphoreType.DMA
    blocks = (2, DEVICES, BLOCK, D)
    feat = (GROUPS, D, TOKENS)
    mlp, rest = 2 * FF, 4 * D

    def sum_scratch(rows):
        piece = rows // 32 // TALL
        spread_out = (2, 8, piece, TALL, D)
        return [
            pltpu.VMEM(spread_out, BF16), pltpu.VMEM(spread_out, BF16), pltpu.VMEM(spread_out, BF16),
            pltpu.VMEM((2, piece, TALL, D), BF16), pltpu.VMEM(spread_out, BF16),
        ]

    out_blocks, grad_blocks, total_mlp, total_rest, total_gain = pl.pallas_call(
        whole_kernel,
        in_specs=[WHOLE] * 8,
        out_specs=[WHOLE] * 5,
        out_shape=[
            shape(blocks), shape(blocks), shape((mlp // TALL, TALL, D)), shape((rest // TALL, TALL, D)),
            shape((8, D), F32),
        ],
        scratch_shapes=[
            pltpu.VMEM(blocks, BF16), pltpu.VMEM(blocks, BF16), pltpu.VMEM(blocks, BF16), pltpu.VMEM(blocks, BF16),
            pltpu.VMEM(ROWS, F32), pltpu.VMEM(ROWS, F32),
            pltpu.VMEM((D, TOKENS), F32), pltpu.VMEM((D, TOKENS), F32),
            pltpu.VMEM((3 * D, D), BF16), pltpu.VMEM((D, D), BF16), pltpu.VMEM((FF, D), BF16), pltpu.VMEM((D, FF), BF16),
            pltpu.VMEM(feat, BF16), pltpu.VMEM(feat, BF16), pltpu.VMEM((GROUPS, 3 * D, TOKENS), BF16),
            pltpu.VMEM(feat, BF16), pltpu.VMEM((GROUPS, 2 * HEADS, TOKENS), F32), pltpu.VMEM(feat, F32),
            pltpu.VMEM(feat, BF16), pltpu.VMEM((3 * D, TOKENS), BF16),
            pltpu.VMEM((mlp, D), F32), pltpu.VMEM((rest, D), F32), pltpu.VMEM((D, TOKENS), F32), pltpu.VMEM((D, TOKENS), F32),
            *sum_scratch(mlp), *sum_scratch(rest),
            pltpu.VMEM((2, 8, D), F32), pltpu.VMEM((8, 8, D), F32), pltpu.VMEM((8, 8, D), F32),
            dma((2, 8)), dma((2, 10)), dma((2, 10)), dma((2, 3)),
        ],
        cost_estimate=pl.CostEstimate(flops=12 * 10**10, bytes_accessed=10**8, transcendentals=0),
        compiler_params=pltpu.CompilerParams(
            collective_id=0, has_side_effects=True, vmem_limit_bytes=63 * 2**20
        ),
    )(
        activations, cotangent, first_gain, joint_weight, output_weight, second_gain, expand_weight, reduce_weight,
    )
    tile = (2, STRIDE, STRIDE, D)
    last = 3 * D // D - 1
    arrived = pl.BlockSpec((2, DEVICES // PARTS, BLOCK, D), lambda i: (0, i, 0, 0))
    placed = pl.BlockSpec((2, STRIDE // PARTS, STRIDE, D), lambda i: (0, i, 0, 0))

    def sums(index):
        return pl.BlockSpec((D // TALL, TALL, D), lambda i: (index(i), 0, 0))

    results = pl.pallas_call(
        finish_kernel,
        grid=(PARTS,),
        in_specs=[
            arrived, arrived, sums(lambda i: i), sums(lambda i: PARTS + i), sums(lambda i: jnp.minimum(i, last)),
            sums(lambda i: last + 1), pl.BlockSpec((8, D), lambda i: (0, 0)),
        ],
        out_specs=[
            placed, placed,
            pl.BlockSpec((D, D), lambda i: (0, jnp.minimum(i, last))), pl.BlockSpec((D, D), lambda i: (0, 0)),
            pl.BlockSpec((D, D), lambda i: (0, i)), pl.BlockSpec((D, D), lambda i: (i, 0)),
            pl.BlockSpec((D,), lambda i: (0,)), pl.BlockSpec((D,), lambda i: (0,)),
        ],
        out_shape=[
            shape(tile), shape(tile), shape((D, 3 * D), F32), shape((D, D), F32), shape((D, FF), F32),
            shape((FF, D), F32), shape((D,), F32), shape((D,), F32),
        ],
        compiler_params=pltpu.CompilerParams(vmem_limit_bytes=63 * 2**20),
    )(out_blocks, grad_blocks, total_mlp, total_mlp, total_rest, total_rest, total_gain)
    return tuple(result.reshape(activations.shape) for result in results[:2]) + tuple(results[2:])


def solution(mesh):
    tile = P("row", "col", None)
    return jax.shard_map(
        shards,
        mesh=mesh,
        in_specs=(tile, tile) + (P(),) * 6,
        out_specs=(tile, tile) + (P(),) * 6,
        check_vma=False,
    )
```

```python
import jax
import jax.numpy as jnp
from jax import lax
from jax.experimental import pallas as pl
from jax.experimental.pallas import tpu as pltpu
from jax.sharding import PartitionSpec as P

HEADS = 12
GRID = 16
GROUPS = 8
TOKENS = 256
D = 384
FF = 1536
WIDE = 32
CHUNK = 512

EPSILON = 1e-05
SQRT_HALF = 0.7071067811865476
INV_ROOT_TAU = 0.3989422804014327
LOG2E = 1.4426950408889634
SCORE_SCALE = WIDE ** (-0.5)
F32 = jnp.float32
BF16 = jnp.bfloat16


def dot_nn(a, b):
    return lax.dot_general(a, b, (((1,), (0,)), ((), ())), preferred_element_type=F32)


def dot_nt(a, b):
    return lax.dot_general(a, b, (((1,), (1,)), ((), ())), preferred_element_type=F32)


def dot_tn(a, b):
    return lax.dot_general(a, b, (((0,), (0,)), ((), ())), preferred_element_type=F32)


def mean0(values):
    return jnp.sum(values, axis=0, keepdims=True) * (1.0 / D)


def gelu_parts(pre):
    gauss = jnp.exp2(pre * pre * (-0.5 * LOG2E))
    t = 1.0 / (1.0 + (0.3275911 * SQRT_HALF) * jnp.abs(pre))
    poly = t * (0.127414796 + t * (-0.142248368 + t * (0.7107068705 + t * (-0.7265760135 + t * 0.5307027145))))
    tail = poly * gauss
    cdf = jnp.where(pre >= 0.0, 1.0 - tail, tail)
    return pre * cdf, cdf + pre * gauss * INV_ROOT_TAU


def members(group):
    start = (group // (GROUPS // 2)) * (GROUPS // 2 * TOKENS) + lax.rem(group, GROUPS // 2)
    return pl.ds(start, TOKENS, stride=GROUPS // 2)


def take_group(rows, group):
    return jnp.concatenate([rows[lane, members(group), :].T for lane in range(D // 128)], axis=0)


def put_group(rows, group, values):
    for lane in range(D // 128):
        rows[lane, members(group), :] = values[lane * 128 : lane * 128 + 128].T


def project_group(group, x_rows, gain, joint_t, x_feat, scaled_first, triple):
    values = take_group(x_rows, group)
    x_feat[group] = values.astype(BF16)
    center = values - mean0(values)
    inv = lax.rsqrt(mean0(center * center) + EPSILON)
    scaled = (center * inv * gain[...]).astype(BF16)
    scaled_first[group] = scaled
    triple[group] = dot_nn(joint_t[...], scaled).astype(BF16)


def head_scores(triple, group, head):
    at = head * WIDE
    query = triple[group, at : at + WIDE]
    key = triple[group, D + at : D + at + WIDE]
    return dot_tn(key, query) * (SCORE_SCALE * LOG2E)


def attend_group(group, triple, mixed, stats):
    ahead = head_scores(triple, group, 0)
    for head in range(HEADS):
        at = head * WIDE
        scores = ahead
        if head + 1 < HEADS:
            ahead = head_scores(triple, group, head + 1)
        value = triple[group, 2 * D + at : 2 * D + at + WIDE]
        top = jnp.max(scores, axis=0, keepdims=True)
        raised = jnp.exp2(scores - top)
        share = 1.0 / jnp.sum(raised, axis=0, keepdims=True)
        stats[group, 2 * head : 2 * head + 1] = top
        stats[group, 2 * head + 1 : 2 * head + 2] = share
        weights = (raised * share).astype(BF16)
        mixed[group, at : at + WIDE] = dot_nn(value, weights).astype(BF16)


def tail_group(
    group, x_feat, cot_rows, mixed, project, project_t, gain, expand, expand_t, reduce, reduce_t,
    result_rows, grad_att, grad_mixed, sum_project, sum_expand, sum_reduce, sum_gain,
):
    blend = mixed[group]
    cot32 = take_group(cot_rows, group)
    cot = cot32.astype(BF16)
    attended = x_feat[group].astype(F32) + dot_nn(project_t[...], blend)
    center = attended - mean0(attended)
    inv = lax.rsqrt(mean0(center * center) + EPSILON)
    normed = center * inv
    scaled = (normed * gain[...]).astype(BF16)
    result = attended
    grad_scaled = None
    def chunk_pair(start):
        part = slice(start, start + CHUNK)
        return dot_nn(expand_t[part, :], scaled), dot_nn(reduce[part, :], cot)

    ahead = chunk_pair(0)
    for start in range(0, FF, CHUNK):
        part = slice(start, start + CHUNK)
        pre, grad_hidden = ahead
        if start + CHUNK < FF:
            ahead = chunk_pair(start + CHUNK)
        value, slope = gelu_parts(pre)
        hidden = value.astype(BF16)
        grad_pre = (grad_hidden.astype(BF16).astype(F32) * slope).astype(BF16)
        result = result + dot_nn(reduce_t[:, part], hidden)
        back = dot_nn(expand[:, part], grad_pre)
        grad_scaled = back if grad_scaled is None else grad_scaled + back
        sum_reduce[part, :] += dot_nt(hidden, cot)
        sum_expand[part, :] += dot_nt(grad_pre, scaled)
    put_group(result_rows, group, result)
    sum_gain[...] += grad_scaled * normed
    lifted = grad_scaled * gain[...]
    grad = cot32 + inv * (lifted - mean0(lifted) - normed * mean0(lifted * normed))
    grad_att[group] = grad
    grad_b = grad.astype(BF16)
    sum_project[...] += dot_nt(blend, grad_b)
    grad_mixed[group] = dot_nn(project[...], grad_b).astype(BF16)


def head_pair(triple, grad_mixed, group, head):
    at = head * WIDE
    value = triple[group, 2 * D + at : 2 * D + at + WIDE]
    return head_scores(triple, group, head), dot_tn(value, grad_mixed[group, at : at + WIDE])


def attend_back_group(group, scaled_first, triple, stats, grad_mixed, grad_triple, sum_joint):
    def spill(head, grad_scores, weights):
        at = head * WIDE
        query = triple[group, at : at + WIDE]
        key = triple[group, D + at : D + at + WIDE]
        grad_out = grad_mixed[group, at : at + WIDE]
        grad_triple[at : at + WIDE] = dot_nn(key, grad_scores).astype(BF16)
        grad_triple[D + at : D + at + WIDE] = dot_nt(query, grad_scores).astype(BF16)
        grad_triple[2 * D + at : 2 * D + at + WIDE] = dot_nt(grad_out, weights).astype(BF16)

    ahead = head_pair(triple, grad_mixed, group, 0)
    for head in range(HEADS):
        scores, grad_weights = ahead
        if head + 1 < HEADS:
            ahead = head_pair(triple, grad_mixed, group, head + 1)
        top = stats[group, 2 * head : 2 * head + 1]
        share = stats[group, 2 * head + 1 : 2 * head + 2]
        weights = jnp.exp2(scores - top) * share
        inner = jnp.sum(weights * grad_weights, axis=0, keepdims=True)
        grad_scores = (weights * (grad_weights - inner) * SCORE_SCALE).astype(BF16)
        spill(head, grad_scores, weights.astype(BF16))
    triple[group] = grad_triple[...]
    sum_joint[...] += dot_nt(grad_triple[...], scaled_first[group])


def head_back_group(group, x_feat, grad_att, grad_triple, gain, joint, grad_rows, sum_gain):
    values = x_feat[group].astype(F32)
    center = values - mean0(values)
    inv = lax.rsqrt(mean0(center * center) + EPSILON)
    normed = center * inv
    grad_scaled = dot_nn(joint[...], grad_triple[group])
    sum_gain[...] += grad_scaled * normed
    lifted = grad_scaled * gain[...]
    grad = grad_att[group] + inv * (lifted - mean0(lifted) - normed * mean0(lifted * normed))
    put_group(grad_rows, group, grad)


AXES = ("row", "col")
MESH = pl.DeviceIdType.MESH
POSITIONS = 262144
DEVICES = 128
LANES = 128
BLOCK = 8
TALL = 16
STRIDE = 32
SPLIT = STRIDE // GROUPS
ROWS = (D // LANES, GROUPS * TOKENS, LANES)
WHOLE = pl.BlockSpec(memory_space=pltpu.VMEM)


def shape(dims, dtype=BF16):
    return jax.ShapeDtypeStruct(dims, dtype)


def pack(tile, packed):
    few = GROUPS // 2

    def step(a, carry):
        near = tile[a].astype(F32)
        far = tile[STRIDE + a].astype(F32)
        for block in range(SPLIT):
            for half in range(2):
                at = block * GROUPS + half * few
                both = jnp.concatenate([near[at : at + few], far[at : at + few]], axis=0)
                packed[half, a * SPLIT + block] = both.astype(BF16)
        return carry

    lax.fori_loop(0, STRIDE, step, 0, unroll=2)


def spread(rows, arrived, half):
    def step(part, carry):
        values = arrived[half, pl.ds(part * 16, 16)].astype(F32).reshape(16 * BLOCK, D)
        at = pl.multiple_of((half * DEVICES + part * 16) * BLOCK, 16 * BLOCK)
        for lane in range(D // LANES):
            rows[lane, pl.ds(at, 16 * BLOCK), :] = values[:, lane * LANES : lane * LANES + LANES]
        return carry

    lax.fori_loop(0, DEVICES // 16, step, 0)


def gather_rows(rows, packed, half):
    def step(part, carry):
        at = pl.multiple_of((half * DEVICES + part * 16) * BLOCK, 16 * BLOCK)
        values = jnp.concatenate([rows[lane, pl.ds(at, 16 * BLOCK), :] for lane in range(D // LANES)], axis=1)
        packed[half, pl.ds(part * 16, 16)] = values.reshape(16, BLOCK, D).astype(BF16)
        return carry

    lax.fori_loop(0, DEVICES // 16, step, 0)


class Place:
    def __init__(self):
        self.row = lax.axis_index("row")
        self.col = lax.axis_index("col")
        self.core = lax.rem(self.col, 2)
        self.other = (self.row, self.col + 1 - 2 * self.core)
        self.slots = (self.col // 2, self.row)
        self.me = self.row * 16 + self.col

    def along(self, half, index):
        return (self.row, index * 2 + self.core) if half == 0 else (index, self.col)

    def visit(self, work):
        z, y = lax.div(self.row, 2), lax.rem(lax.div(self.col, 2), 4)
        x = lax.rem(self.row, 2) * 2 + lax.div(self.col, 8)
        near = []
        for jump in range(8):
            to_x, to_core = lax.rem(x + jump // 2, 4), lax.rem(self.core + jump % 2, 2)
            near.append((lax.div(to_x, 2), lax.rem(to_x, 2) * 8 + to_core))

        def corner(z, y, first):
            for row, col in near[first:]:
                work(z * 2 + row, y * 2 + col)

        def step(turn, carry):
            jump = lax.rem(turn * 5, 16)
            corner(lax.rem(z + lax.div(jump, 4), 4), lax.rem(y + lax.rem(jump, 4), 4), 0)
            return carry

        corner(z, y, 1)
        lax.fori_loop(1, 16, step, 0)


def remote(source, target, sems, index, device):
    return pltpu.make_async_remote_copy(
        src_ref=source, dst_ref=target, send_sem=sems.at[0, index], recv_sem=sems.at[1, index],
        device_id=device, device_id_type=MESH,
    )


def settle(some, sems, side, index):
    pltpu.make_async_copy(some, some, sems.at[side, index]).wait()


def swap_start(place, packed, arrived, sems, which, half):
    def send(row, col):
        source, target = packed.at[half, row * 16 + col], arrived.at[half, place.me]
        remote(source, target, sems, which * 2 + half, (row, col)).start()

    place.visit(send)
    arrived[half, place.me] = packed[half, place.me]


def swap_start_both(place, packed, arrived, sems, which):
    def send(row, col):
        source, target = packed.at[:, row * 16 + col], arrived.at[:, place.me]
        remote(source, target, sems, which * 2, (row, col)).start()

    place.visit(send)
    arrived[:, place.me] = packed[:, place.me]


def swap_wait_both(some, sems, side, which):
    settle(some.at[:, pl.ds(0, DEVICES - 1)], sems, side, which * 2)


def swap_wait(some, sems, side, which, half):
    settle(some.at[half, pl.ds(0, DEVICES - 1)], sems, side, which * 2 + half)


def summed(pieces):
    acc = pieces[0].astype(F32)
    for piece in pieces[1:]:
        acc = acc + piece.astype(F32)
    return acc


class DeviceSum:
    def __init__(self, place, sums, total, away, sibling, in_a, part, in_b, sems):
        self.place, self.sums, self.total = place, sums, total
        self.away, self.sibling, self.in_a, self.part, self.in_b, self.sems = away, sibling, in_a, part, in_b, sems
        self.piece = part.shape[1]
        self.half = 8 * self.piece
        self.here = place.core * 2 * self.half

    def rows_of(self, core, half, q):
        start = pl.multiple_of((core * 2 * self.half + half * self.half + q * self.piece) * TALL, TALL)
        return self.sums[pl.ds(start, self.piece * TALL), :]

    def shout(self, source, target, index, half):
        def step(offset, carry):
            q = lax.rem(self.place.slots[half] + offset, 8)
            remote(source(q), target, self.sems, index, self.place.along(half, q)).start()
            return carry

        lax.fori_loop(1, 8, step, 0)

    def start(self):
        for half in range(2):
            def cast(q, carry):
                rows = self.rows_of(1 - self.place.core, half, q).astype(BF16)
                self.away[half, q] = rows.reshape(self.piece, TALL, D)
                return carry

            lax.fori_loop(0, 8, cast, 0)
            remote(self.away.at[half], self.sibling.at[half], self.sems, half, self.place.other).start()

    def round_a(self):
        for half in range(2):
            settle(self.away.at[half], self.sems, 0, half)
            settle(self.sibling.at[half], self.sems, 1, half)

            def add(q, carry):
                kept = self.rows_of(self.place.core, half, q).reshape(self.piece, TALL, D)
                self.away[half, q] = (kept + self.sibling[half, q].astype(F32)).astype(BF16)
                return carry

            lax.fori_loop(0, 8, add, 0)
            slot = self.place.slots[half]
            self.shout(lambda q: self.away.at[half, q], self.in_a.at[half, slot], 2 + half, half)
            self.in_a[half, slot] = self.away[half, slot]

    def round_b(self):
        for half in range(2):
            settle(self.away.at[half, pl.ds(0, 7)], self.sems, 0, 2 + half)
            settle(self.in_a.at[half, pl.ds(0, 7)], self.sems, 1, 2 + half)

            def add(block, carry):
                self.part[half, block] = summed([self.in_a[half, q, block] for q in range(8)]).astype(BF16)
                return carry

            lax.fori_loop(0, self.piece, add, 0)
            slot = self.place.slots[1 - half]
            self.shout(lambda q: self.part.at[half], self.in_b.at[half, slot], 4 + half, 1 - half)
            self.in_b[half, slot] = self.part[half]

    def round_c(self):
        for half in range(2):
            settle(self.in_b.at[half, pl.ds(0, 7)], self.sems, 0, 4 + half)
            settle(self.in_b.at[half, pl.ds(0, 7)], self.sems, 1, 4 + half)
            base = self.here + half * self.half + self.place.slots[half] * self.piece

            def add(block, carry):
                self.total[base + block] = summed([self.in_b[half, q, block] for q in range(8)]).astype(BF16)
                return carry

            lax.fori_loop(0, self.piece, add, 0)
            spot = self.total.at[pl.ds(base, self.piece)]
            self.shout(lambda q: spot, spot, 6 + half, half)

    def round_d(self):
        for half in range(2):
            seven = self.total.at[pl.ds(0, 7 * self.piece)]
            settle(seven, self.sems, 0, 6 + half)
            settle(seven, self.sems, 1, 6 + half)
            spot = self.total.at[pl.ds(self.here + half * self.half, self.half)]
            remote(spot, spot, self.sems, 8 + half, self.place.other).start()

    def finish(self):
        for half in range(2):
            spot = self.total.at[pl.ds(0, self.half)]
            settle(spot, self.sems, 0, 8 + half)
            settle(spot, self.sems, 1, 8 + half)


def whole_kernel(
    activations, cotangent, first_gain, joint, project, second_gain, expand, reduce,
    block_out, grad_in, total_mlp, total_rest, total_gain,
    packed_a, packed_b, act, cot, rows_a, rows_b,
    gain_a, gain_b, joint_t, project_t, expand_t, reduce_t,
    x_feat, scaled_first, triple, mixed, stats, grad_att, grad_mixed, grad_triple,
    sum_mlp, sum_rest, sum_first, sum_second,
    mlp_away, mlp_sibling, mlp_in_a, mlp_part, mlp_in_b,
    rest_away, rest_sibling, rest_in_a, rest_part, rest_in_b,
    gain_pair, gain_x, gain_y,
    swap_sems, mlp_sems, rest_sems, gain_sems,
):
    place = Place()
    barrier = pltpu.get_barrier_semaphore()

    def greet(row, col):
        pl.semaphore_signal(barrier, inc=1, device_id=(row, col), device_id_type=MESH)

    place.visit(greet)
    pack(activations, packed_a)
    gain_a[...] = jnp.broadcast_to(first_gain[...].reshape(1, D), (TOKENS, D)).T
    gain_b[...] = jnp.broadcast_to(second_gain[...].reshape(1, D), (TOKENS, D)).T
    for sums in (sum_mlp, sum_rest, sum_first, sum_second):
        sums[...] = jnp.zeros_like(sums)
    pl.semaphore_wait(barrier, DEVICES - 1)
    for half in range(2):
        swap_start(place, packed_a, act, swap_sems, 0, half)
    pack(cotangent, packed_b)
    swap_start_both(place, packed_b, cot, swap_sems, 1)
    for natural, turned in ((joint, joint_t), (project, project_t), (expand, expand_t)):
        for start in range(0, natural.shape[1], D):
            turned[start : start + D, :] = natural[:, start : start + D].T
    for start in range(0, FF, D):
        reduce_t[:, start : start + D] = reduce[start : start + D, :].T

    def by_halves(work):
        def step(half, carry):
            work(half)
            return carry

        lax.fori_loop(0, 2, step, 0)

    def groups_of(half, work):
        def step(group, carry):
            work(group)
            return carry

        lax.fori_loop(half * (GROUPS // 2), half * (GROUPS // 2) + GROUPS // 2, step, 0)

    def front(half):
        swap_wait(act, swap_sems, 1, 0, half)
        spread(rows_a, act, half)

        def work(group):
            project_group(group, rows_a, gain_a, joint_t, x_feat, scaled_first, triple)
            attend_group(group, triple, mixed, stats)

        groups_of(half, work)

    by_halves(front)
    for half in range(2):
        swap_wait(packed_a, swap_sems, 0, 0, half)
    sum_project = sum_rest.at[pl.ds(3 * D, D)]
    sum_joint = sum_rest.at[pl.ds(0, 3 * D)]
    sum_expand = sum_mlp.at[pl.ds(0, FF)]
    sum_reduce = sum_mlp.at[pl.ds(FF, FF)]

    mlp = DeviceSum(place, sum_mlp, total_mlp, mlp_away, mlp_sibling, mlp_in_a, mlp_part, mlp_in_b, mlp_sems)
    rest = DeviceSum(place, sum_rest, total_rest, rest_away, rest_sibling, rest_in_a, rest_part, rest_in_b, rest_sems)

    def middle(half):
        spread(rows_b, cot, half)

        def work(group):
            tail_group(
                group, x_feat, rows_b, mixed, project, project_t, gain_b, expand, expand_t, reduce, reduce_t,
                rows_a, grad_att, grad_mixed, sum_project, sum_expand, sum_reduce, sum_second,
            )

        groups_of(half, work)
        pl.when(half == 1)(mlp.start)
        gather_rows(rows_a, packed_a, half)
        swap_start(place, packed_a, block_out, swap_sems, 2, half)

    swap_wait_both(cot, swap_sems, 1, 1)
    by_halves(middle)
    swap_wait_both(packed_b, swap_sems, 0, 1)

    def attention(group, carry):
        for turn, work in ((3, mlp.round_a), (5, mlp.round_b), (7, mlp.round_c)):
            pl.when(group == turn)(work)
        attend_back_group(group, scaled_first, triple, stats, grad_mixed, grad_triple, sum_joint)
        return carry

    lax.fori_loop(0, GROUPS, attention, 0)
    rest.start()

    def gain_round(values, slots, index, half):
        slot = place.slots[half]
        slots[slot] = values

        def step(offset, carry):
            q = lax.rem(slot + offset, 8)
            remote(slots.at[slot], slots.at[slot], gain_sems, index, place.along(half, q)).start()
            return carry

        lax.fori_loop(1, 8, step, 0)

    def gain_sum(slots, index):
        settle(slots.at[pl.ds(0, 7)], gain_sems, 0, index)
        settle(slots.at[pl.ds(0, 7)], gain_sems, 1, index)
        return summed([slots[q] for q in range(8)])

    def gain_copy():
        return remote(gain_pair.at[0], gain_pair.at[1], gain_sems, 0, place.other)

    def gain_start():
        both = [jnp.sum(sums[...].T, axis=0, keepdims=True) for sums in (sum_first, sum_second)]
        gain_pair[0] = jnp.concatenate(both + [jnp.zeros((6, D), F32)], axis=0)
        gain_copy().start()

    def gain_next():
        gain_copy().wait()
        gain_round(gain_pair[0] + gain_pair[1], gain_x, 1, 0)

    def back(half):
        def head(group):
            for turn, work in ((2, rest.round_a), (4, mlp.round_d), (6, rest.round_c)):
                pl.when(group == turn)(work)
            head_back_group(group, x_feat, grad_att, triple, gain_a, joint, rows_b, sum_first)

        groups_of(half, head)
        pl.when(half == 1)(gain_start)
        gather_rows(rows_b, packed_b, half)
        pl.when(half == 0)(rest.round_b)
        pl.when(half == 1)(gain_next)
        swap_start(place, packed_b, grad_in, swap_sems, 3, half)

    by_halves(back)
    gain_round(gain_sum(gain_x, 1), gain_y, 2, 1)
    rest.round_d()
    total_gain[...] = gain_sum(gain_y, 2)
    mlp.finish()
    for packed, arrived, which in ((packed_a, block_out, 2), (packed_b, grad_in, 3)):
        for half in range(2):
            swap_wait(packed, swap_sems, 0, which, half)
            swap_wait(arrived, swap_sems, 1, which, half)
    rest.finish()


PARTS = 4


def finish_kernel(
    out_blocks, grad_blocks, expand, reduce, joint, project, gains,
    block_out, grad_in, g_joint, g_project, g_expand, g_reduce, g_first, g_second,
):
    factor = float(POSITIONS) ** -0.5
    few = GROUPS // 2
    for arrived, tile in ((out_blocks, block_out), (grad_blocks, grad_in)):
        for a in range(STRIDE // PARTS):
            early = [arrived[0, a * SPLIT + block].astype(F32) for block in range(SPLIT)]
            late = [arrived[1, a * SPLIT + block].astype(F32) for block in range(SPLIT)]
            for side in range(2):
                part = slice(side * few, side * few + few)
                pieces = [piece[part] for pair in zip(early, late) for piece in pair]
                tile[side, a] = jnp.concatenate(pieces, axis=0).astype(BF16)

    def natural(source):
        return source[...].astype(F32).reshape(D, D) * factor

    g_expand[...] = natural(expand).T
    g_reduce[...] = natural(reduce)
    g_joint[...] = natural(joint).T
    g_project[...] = natural(project)
    g_first[...] = gains[0] * factor
    g_second[...] = gains[1] * factor


def shards(
    activations, cotangent, first_gain, joint_weight, output_weight, second_gain, expand_weight, reduce_weight
):
    dma = pltpu.SemaphoreType.DMA
    blocks = (2, DEVICES, BLOCK, D)
    feat = (GROUPS, D, TOKENS)
    mlp, rest = 2 * FF, 4 * D

    def sum_scratch(rows):
        piece = rows // 32 // TALL
        spread_out = (2, 8, piece, TALL, D)
        return [
            pltpu.VMEM(spread_out, BF16), pltpu.VMEM(spread_out, BF16), pltpu.VMEM(spread_out, BF16),
            pltpu.VMEM((2, piece, TALL, D), BF16), pltpu.VMEM(spread_out, BF16),
        ]

    out_blocks, grad_blocks, total_mlp, total_rest, total_gain = pl.pallas_call(
        whole_kernel,
        in_specs=[WHOLE] * 8,
        out_specs=[WHOLE] * 5,
        out_shape=[
            shape(blocks), shape(blocks), shape((mlp // TALL, TALL, D)), shape((rest // TALL, TALL, D)),
            shape((8, D), F32),
        ],
        scratch_shapes=[
            pltpu.VMEM(blocks, BF16), pltpu.VMEM(blocks, BF16), pltpu.VMEM(blocks, BF16), pltpu.VMEM(blocks, BF16),
            pltpu.VMEM(ROWS, F32), pltpu.VMEM(ROWS, F32),
            pltpu.VMEM((D, TOKENS), F32), pltpu.VMEM((D, TOKENS), F32),
            pltpu.VMEM((3 * D, D), BF16), pltpu.VMEM((D, D), BF16), pltpu.VMEM((FF, D), BF16), pltpu.VMEM((D, FF), BF16),
            pltpu.VMEM(feat, BF16), pltpu.VMEM(feat, BF16), pltpu.VMEM((GROUPS, 3 * D, TOKENS), BF16),
            pltpu.VMEM(feat, BF16), pltpu.VMEM((GROUPS, 2 * HEADS, TOKENS), F32), pltpu.VMEM(feat, F32),
            pltpu.VMEM(feat, BF16), pltpu.VMEM((3 * D, TOKENS), BF16),
            pltpu.VMEM((mlp, D), F32), pltpu.VMEM((rest, D), F32), pltpu.VMEM((D, TOKENS), F32), pltpu.VMEM((D, TOKENS), F32),
            *sum_scratch(mlp), *sum_scratch(rest),
            pltpu.VMEM((2, 8, D), F32), pltpu.VMEM((8, 8, D), F32), pltpu.VMEM((8, 8, D), F32),
            dma((2, 8)), dma((2, 10)), dma((2, 10)), dma((2, 3)),
        ],
        cost_estimate=pl.CostEstimate(flops=12 * 10**10, bytes_accessed=10**8, transcendentals=0),
        compiler_params=pltpu.CompilerParams(
            collective_id=0, has_side_effects=True, vmem_limit_bytes=63 * 2**20
        ),
    )(
        activations, cotangent, first_gain, joint_weight, output_weight, second_gain, expand_weight, reduce_weight,
    )
    tile = (2, STRIDE, STRIDE, D)
    last = 3 * D // D - 1
    arrived = pl.BlockSpec((2, DEVICES // PARTS, BLOCK, D), lambda i: (0, i, 0, 0))
    placed = pl.BlockSpec((2, STRIDE // PARTS, STRIDE, D), lambda i: (0, i, 0, 0))

    def sums(index):
        return pl.BlockSpec((D // TALL, TALL, D), lambda i: (index(i), 0, 0))

    results = pl.pallas_call(
        finish_kernel,
        grid=(PARTS,),
        in_specs=[
            arrived, arrived, sums(lambda i: i), sums(lambda i: PARTS + i), sums(lambda i: jnp.minimum(i, last)),
            sums(lambda i: last + 1), pl.BlockSpec((8, D), lambda i: (0, 0)),
        ],
        out_specs=[
            placed, placed,
            pl.BlockSpec((D, D), lambda i: (0, jnp.minimum(i, last))), pl.BlockSpec((D, D), lambda i: (0, 0)),
            pl.BlockSpec((D, D), lambda i: (0, i)), pl.BlockSpec((D, D), lambda i: (i, 0)),
            pl.BlockSpec((D,), lambda i: (0,)), pl.BlockSpec((D,), lambda i: (0,)),
        ],
        out_shape=[
            shape(tile), shape(tile), shape((D, 3 * D), F32), shape((D, D), F32), shape((D, FF), F32),
            shape((FF, D), F32), shape((D,), F32), shape((D,), F32),
        ],
        compiler_params=pltpu.CompilerParams(vmem_limit_bytes=63 * 2**20),
    )(out_blocks, grad_blocks, total_mlp, total_mlp, total_rest, total_rest, total_gain)
    return tuple(result.reshape(activations.shape) for result in results[:2]) + tuple(results[2:])


def solution(mesh):
    tile = P("row", "col", None)
    return jax.shard_map(
        shards,
        mesh=mesh,
        in_specs=(tile, tile) + (P(),) * 6,
        out_specs=(tile, tile) + (P(),) * 6,
        check_vma=False,
    )
```
